32 devices in a mesh: dp: 8 (over z, y), vocab: 4 (over x, core).
Axes of the slice: x: 2, y: 2, z: 4, core: 2. Of those that a mesh axis runs over, the one named last changes fastest.
Arguments:
- token_ids: int32 [32, 512], P(('dp', 'vocab')), may hold values from 0 to 30719
- segment_ids: int32 [32, 512], P(('dp', 'vocab')), may hold values from 0 to 7, never falling along the last dimension, each value on 1 to 256 neighbouring positions
- labels: int32 [32, 512], P(('dp', 'vocab')), may hold values from 0 to 30719
- loss_mask: int32 [32, 512], P(('dp', 'vocab')), may hold values from 0 to 1, as said below
- teacher_group: int32 [32], P(('dp', 'vocab')), may hold values from 0 to 2
- teacher_inputs: bfloat16 [32, 512, 768], P(('dp', 'vocab')), may hold values from -6 to 6
- teacher_table: bfloat16 [3, 768, 30720], P(None, None, 'vocab'), may hold values from -0.4375 to 0.4375
- teacher_qkv: bfloat16 [3, 768, 2304], P(None, ('dp', 'vocab')), may hold values from -0.21875 to 0.21875
- teacher_out: bfloat16 [3, 768, 768], P(None, ('dp', 'vocab')), may hold values from -0.875 to 0.875
- teacher_up: bfloat16 [3, 768, 3072], P(None, ('dp', 'vocab')), may hold values from -0.21875 to 0.21875
- teacher_down: bfloat16 [3, 3072, 768], P(None, ('dp', 'vocab')), may hold values from -0.109375 to 0.109375
- teacher_gains: float32 [3, 6, 768], replicated, may hold values from 0.5 to 1.5
- step_count: int32 [], replicated, may hold values from 2 to 20
- embed_w: float32 [30720, 512], P('vocab', 'dp'), may hold values from -0.5 to 0.5
- embed_m: float32 [30720, 512], P('vocab', 'dp'), may hold values from -1.9073486e-06 to 1.9073486e-06
- embed_v: float32 [30720, 512], P('vocab', 'dp'), may hold values from 6.5309676e-16 to 1.0449548e-14
- pos_w: float32 [512, 512], P(('dp', 'vocab')), may hold values from -0.5 to 0.5
- pos_m: float32 [512, 512], P(('dp', 'vocab')), may hold values from -1.9073486e-06 to 1.9073486e-06
- pos_v: float32 [512, 512], P(('dp', 'vocab')), may hold values from 6.5309676e-16 to 1.0449548e-14
- qkv_w: float32 [512, 1536], P(('dp', 'vocab')), may hold values from -0.25 to 0.25
- qkv_m: float32 [512, 1536], P(('dp', 'vocab')), may hold values from -1.9073486e-06 to 1.9073486e-06
- qkv_v: float32 [512, 1536], P(('dp', 'vocab')), may hold values from 6.5309676e-16 to 1.0449548e-14
- out_w: float32 [512, 512], P(('dp', 'vocab')), may hold values from -1 to 1
- out_m: float32 [512, 512], P(('dp', 'vocab')), may hold values from -1.9073486e-06 to 1.9073486e-06
- out_v: float32 [512, 512], P(('dp', 'vocab')), may hold values from 6.5309676e-16 to 1.0449548e-14
- up_w: float32 [512, 2048], P(('dp', 'vocab')), may hold values from -0.25 to 0.25
- up_m: float32 [512, 2048], P(('dp', 'vocab')), may hold values from -1.9073486e-06 to 1.9073486e-06
- up_v: float32 [512, 2048], P(('dp', 'vocab')), may hold values from 6.5309676e-16 to 1.0449548e-14
- down_w: float32 [2048, 512], P(('dp', 'vocab')), may hold values from -0.125 to 0.125
- down_m: float32 [2048, 512], P(('dp', 'vocab')), may hold values from -1.9073486e-06 to 1.9073486e-06
- down_v: float32 [2048, 512], P(('dp', 'vocab')), may hold values from 6.5309676e-16 to 1.0449548e-14
- gains_w: float32 [6, 512], replicated, may hold values from 0.5 to 1.5
- gains_m: float32 [6, 512], replicated, may hold values from -7.6293945e-06 to 7.6293945e-06
- gains_v: float32 [6, 512], replicated, may hold values from 1.0449548e-14 to 1.6719277e-13
Outputs:
- loss: float32 [], replicated
- grad_norm: float32 [], replicated
- embed_m_new: float32 [30720, 512], P('vocab', 'dp')
- embed_v_new: float32 [30720, 512], P('vocab', 'dp')
- embed_w_new: float32 [30720, 512], P('vocab', 'dp')
- pos_m_new: float32 [512, 512], P(('dp', 'vocab'))
- pos_v_new: float32 [512, 512], P(('dp', 'vocab'))
- pos_w_new: float32 [512, 512], P(('dp', 'vocab'))
- qkv_m_new: float32 [512, 1536], P(('dp', 'vocab'))
- qkv_v_new: float32 [512, 1536], P(('dp', 'vocab'))
- qkv_w_new: float32 [512, 1536], P(('dp', 'vocab'))
- out_m_new: float32 [512, 512], P(('dp', 'vocab'))
- out_v_new: float32 [512, 512], P(('dp', 'vocab'))
- out_w_new: float32 [512, 512], P(('dp', 'vocab'))
- up_m_new: float32 [512, 2048], P(('dp', 'vocab'))
- up_v_new: float32 [512, 2048], P(('dp', 'vocab'))
- up_w_new: float32 [512, 2048], P(('dp', 'vocab'))
- down_m_new: float32 [2048, 512], P(('dp', 'vocab'))
- down_v_new: float32 [2048, 512], P(('dp', 'vocab'))
- down_w_new: float32 [2048, 512], P(('dp', 'vocab'))
- gains_m_new: float32 [6, 512], replicated
- gains_v_new: float32 [6, 512], replicated
- gains_w_new: float32 [6, 512], replicated
The draws below stay inside these ranges and needn't reach their ends.
Inputs may be any that keep to these rules, and one draw needn't show every extreme that they name: `segment_ids`: within a row segment numbers never fall; each segment holds 1 to 256 positions. `loss_mask`: 1 marks a position that counts.
All inputs are finite; a program needn't handle non-finite values.
Results may differ from the reference program's by a relative error of at most 0.0072.
Values may be sent and summed in bfloat16 or wider, within the bound.
A program may use at most 320 MiB of HBM per device.

```python
import math
import jax
import jax.numpy as jnp
import numpy as np
from jax import lax

D = 512
FF = 2048
MAXPOS = 512
VOCAB = 30720
TD = 768
FFT = 3072
LEN = 512
SEGS = 8
ROWS = 32
NPARAM = 19139584


def draw_loss_mask(key, part):
    row_index = jnp.arange(ROWS, dtype=jnp.int32)
    limit = 100 + 800 * (2 * row_index + 1) // (2 * ROWS)
    rolls = jax.random.randint(key, (ROWS, LEN), 0, 1000, dtype=jnp.int32)
    return (rolls < limit[:, None]).astype(jnp.int32)


def place_ends(values, rng, low, largest):
    longest = values.shape.index(max(values.shape))
    spots = []
    for shift in (0, 1):
        where = [jax.random.randint(jax.random.fold_in(rng, axis), (), 0, length) for axis, length in enumerate(values.shape)]
        where[longest] = (where[longest] + shift) % values.shape[longest]
        spots.append(tuple(where))
    return values.at[spots[0]].set(low).at[spots[1]].set(largest)


def block_levels(rng, shape, pieces, low, high):
    factor_of = 1.0
    for axis_at, blocks in pieces:
        draws = jax.random.uniform(jax.random.fold_in(jax.random.fold_in(rng, 6), axis_at), (blocks,), jnp.float32, low / len(pieces), high / len(pieces))
        factor_of = factor_of * jnp.repeat(jnp.exp(draws), shape[axis_at] // blocks).reshape((-1,) + (1,) * (len(shape) - 1 - axis_at))
    return factor_of


def rank_table(amount, lean):
    weights = [(1 << 20) // math.isqrt(standing ** lean) + 1 for standing in range(1, amount + 1)]
    scale = 1 + sum(weights) // (1 << 30)
    return np.cumsum(np.array([max(1, weight // scale) for weight in weights]))


def skewed_ids(rng, dims, count, skew):
    grid = rank_table(count, skew)
    pick = jax.random.randint(jax.random.fold_in(rng, 1), dims, 0, int(grid[count - 1]))
    rank = jnp.searchsorted(jnp.asarray(grid, jnp.int32), pick, side="right")
    return jax.random.permutation(jax.random.fold_in(rng, 2), count)[rank].astype(jnp.int32)


def profile(count, total, reach, lean):
    loads = [(1 << 20) // math.isqrt(standing ** lean) + 1 for standing in range(2, count + 1)]
    rest, holding = total - reach - (count - 1), [1] * (count - 1)
    while rest > 0:
        movable = [i for i in range(count - 1) if holding[i] < reach]
        pool, budget = sum([loads[i] for i in movable]), rest
        for i in movable:
            addition = min(reach - holding[i], max(1, budget * loads[i] // pool), rest)
            holding[i] = holding[i] + addition
            rest = rest - addition
    return np.array([reach] + holding)


def ragged(key, count, total, most, skew):
    if count == 2:
        one = jax.random.randint(key, (), max(1, total - most), min(most, total - 1) + 1)
        return jnp.stack([one, total - one])
    sizes = jnp.asarray(profile(count, total, most, skew), jnp.int32)
    couples = (count - 1) // 2
    source_of, sink = sizes[1:1 + 2 * couples:2], sizes[2:2 + 2 * couples:2]
    margin = jnp.minimum(source_of - 1, most - sink)
    passed = jax.random.randint(jax.random.fold_in(key, 1), (couples,), 0, 1 << 20) % (margin + 1)
    sizes = sizes.at[1:1 + 2 * couples:2].set(source_of - passed).at[2:2 + 2 * couples:2].set(sink + passed)
    return sizes[jax.random.permutation(jax.random.fold_in(key, 2), count)]


def scatter_about(own_key, shape, spread, most, cuts=(), kind=jnp.bfloat16):
    loudness = block_levels(own_key, shape, cuts, -0.22, 0.18) if cuts else 1.0
    entries = jax.random.normal(own_key, shape, jnp.float32) * spread * loudness
    return jnp.minimum(jnp.maximum(entries, -most), most).astype(kind)


def setup_inputs(seed: int = 0) -> dict:
    keys = jax.random.split(jax.random.key(seed), 35)
    return {
        "token_ids": place_ends(skewed_ids(keys[0], (ROWS, LEN), VOCAB, 2), jax.random.fold_in(keys[0], 3), 0, VOCAB - 1).astype(jnp.int32),
        "segment_ids": jax.vmap(lambda own: jnp.searchsorted(jnp.cumsum(ragged(own, SEGS, LEN, LEN // 2, 0)), jnp.arange(LEN), side="right"))(jax.random.split(keys[1], ROWS)).reshape((ROWS, LEN)).astype(jnp.int32),
        "labels": place_ends(jax.random.randint(keys[2], (ROWS, LEN), 0, VOCAB), jax.random.fold_in(keys[2], 1), 0, VOCAB - 1).astype(jnp.int32),
        "loss_mask": draw_loss_mask(jax.random.fold_in(keys[34], 71), 0),
        "teacher_group": place_ends(jax.random.randint(keys[4], (ROWS,), 0, 3), jax.random.fold_in(keys[4], 1), 0, 2).astype(jnp.int32),
        "teacher_inputs": scatter_about(keys[5], (ROWS, LEN, TD), 1.0, 6.0, ((0, 32),)),
        "teacher_table": scatter_about(keys[6], (3, TD, VOCAB), (TD // 4) ** -0.5, 0.4375, ((2, 4),)),
        "teacher_qkv": scatter_about(keys[7], (3, TD, 3 * TD), TD ** -0.5, 0.21875, ((1, 32),)),
        "teacher_out": scatter_about(keys[8], (3, TD, TD), (TD // 16) ** -0.5, 0.875, ((1, 32),)),
        "teacher_up": scatter_about(keys[9], (3, TD, FFT), TD ** -0.5, 0.21875, ((1, 32),)),
        "teacher_down": scatter_about(keys[10], (3, FFT, TD), FFT ** -0.5, 0.109375, ((1, 32),)),
        "teacher_gains": jnp.clip(1.0 + 0.1 * jax.random.normal(keys[11], (3, 6, TD), jnp.float32), 0.5, 1.5),
        "step_count": jax.random.randint(keys[12], (), 2, 21).astype(jnp.int32),
        "embed_w": scatter_about(keys[13], (VOCAB, D), (D // 4) ** -0.5, 0.5, ((0, 4), (1, 8)), jnp.float32),
        "embed_m": scatter_about(keys[14], (VOCAB, D), (0.00055 * NPARAM ** -0.5), 1.9073486328125e-06, ((0, 4), (1, 8)), jnp.float32),
        "embed_v": jnp.clip(jnp.exp(math.log(1.0449548161711817e-14) - 2.7725887 * jax.random.uniform(keys[15], (VOCAB, D), jnp.float32) ** block_levels(keys[15], (VOCAB, D), ((0, 4), (1, 8)), -0.2, 0.2)), 6.530967601069886e-16, 1.0449548161711817e-14),
        "pos_w": scatter_about(keys[16], (MAXPOS, D), (D // 4) ** -0.5, 0.5, ((0, 32),), jnp.float32),
        "pos_m": scatter_about(keys[17], (MAXPOS, D), (0.00055 * NPARAM ** -0.5), 1.9073486328125e-06, ((0, 32),), jnp.float32),
        "pos_v": jnp.clip(jnp.exp(math.log(1.0449548161711817e-14) - 2.7725887 * jax.random.uniform(keys[18], (MAXPOS, D), jnp.float32) ** block_levels(keys[18], (MAXPOS, D), ((0, 32),), -0.2, 0.2)), 6.530967601069886e-16, 1.0449548161711817e-14),
        "qkv_w": scatter_about(keys[19], (D, 3 * D), D ** -0.5, 0.25, ((0, 32),), jnp.float32),
        "qkv_m": scatter_about(keys[20], (D, 3 * D), (0.00055 * NPARAM ** -0.5), 1.9073486328125e-06, ((0, 32),), jnp.float32),
        "qkv_v": jnp.clip(jnp.exp(math.log(1.0449548161711817e-14) - 2.7725887 * jax.random.uniform(keys[21], (D, 3 * D), jnp.float32) ** block_levels(keys[21], (D, 3 * D), ((0, 32),), -0.2, 0.2)), 6.530967601069886e-16, 1.0449548161711817e-14),
        "out_w": scatter_about(keys[22], (D, D), (D // 16) ** -0.5, 1.0, ((0, 32),), jnp.float32),
        "out_m": scatter_about(keys[23], (D, D), (0.00055 * NPARAM ** -0.5), 1.9073486328125e-06, ((0, 32),), jnp.float32),
        "out_v": jnp.clip(jnp.exp(math.log(1.0449548161711817e-14) - 2.7725887 * jax.random.uniform(keys[24], (D, D), jnp.float32) ** block_levels(keys[24], (D, D), ((0, 32),), -0.2, 0.2)), 6.530967601069886e-16, 1.0449548161711817e-14),
        "up_w": scatter_about(keys[25], (D, FF), D ** -0.5, 0.25, ((0, 32),), jnp.float32),
        "up_m": scatter_about(keys[26], (D, FF), (0.00055 * NPARAM ** -0.5), 1.9073486328125e-06, ((0, 32),), jnp.float32),
        "up_v": jnp.clip(jnp.exp(math.log(1.0449548161711817e-14) - 2.7725887 * jax.random.uniform(keys[27], (D, FF), jnp.float32) ** block_levels(keys[27], (D, FF), ((0, 32),), -0.2, 0.2)), 6.530967601069886e-16, 1.0449548161711817e-14),
        "down_w": scatter_about(keys[28], (FF, D), FF ** -0.5, 0.125, ((0, 32),), jnp.float32),
        "down_m": scatter_about(keys[29], (FF, D), (0.00055 * NPARAM ** -0.5), 1.9073486328125e-06, ((0, 32),), jnp.float32),
        "down_v": jnp.clip(jnp.exp(math.log(1.0449548161711817e-14) - 2.7725887 * jax.random.uniform(keys[30], (FF, D), jnp.float32) ** block_levels(keys[30], (FF, D), ((0, 32),), -0.2, 0.2)), 6.530967601069886e-16, 1.0449548161711817e-14),
        "gains_w": jnp.clip(1.0 + 0.1 * jax.random.normal(keys[31], (6, D), jnp.float32), 0.5, 1.5),
        "gains_m": scatter_about(keys[32], (6, D), (0.0022 * NPARAM ** -0.5), 7.62939453125e-06, (), jnp.float32),
        "gains_v": jnp.clip(jnp.exp(jax.random.uniform(keys[33], (6, D), jnp.float32, math.log(1.0449548161711817e-14), math.log(1.6719277058738907e-13))), 1.0449548161711817e-14, 1.6719277058738907e-13),
    }


@jax.custom_vjp
def low(v):
    return lax.optimization_barrier(v.astype(jnp.bfloat16)).astype(jnp.float32)

@jax.custom_vjp
def low_back(v):
    return v

def low_keep(v):
    return (low(v), None)

def low_pass(kept, grad):
    return (grad,)

def back_keep(v):
    return (v, None)

def back_low(kept, grad):
    return (low(grad),)
low.defvjp(low_keep, low_pass)
low_back.defvjp(back_keep, back_low)
NORM_EPS = 1e-05
MIX_ALPHA = 0.5
CLIP_NORM = 0.005
LEARN_RATE = 0.03
GAIN_RATE = 0.4
BETA_ONE = 0.9
BETA_TWO = 0.999
ADAM_EPS = 1e-08
WEIGHT_DECAY = 0.01
GELU_C = 0.7978845608028654
HIGHEST = lax.Precision.HIGHEST

def layer_norm(values, gain, shift):
    center = values - lax.optimization_barrier(jnp.mean(values, -1, keepdims=True))
    return center * lax.rsqrt(lax.optimization_barrier(jnp.mean(center * center, -1, keepdims=True)) + NORM_EPS) * gain + shift

def gelu_tanh(values):
    return 0.5 * values * (1.0 + jnp.tanh(GELU_C * (values + 0.044715 * values * values * values)))

def positions(segment):
    codes = jnp.arange(SEGS, dtype=jnp.int32)
    starts = lax.optimization_barrier(jnp.sum((segment[None, :] < codes[:, None]).astype(jnp.int32), 1))
    member = (segment[:, None] == codes[None, :]).astype(jnp.int32)
    return jnp.arange(segment.shape[0], dtype=jnp.int32) - lax.optimization_barrier(jnp.sum(member * starts[None, :], 1))

def log_total(values):
    top = lax.optimization_barrier(jnp.max(values, -1, keepdims=True))
    return top[:, 0] + jnp.log(lax.optimization_barrier(jnp.sum(jnp.exp(values - top), -1)))

def encode(hidden, segment_row, qkv_t, out_t, up_t, down_t, gains):
    seq_len = segment_row.shape[0]
    width = qkv_t.shape[0]
    h_zero = layer_norm(hidden, gains[0], gains[1])
    packed = low_back(low(jnp.dot(low(h_zero), qkv_t, precision=HIGHEST)))
    queries = packed[:, :width].reshape(seq_len, -1, 64)
    keys_all = packed[:, width:2 * width].reshape(seq_len, -1, 64)
    values_all = packed[:, 2 * width:].reshape(seq_len, -1, 64)
    scores = low_back(jnp.einsum('qhd,khd->hqk', queries, keys_all, precision=HIGHEST) * 0.125)
    same = (segment_row[:, None] == segment_row[None, :])[None]
    scores = jnp.where(same, scores, -1e+30)
    scores = scores - lax.optimization_barrier(jnp.max(scores, -1, keepdims=True))
    expd = jnp.exp(scores)
    probs = low(expd / lax.optimization_barrier(jnp.sum(expd, -1, keepdims=True)))
    context = jnp.einsum('hqk,khd->qhd', probs, values_all, precision=HIGHEST).reshape(seq_len, width)
    context = low_back(low(context))
    h_one = layer_norm(h_zero + low_back(jnp.dot(context, out_t, precision=HIGHEST)), gains[2], gains[3])
    inner = low_back(jnp.dot(low(h_one), up_t, precision=HIGHEST))
    branch = low_back(jnp.dot(low(gelu_tanh(inner)), down_t, precision=HIGHEST))
    return layer_norm(h_one + branch, gains[4], gains[5])

def row_loss(params, teacher_f32, token_row, segment_row, label_row, mask_row, group_one, state_row):
    embed, pos_t, qkv_t, out_t, up_t, down_t, gains = params
    hidden = embed[token_row] + pos_t[positions(segment_row)]
    h_two = encode(hidden, segment_row, qkv_t, out_t, up_t, down_t, gains)
    student = low_back(jnp.dot(low(h_two), embed.T, precision=HIGHEST))
    teacher = low(jnp.dot(state_row, teacher_f32[group_one], precision=HIGHEST))
    student_lse = log_total(student)
    teacher_lse = log_total(teacher)
    teacher_prob = jnp.exp(teacher - teacher_lse[:, None])
    diverge = lax.optimization_barrier(jnp.sum(teacher_prob * (teacher - student), -1)) - teacher_lse + student_lse
    picked = jnp.take_along_axis(student, label_row[:, None], 1)[:, 0]
    return jnp.sum(mask_row.astype(jnp.float32) * (MIX_ALPHA * diverge + student_lse - picked))

def adam(weight, first, second, grad, fix_one, fix_two, rate):
    first = BETA_ONE * first + (1.0 - BETA_ONE) * grad
    second = BETA_TWO * second + (1.0 - BETA_TWO) * grad * grad
    update = first / fix_one / (jnp.sqrt(second / fix_two) + ADAM_EPS)
    return (first, second, weight - rate * (update + WEIGHT_DECAY * weight))

def reference(token_ids, segment_ids, labels, loss_mask, teacher_group, teacher_inputs, teacher_table, teacher_qkv, teacher_out, teacher_up, teacher_down, teacher_gains, step_count, embed_w, embed_m, embed_v, pos_w, pos_m, pos_v, qkv_w, qkv_m, qkv_v, out_w, out_m, out_v, up_w, up_m, up_v, down_w, down_m, down_v, gains_w, gains_m, gains_v):
    masters = (embed_w, pos_w, qkv_w, out_w, up_w, down_w)
    params = tuple((lax.optimization_barrier(w.astype(jnp.bfloat16)).astype(jnp.float32) for w in masters)) + (gains_w,)
    teacher_f32 = teacher_table.astype(jnp.float32)
    teacher_layers = tuple((w.astype(jnp.float32) for w in (teacher_qkv, teacher_out, teacher_up, teacher_down)))

    def teacher_row(item):
        inputs_row, segment_row, group = item
        return low(encode(inputs_row.astype(jnp.float32), segment_row, teacher_layers[0][group], teacher_layers[1][group], teacher_layers[2][group], teacher_layers[3][group], teacher_gains[group]))
    teacher_hidden = lax.map(teacher_row, (teacher_inputs, segment_ids, teacher_group))
    counted = jnp.maximum(jnp.sum(loss_mask.astype(jnp.float32)), 1.0)
    checked = jax.checkpoint(row_loss)

    def total_loss(weights):

        def one_row(carry, row):
            token_row, segment_row, label_row, mask_row, group_one, state_row = row
            term = checked(weights, teacher_f32, token_row, segment_row, label_row, mask_row, group_one, state_row)
            return (carry + term, None)
        total, unused = lax.scan(one_row, jnp.float32(0.0), (token_ids, segment_ids, labels, loss_mask, teacher_group, teacher_hidden))
        return total / counted
    loss, pullback = jax.vjp(total_loss, params)
    grads = pullback(jnp.float32(1.0))[0]
    squares = jnp.float32(0.0)
    for grad in grads:
        squares = squares + jnp.sum(grad * grad)
    grad_norm = jnp.sqrt(squares)
    factor = CLIP_NORM / jnp.maximum(grad_norm, CLIP_NORM)
    count_f = step_count.astype(jnp.float32)
    fix_one = 1.0 - jnp.power(BETA_ONE, count_f)
    fix_two = 1.0 - jnp.power(BETA_TWO, count_f)
    e_m, e_v, e_w = adam(embed_w, embed_m, embed_v, grads[0] * factor, fix_one, fix_two, LEARN_RATE)
    p_m, p_v, p_w = adam(pos_w, pos_m, pos_v, grads[1] * factor, fix_one, fix_two, LEARN_RATE)
    q_m, q_v, q_w = adam(qkv_w, qkv_m, qkv_v, grads[2] * factor, fix_one, fix_two, LEARN_RATE)
    o_m, o_v, o_w = adam(out_w, out_m, out_v, grads[3] * factor, fix_one, fix_two, LEARN_RATE)
    u_m, u_v, u_w = adam(up_w, up_m, up_v, grads[4] * factor, fix_one, fix_two, LEARN_RATE)
    d_m, d_v, d_w = adam(down_w, down_m, down_v, grads[5] * factor, fix_one, fix_two, LEARN_RATE)
    g_m, g_v, g_w = adam(gains_w, gains_m, gains_v, grads[6] * factor, fix_one, fix_two, GAIN_RATE)
    return (loss, grad_norm, e_m, e_v, e_w, p_m, p_v, p_w, q_m, q_v, q_w, o_m, o_v, o_w, u_m, u_v, u_w, d_m, d_v, d_w, g_m, g_v, g_w)
```

```python
import functools

import jax
import jax.numpy as jnp
from jax import lax
from jax.experimental import pallas as pl
from jax.experimental.pallas import tpu as pltpu
from jax.sharding import PartitionSpec as P

SEGS = 8
NORM_EPS = 1e-05
MIX_ALPHA = 0.5
CLIP_NORM = 0.005
LEARN_RATE = 0.03
GAIN_RATE = 0.4
BETA_ONE = 0.9
BETA_TWO = 0.999
ADAM_EPS = 1e-08
WEIGHT_DECAY = 0.01
GELU_C = 0.7978845608028654
MESH = pl.DeviceIdType.MESH
F32 = jnp.float32
B16 = jnp.bfloat16
ANYWHERE = pl.BlockSpec(memory_space=pl.ANY)
IN_VMEM = pl.BlockSpec(memory_space=pltpu.VMEM)
MIB = 1 << 20

CYCLES = (
    (0, 1, 3, 2, 6, 7, 5, 9, 11, 10, 14, 15, 13, 12, 8, 4),
    (0, 1, 5, 4, 6, 10, 8, 9, 13, 12, 14, 15, 11, 7, 3, 2),
    (0, 2, 6, 7, 3, 1, 5, 9, 13, 15, 11, 10, 14, 12, 8, 4),
)


def chip_cycle(count, which):
    return CYCLES[which] if count == 16 else tuple(range(count))


def dp_cycle(count):
    return tuple(range(0, count, 2)) + tuple(range(count - 1 - count % 2, 0, -2))


def lookup(table, index):
    out = jnp.int32(table[0])
    for k in range(1, len(table)):
        out = jnp.where(index == k, table[k], out)
    return out


class Ring:
    def __init__(self, D, V, which):
        self.D, self.V = D, V
        d, v = lax.axis_index("dp"), lax.axis_index("vocab")
        self.core, self.v = lax.rem(v, 2), v
        self.over_dp = which == "dp"
        self.n = D if self.over_dp else D * V // 2
        self.table = dp_cycle(D) if self.over_dp else chip_cycle(self.n, which)
        self.me = d if self.over_dp else d * (V // 2) + v // 2
        inverse = tuple(self.table.index(k) for k in range(self.n))
        self.pos = lookup(inverse, self.me)

    def at(self, ahead):
        return lookup(self.table, lax.rem(self.pos + ahead + self.n, self.n))

    def device(self, place):
        if self.over_dp:
            return (place, self.v)
        half = self.V // 2
        return (place // half, lax.rem(place, half) * 2 + self.core)

    def hops(self, parity):
        more, less = self.n // 2, self.n - 1 - self.n // 2
        return (more, less) if parity == 0 else (less, more)


def sibling():
    v = lax.axis_index("vocab")
    return (lax.axis_index("dp"), v + 1 - 2 * lax.rem(v, 2))


def greet(devices):
    barrier = pltpu.get_barrier_semaphore()
    for device in devices:
        pl.semaphore_signal(barrier, inc=1, device_id=device, device_id_type=MESH)
    pl.semaphore_wait(barrier, len(devices))


def on_condition(condition, body):
    if condition is True:
        body()
    elif condition is not False:
        pl.when(condition)(body)


def gather_kernel(D, V, spec, count, *refs):
    ins, outs = refs[:count], refs[count : 2 * count]
    ssem, rsem, xssem, xrsem, lsem = refs[2 * count :]
    rings = {w: Ring(D, V, w) for w in dict.fromkeys(p[3] for p in spec)}
    core = lax.rem(lax.axis_index("vocab"), 2)
    sib = sibling()
    nexts = {w: (r.at(1), r.at(-1)) for w, r in rings.items()}
    both = any(p[3] != "dp" for p in spec)
    greet(
        [r.device(place) for w, r in rings.items() for place in nexts[w]]
        + ([sib] if both else [])
    )

    def dst(piece, slot):
        which, k, lead, _, _ = piece
        return outs[which].at[k, slot] if lead else outs[which].at[slot, k]

    def slot_of(ring, place):
        return place if ring.over_dp else place * 2 + core

    streams = []
    for number, piece in enumerate(spec):
        ring = rings[piece[3]]
        for turn, hops in zip((0, 1), ring.hops(piece[4])):
            streams.append((piece, ring, turn, hops, number))

    def origin(stream, s):
        _, ring, turn, _, _ = stream
        return slot_of(ring, ring.at(-s) if turn == 0 else ring.at(s))

    def remote(i, s, src, slot):
        piece, ring, turn, _, _ = streams[i]
        return pltpu.make_async_remote_copy(
            src_ref=src,
            dst_ref=dst(piece, slot),
            send_sem=ssem.at[s, i],
            recv_sem=rsem.at[s, i],
            device_id=ring.device(nexts[piece[3]][turn]),
            device_id_type=MESH,
        )

    def across(i, s, src, slot):
        return pltpu.make_async_remote_copy(
            src_ref=src,
            dst_ref=dst(streams[i][0], slot),
            send_sem=xssem.at[s, i],
            recv_sem=xrsem.at[s, i],
            device_id=sib,
            device_id_type=MESH,
        )

    def own(i):
        piece, ring, _, _, _ = streams[i]
        return ins[piece[0]].at[piece[1]], slot_of(ring, ring.me)

    for i in range(len(streams)):
        remote(i, 0, *own(i)).start()
    for i, stream in enumerate(streams):
        if stream[2] == 0:
            src, slot = own(i)
            pltpu.make_async_copy(src, dst(stream[0], slot), lsem.at[stream[4]]).start()
            if not stream[1].over_dp:
                across(i, 0, src, slot).start()
    longest = max(s[3] for s in streams)

    def within(s, hops):
        return True if hops == longest else s <= hops

    def body(s, carry):
        for i, stream in enumerate(streams):

            def take(i=i, stream=stream):
                slot = origin(stream, s)
                block = dst(stream[0], slot)
                remote(i, s - 1, block, slot).wait_recv()
                pl.when(s < stream[3])(lambda: remote(i, s, block, slot).start())
                if not stream[1].over_dp:
                    across(i, s, block, slot).start()

            on_condition(within(s, stream[3]), take)
        return carry

    lax.fori_loop(1, longest + 1, body, 0)

    def finish(s, carry):
        for i, stream in enumerate(streams):

            def end(i=i, stream=stream):
                slot = origin(stream, s)
                block = dst(stream[0], slot)
                pl.when(s < stream[3])(lambda: remote(i, s, block, slot).wait_send())
                if not stream[1].over_dp:

                    def crossed():
                        across(i, s, block, slot).wait_send()
                        theirs = slot + 1 - 2 * core
                        across(i, s, block, theirs).wait_recv()

                    on_condition(True if stream[2] == 0 else s > 0, crossed)

            on_condition(within(s, stream[3]), end)
        return carry

    lax.fori_loop(0, longest + 1, finish, 0)
    for i, stream in enumerate(streams):
        if stream[2] == 0:
            src, slot = own(i)
            pltpu.make_async_copy(src, dst(stream[0], slot), lsem.at[stream[4]]).wait()


def ring_gather(D, V, arrays, spec, ident):
    shapes = []
    for which, array in enumerate(arrays):
        piece = next(p for p in spec if p[0] == which)
        places = D if piece[3] == "dp" else D * V
        lead = array.shape[:1]
        shape = lead + (places,) if piece[2] else (places,) + lead
        shapes.append(jax.ShapeDtypeStruct(shape + array.shape[1:], array.dtype))
    longest = max((D if p[3] == "dp" else D * V // 2) // 2 for p in spec) + 1
    sems = pltpu.SemaphoreType.DMA((longest, 2 * len(spec)))
    return pl.pallas_call(
        functools.partial(gather_kernel, D, V, spec, len(arrays)),
        out_shape=shapes,
        in_specs=[ANYWHERE] * len(arrays),
        out_specs=[ANYWHERE] * len(arrays),
        scratch_shapes=[sems] * 4 + [pltpu.SemaphoreType.DMA((len(spec),))],
        compiler_params=pltpu.CompilerParams(collective_id=ident, has_side_effects=True),
    )(*arrays)


def scatter_kernel(D, V, spec, *refs):
    count = len(spec)
    ins, outs = refs[:count], refs[count : 2 * count]
    scratch = list(refs[2 * count :])
    ssem, rsem, xssem, xrsem = scratch[-4:]
    rings = {w: Ring(D, V, w) for w in dict.fromkeys(p[0] for p in spec)}
    core = lax.rem(lax.axis_index("vocab"), 2)
    sib = sibling()
    nexts = {w: (r.at(1), r.at(-1)) for w, r in rings.items()}
    crossing = any(w != "dp" for w in rings)
    greet(
        [r.device(place) for w, r in rings.items() for place in nexts[w]]
        + ([sib] if crossing else [])
    )
    sums, slots = [], []
    for number, (which, parity) in enumerate(spec):
        if which == "dp":
            sums.append(ins[number])
        else:
            sums.append(scratch.pop(0))
        slots.append((scratch.pop(0), scratch.pop(0)))
    streams = []
    for number, (which, parity) in enumerate(spec):
        for turn, hops in zip((0, 1), rings[which].hops(parity)):
            streams.append((number, rings[which], turn, hops, which))
    streams = [s for s in streams if s[3] > 0]

    def place(stream, ahead):
        return stream[1].at(ahead) if stream[2] == 0 else stream[1].at(-ahead)

    def remote(i, s, src):
        number, ring, turn, hops, which = streams[i]
        return pltpu.make_async_remote_copy(
            src_ref=src,
            dst_ref=slots[number][turn].at[s],
            send_sem=ssem.at[s, i],
            recv_sem=rsem.at[s, i],
            device_id=ring.device(nexts[which][turn]),
            device_id_type=MESH,
        )

    def across(number):
        return pltpu.make_async_remote_copy(
            src_ref=ins[number].at[:, 1 - core],
            dst_ref=sums[number],
            send_sem=xssem.at[number],
            recv_sem=xrsem.at[number],
            device_id=sib,
            device_id_type=MESH,
        )

    def first(i):
        number, _, _, hops, _ = streams[i]
        return remote(i, 0, sums[number].at[place(streams[i], hops)])

    for number, (which, _) in enumerate(spec):
        if which != "dp":
            across(number).start()
    for i, stream in enumerate(streams):
        if stream[4] == "dp":
            first(i).start()
    for number, (which, _) in enumerate(spec):
        if which != "dp":
            across(number).wait_recv()

            def add(k, carry, number=number):
                total = sums[number][k].astype(F32) + ins[number][k, core].astype(F32)
                sums[number][k] = total.astype(B16)
                return carry

            lax.fori_loop(0, rings[which].n, add, 0)
            for i, stream in enumerate(streams):
                if stream[0] == number:
                    first(i).start()
    longest = max(s[3] for s in streams)
    stride = {w: max(1, longest // max(max(r.hops(0)), 1)) for w, r in rings.items()}

    def body(s, carry):
        for i, stream in enumerate(streams):
            number, ring, turn, hops, which = stream
            by = stride[which]

            def take(i=i, stream=stream, number=number, turn=turn, hops=hops, by=by):
                step = s // by
                block = slots[number][turn].at[step - 1]
                remote(i, step - 1, block).wait_recv()

                def onward():
                    mine = sums[number].at[place(stream, hops - step)]
                    block[...] = (block[...].astype(F32) + mine[...].astype(F32)).astype(B16)
                    remote(i, step, block).start()

                pl.when(step < hops)(onward)

            condition = True
            if by > 1 or hops * by < longest:
                condition = (lax.rem(s, by) == 0) & (s // by <= hops)
            on_condition(condition, take)
        return carry

    lax.fori_loop(1, longest + 1, body, 0)
    for number, (which, parity) in enumerate(spec):
        total = sums[number][rings[which].me].astype(F32)
        for turn, hops in zip((0, 1), rings[which].hops(parity)):
            if hops > 0:
                total = total + slots[number][turn][hops - 1].astype(F32)
        outs[number][...] = total
    for i, stream in enumerate(streams):
        number, ring, turn, hops, which = stream
        first(i).wait_send()

        def sent(s, carry, i=i, number=number, turn=turn):
            remote(i, s, slots[number][turn].at[s - 1]).wait_send()
            return carry

        lax.fori_loop(1, hops, sent, 0)
    for number, (which, _) in enumerate(spec):
        if which != "dp":
            across(number).wait_send()


def ring_scatter(D, V, arrays, spec, ident):
    scratch, shapes = [], []
    for array, (which, parity) in zip(arrays, spec):
        block = array.shape[-2:]
        n = D if which == "dp" else D * V // 2
        if which != "dp":
            scratch.append(pltpu.VMEM((n,) + block, B16))
        more, less = n // 2, n - 1 - n // 2
        scratch += [pltpu.VMEM((max(k, 1),) + block, B16) for k in ((more, less), (less, more))[parity]]
        shapes.append(jax.ShapeDtypeStruct(block, F32))
    longest = max((D if w == "dp" else D * V // 2) // 2 for w, _ in spec)
    sems = pltpu.SemaphoreType.DMA((longest, 2 * len(spec)))
    single = pltpu.SemaphoreType.DMA((len(spec),))
    return pl.pallas_call(
        functools.partial(scatter_kernel, D, V, spec),
        out_shape=shapes,
        in_specs=[IN_VMEM] * len(arrays),
        out_specs=[IN_VMEM] * len(arrays),
        scratch_shapes=scratch + [sems, sems, single, single],
        compiler_params=pltpu.CompilerParams(
            collective_id=ident, has_side_effects=True, vmem_limit_bytes=56 * MIB
        ),
    )(*arrays)


def vocab_gather_kernel(V, count, *refs):
    ins, outs = refs[:count], refs[count : 2 * count]
    ssem, rsem, xssem, xrsem, lsem = refs[2 * count :]
    d, v = lax.axis_index("dp"), lax.axis_index("vocab")
    half = V // 2
    core, chip = lax.rem(v, 2), v // 2
    sib = sibling()

    def other(k):
        return lax.rem(chip + k + half, half) * 2 + core

    greet([(d, other(k)) for k in range(1, half)] + [sib])

    def send(q, k):
        return pltpu.make_async_remote_copy(
            src_ref=ins[q],
            dst_ref=outs[q].at[v],
            send_sem=ssem.at[q, k],
            recv_sem=rsem.at[q, k],
            device_id=(d, other(k)),
            device_id_type=MESH,
        )

    def across(q, k, src, slot):
        return pltpu.make_async_remote_copy(
            src_ref=src,
            dst_ref=outs[q].at[slot],
            send_sem=xssem.at[q, k],
            recv_sem=xrsem.at[q, k],
            device_id=sib,
            device_id_type=MESH,
        )

    for q in range(count):
        for k in range(1, half):
            send(q, k).start()
    for q in range(count):
        across(q, 0, ins[q], v).start()
        pltpu.make_async_copy(ins[q], outs[q].at[v], lsem.at[q]).start()
    for q in range(count):
        for k in range(1, half):
            slot = other(-k)
            send(q, k).wait_recv()
            across(q, k, outs[q].at[slot], slot).start()
    for q in range(count):
        pltpu.make_async_copy(ins[q], outs[q].at[v], lsem.at[q]).wait()
        for k in range(half):
            slot = other(-k)
            if k:
                send(q, k).wait_send()
            across(q, k, outs[q].at[slot], slot).wait_send()
            across(q, k, outs[q].at[slot], slot + 1 - 2 * core).wait_recv()


def vocab_gather(V, arrays, ident):
    count = len(arrays)
    sems = pltpu.SemaphoreType.DMA((count, V // 2))
    return pl.pallas_call(
        functools.partial(vocab_gather_kernel, V, count),
        out_shape=[jax.ShapeDtypeStruct((V,) + a.shape, a.dtype) for a in arrays],
        in_specs=[ANYWHERE] * count,
        out_specs=[ANYWHERE] * count,
        scratch_shapes=[sems] * 4 + [pltpu.SemaphoreType.DMA((count,))],
        compiler_params=pltpu.CompilerParams(collective_id=ident, has_side_effects=True),
    )(*arrays)


def vocab_scatter_kernel(V, in_ref, out_ref, sums, taken, ssem, rsem, xsem):
    d, v = lax.axis_index("dp"), lax.axis_index("vocab")
    half = V // 2
    core, chip = lax.rem(v, 2), v // 2
    sib = sibling()

    def other(k):
        return lax.rem(chip + k + half, half)

    greet([(d, other(k) * 2 + core) for k in range(1, half)] + [sib])
    across = pltpu.make_async_remote_copy(
        src_ref=in_ref.at[:, 1 - core],
        dst_ref=sums,
        send_sem=xsem.at[0],
        recv_sem=xsem.at[1],
        device_id=sib,
        device_id_type=MESH,
    )
    across.start()
    across.wait_recv()

    def send(k):
        return pltpu.make_async_remote_copy(
            src_ref=sums.at[other(k)],
            dst_ref=taken.at[k - 1],
            send_sem=ssem.at[k - 1],
            recv_sem=rsem.at[k - 1],
            device_id=(d, other(k) * 2 + core),
            device_id_type=MESH,
        )

    for k in [*range(1, half), 0]:
        to = other(k)
        total = sums[to].astype(F32) + in_ref[to, core].astype(F32)
        sums[to] = total.astype(B16)
        if k:
            send(k).start()
    total = sums[chip].astype(F32)
    for k in range(1, half):
        send(k).wait_recv()
        total = total + taken[k - 1].astype(F32)
    out_ref[...] = total
    for k in range(1, half):
        send(k).wait_send()
    across.wait_send()


def vocab_scatter(V, array, ident):
    half = V // 2
    block = array.shape[1:]
    sems = pltpu.SemaphoreType.DMA((max(half - 1, 1),))
    return pl.pallas_call(
        functools.partial(vocab_scatter_kernel, V),
        out_shape=jax.ShapeDtypeStruct(block, F32),
        in_specs=[IN_VMEM],
        out_specs=IN_VMEM,
        scratch_shapes=[
            pltpu.VMEM((half,) + block, B16),
            pltpu.VMEM((max(half - 1, 1),) + block, B16),
            sems,
            sems,
            pltpu.SemaphoreType.DMA((2,)),
        ],
        compiler_params=pltpu.CompilerParams(
            collective_id=ident, has_side_effects=True, vmem_limit_bytes=40 * MIB
        ),
    )(array.reshape((half, 2) + block))


def total_kernel(D, V, in_ref, out_ref, first, second, ssem, rsem):
    d, v = lax.axis_index("dp"), lax.axis_index("vocab")
    peers = [(d, lax.rem(v + k, V)) for k in range(1, V)]
    peers += [(lax.rem(d + k, D), v) for k in range(1, D)]
    greet(peers)

    def send(k):
        over = first if k < V - 1 else second
        mine = v if k < V - 1 else d
        return pltpu.make_async_remote_copy(
            src_ref=over.at[mine],
            dst_ref=over.at[mine],
            send_sem=ssem.at[k],
            recv_sem=rsem.at[k],
            device_id=peers[k],
            device_id_type=MESH,
        )

    def stage(slots, mine, value, low, high):
        slots[mine] = value
        for k in range(low, high):
            send(k).start()
        for k in range(low, high):
            send(k).wait_recv()
        total = slots[0]
        for k in range(1, slots.shape[0]):
            total = total + slots[k]
        return total

    total = stage(first, v, in_ref[...], 0, V - 1)
    out_ref[...] = stage(second, d, total, V - 1, V + D - 2)
    for k in range(V + D - 2):
        send(k).wait_send()


def total_all(D, V, array, ident):
    sems = pltpu.SemaphoreType.DMA((V + D - 2,))
    return pl.pallas_call(
        functools.partial(total_kernel, D, V),
        out_shape=jax.ShapeDtypeStruct(array.shape, F32),
        in_specs=[IN_VMEM],
        out_specs=IN_VMEM,
        scratch_shapes=[pltpu.VMEM((V,) + array.shape, F32), pltpu.VMEM((D,) + array.shape, F32), sems, sems],
        compiler_params=pltpu.CompilerParams(collective_id=ident, has_side_effects=True),
    )(array)


def tile_of(size):
    return next(t for t in (1280, 768, 512, 256, 128) if size % t == 0)


def lane_fold(values, combine):
    out = values[:, :128]
    for k in range(1, values.shape[1] // 128):
        out = combine(out, values[:, k * 128 : (k + 1) * 128])
    return out


def running(values, top_ref, sum_ref, rows):
    old = top_ref[rows, :]
    top = jnp.maximum(old, lane_fold(values, jnp.maximum))
    fade = jnp.exp(old - top)
    expd = jnp.concatenate(
        [jnp.exp(values[:, k * 128 : (k + 1) * 128] - top) for k in range(values.shape[1] // 128)], 1
    )
    top_ref[rows, :] = top
    sum_ref[rows, :] = sum_ref[rows, :] * fade + lane_fold(expd, jnp.add)
    return expd, fade


def pack_rows(columns):
    lane = lax.broadcasted_iota(jnp.int32, (columns[0].shape[0], 128), 1)
    packed = jnp.zeros(lane.shape, F32)
    for k, column in enumerate(columns):
        packed = jnp.where(lane == k, column, packed)
    return packed.T[:8]


def student_stats_kernel(block, hidden_ref, table_ref, out_ref, top_ref, sum_ref):
    step = pl.program_id(0)

    @pl.when(step == 0)
    def _():
        top_ref[...] = jnp.full(top_ref.shape, -jnp.inf, F32)
        sum_ref[...] = jnp.zeros(sum_ref.shape, F32)

    def one(k, carry):
        rows = pl.ds(pl.multiple_of(k * block, block), block)
        logits = jnp.dot(hidden_ref[rows, :], table_ref[...], preferred_element_type=F32)
        running(logits, top_ref, sum_ref, rows)
        return carry

    lax.fori_loop(0, hidden_ref.shape[0] // block, one, 0)

    @pl.when(step == pl.num_programs(0) - 1)
    def _():
        top = jnp.max(top_ref[...], 1, keepdims=True)
        total = jnp.sum(sum_ref[...] * jnp.exp(top_ref[...] - top), 1, keepdims=True)
        out_ref[...] = pack_rows([top, total])


def student_stats(hidden, table):
    tokens, width = hidden.shape
    size = table.shape[1]
    tile = tile_of(size)
    return pl.pallas_call(
        functools.partial(student_stats_kernel, 256),
        grid=(size // tile,),
        out_shape=jax.ShapeDtypeStruct((8, tokens), F32),
        in_specs=[
            pl.BlockSpec((tokens, width), lambda j: (0, 0)),
            pl.BlockSpec((width, tile), lambda j: (0, j)),
        ],
        out_specs=pl.BlockSpec((8, tokens), lambda j: (0, 0)),
        scratch_shapes=[pltpu.VMEM((tokens, 128), F32)] * 2,
        compiler_params=pltpu.CompilerParams(vmem_limit_bytes=48 * MIB),
    )(hidden, table)


def student_grad_kernel(
    block, hidden_ref, turned_ref, table_ref, lse_ref, weight_ref, label_ref, dh_ref, grad_ref, pick_ref
):
    step = pl.program_id(0)
    tile = table_ref.shape[1]

    @pl.when(step == 0)
    def _():
        dh_ref[...] = jnp.zeros(dh_ref.shape, F32)
        pick_ref[...] = jnp.zeros(pick_ref.shape, F32)

    grad_ref[...] = jnp.zeros(grad_ref.shape, F32)

    def one(k, carry):
        rows = pl.ds(pl.multiple_of(k * block, block), block)
        logits = jnp.dot(hidden_ref[rows, :], table_ref[...], preferred_element_type=F32)
        soft = jnp.exp(logits - lse_ref[rows, :])
        weight = weight_ref[rows, :]
        lane = lax.broadcasted_iota(jnp.int32, logits.shape, 1)
        hit = lane == label_ref[rows, :] - step * tile
        dlogits = (((1.0 + MIX_ALPHA) * weight) * soft - jnp.where(hit, weight, 0.0)).astype(B16)
        pick_ref[rows, :] += lane_fold(jnp.where(hit, logits, 0.0), jnp.add)
        dh_ref[rows, :] += lax.dot_general(
            dlogits, table_ref[...], (((1,), (1,)), ((), ())), preferred_element_type=F32
        )
        grad_ref[...] += jnp.dot(turned_ref[:, rows], dlogits, preferred_element_type=F32)
        return carry

    lax.fori_loop(0, hidden_ref.shape[0] // block, one, 0)


def student_grad(hidden, turned, table, lse, weight, label):
    tokens, width = hidden.shape
    size = table.shape[1]
    tile = tile_of(size)
    whole = lambda *shape: pl.BlockSpec(shape, lambda j: (0, 0))
    return pl.pallas_call(
        functools.partial(student_grad_kernel, 512),
        grid=(size // tile,),
        out_shape=[
            jax.ShapeDtypeStruct((tokens, width), F32),
            jax.ShapeDtypeStruct((width, size), F32),
            jax.ShapeDtypeStruct((tokens, 128), F32),
        ],
        in_specs=[
            whole(tokens, width),
            whole(width, tokens),
            pl.BlockSpec((width, tile), lambda j: (0, j)),
            whole(tokens, 1),
            whole(tokens, 1),
            whole(tokens, 1),
        ],
        out_specs=[
            whole(tokens, width),
            pl.BlockSpec((width, tile), lambda j: (0, j)),
            whole(tokens, 128),
        ],
        compiler_params=pltpu.CompilerParams(vmem_limit_bytes=56 * MIB),
    )(hidden, turned, table, lse, weight, label)


def teacher_stats_kernel(group_ref, hidden_ref, table_ref, out_ref, stats_ref, top_ref, sum_ref, cross_ref):
    step, row = pl.program_id(0), pl.program_id(1)
    length = hidden_ref.shape[1]
    rows = pl.ds(pl.multiple_of(row * length, length), length)

    @pl.when(step == 0)
    def _():
        top_ref[rows, :] = jnp.full((length, 128), -jnp.inf, F32)
        sum_ref[rows, :] = jnp.zeros((length, 128), F32)
        cross_ref[rows, :] = jnp.zeros((length, 128), F32)

    rounded = jnp.dot(hidden_ref[0], table_ref[0], preferred_element_type=F32).astype(B16)
    out_ref[0] = rounded
    values = rounded.astype(F32)
    expd, fade = running(values, top_ref, sum_ref, rows)
    cross_ref[rows, :] = cross_ref[rows, :] * fade + lane_fold(expd * values, jnp.add)

    @pl.when((step == pl.num_programs(0) - 1) & (row == pl.num_programs(1) - 1))
    def _():
        top = jnp.max(top_ref[...], 1, keepdims=True)
        scale = jnp.exp(top_ref[...] - top)
        total = jnp.sum(sum_ref[...] * scale, 1, keepdims=True)
        cross = jnp.sum(cross_ref[...] * scale, 1, keepdims=True)
        stats_ref[...] = pack_rows([top, total, cross])


def teacher_stats(groups, hidden, tables):
    count, length, width = hidden.shape
    size = tables.shape[2]
    tile = tile_of(size)
    tokens = count * length
    return pl.pallas_call(
        teacher_stats_kernel,
        grid_spec=pltpu.PrefetchScalarGridSpec(
            num_scalar_prefetch=1,
            grid=(size // tile, count),
            in_specs=[
                pl.BlockSpec((1, length, width), lambda j, r, g: (r, 0, 0)),
                pl.BlockSpec((1, width, tile), lambda j, r, g: (g[r], 0, j)),
            ],
            out_specs=[
                pl.BlockSpec((1, length, tile), lambda j, r, g: (r, 0, j)),
                pl.BlockSpec((8, tokens), lambda j, r, g: (0, 0)),
            ],
            scratch_shapes=[pltpu.VMEM((tokens, 128), F32)] * 3,
        ),
        out_shape=[
            jax.ShapeDtypeStruct((count, length, size), B16),
            jax.ShapeDtypeStruct((8, tokens), F32),
        ],
        compiler_params=pltpu.CompilerParams(vmem_limit_bytes=48 * MIB),
    )(groups, hidden, tables)


def teacher_grad_kernel(teacher_ref, turned_ref, table_ref, lse_ref, weight_ref, gradin_ref, dh_ref, grad_ref):
    step = pl.program_id(0)
    count, length = teacher_ref.shape[:2]

    @pl.when(step == 0)
    def _():
        dh_ref[...] = jnp.zeros(dh_ref.shape, F32)

    grad_ref[...] = gradin_ref[...]

    def one(k, carry):
        rows = pl.ds(pl.multiple_of(k * length, length), length)
        target = jnp.exp(teacher_ref[k].astype(F32) - lse_ref[rows, :])
        dlogits = ((-MIX_ALPHA * weight_ref[rows, :]) * target).astype(B16)
        dh_ref[rows, :] += lax.dot_general(
            dlogits, table_ref[...], (((1,), (1,)), ((), ())), preferred_element_type=F32
        )
        grad_ref[...] += jnp.dot(turned_ref[:, rows], dlogits, preferred_element_type=F32)
        return carry

    lax.fori_loop(0, count, one, 0)


def teacher_grad(teacher, turned, table, lse, weight, grad):
    count, length, size = teacher.shape
    width, tokens = turned.shape
    tile = tile_of(size)
    whole = lambda *shape: pl.BlockSpec(shape, lambda j: (0, 0))
    return pl.pallas_call(
        teacher_grad_kernel,
        grid=(size // tile,),
        out_shape=[jax.ShapeDtypeStruct((tokens, width), F32), jax.ShapeDtypeStruct((width, size), F32)],
        in_specs=[
            pl.BlockSpec((count, length, tile), lambda j: (0, 0, j)),
            whole(width, tokens),
            pl.BlockSpec((width, tile), lambda j: (0, j)),
            whole(tokens, 1),
            whole(tokens, 1),
            pl.BlockSpec((width, tile), lambda j: (0, j)),
        ],
        out_specs=[whole(tokens, width), pl.BlockSpec((width, tile), lambda j: (0, j))],
        compiler_params=pltpu.CompilerParams(vmem_limit_bytes=60 * MIB),
    )(teacher, turned, table, lse, weight, grad)


def pick_kernel(block, ids_ref, table_ref, out_ref):
    step = pl.program_id(0)
    tile = table_ref.shape[1]

    @pl.when(step == 0)
    def _():
        out_ref[...] = jnp.zeros(out_ref.shape, F32)

    def one(k, carry):
        rows = pl.ds(pl.multiple_of(k * block, block), block)
        lane = lax.broadcasted_iota(jnp.int32, (block, tile), 1)
        hit = jnp.where(lane == ids_ref[rows, :] - step * tile, 1.0, 0.0).astype(B16)
        out_ref[rows, :] += lax.dot_general(
            hit, table_ref[...], (((1,), (1,)), ((), ())), preferred_element_type=F32
        )
        return carry

    lax.fori_loop(0, ids_ref.shape[0] // block, one, 0)


def pick_rows(ids, table):
    tokens = ids.shape[0]
    width, size = table.shape
    tile = tile_of(size)
    return pl.pallas_call(
        functools.partial(pick_kernel, 512),
        grid=(size // tile,),
        out_shape=jax.ShapeDtypeStruct((tokens, width), F32),
        in_specs=[
            pl.BlockSpec((tokens, 1), lambda j: (0, 0)),
            pl.BlockSpec((width, tile), lambda j: (0, j)),
        ],
        out_specs=pl.BlockSpec((tokens, width), lambda j: (0, 0)),
        compiler_params=pltpu.CompilerParams(vmem_limit_bytes=48 * MIB),
    )(ids, table)


def spread_kernel(ids_ref, turned_ref, grad_ref, out_ref):
    step = pl.program_id(0)
    tile = grad_ref.shape[1]
    count, _, length = turned_ref.shape

    def one(k, total):
        rows = pl.ds(pl.multiple_of(k * length, length), length)
        lane = lax.broadcasted_iota(jnp.int32, (length, tile), 1)
        hit = jnp.where(lane == ids_ref[rows, :] - step * tile, 1.0, 0.0).astype(B16)
        return total + jnp.dot(turned_ref[k], hit, preferred_element_type=F32)

    out_ref[...] = lax.fori_loop(0, count, one, grad_ref[...]).astype(B16)


def spread_rows(ids, turned, grad):
    tokens = ids.shape[0]
    width, size = grad.shape
    tile = tile_of(size)
    return pl.pallas_call(
        spread_kernel,
        grid=(size // tile,),
        out_shape=jax.ShapeDtypeStruct((width, size), B16),
        in_specs=[
            pl.BlockSpec((tokens, 1), lambda j: (0, 0)),
            pl.BlockSpec(turned.shape, lambda j: (0, 0, 0)),
            pl.BlockSpec((width, tile), lambda j: (0, j)),
        ],
        out_specs=pl.BlockSpec((width, tile), lambda j: (0, j)),
        compiler_params=pltpu.CompilerParams(vmem_limit_bytes=48 * MIB),
    )(ids, turned, grad)


def norm_rows(values, gain, shift):
    center = values - jnp.mean(values, -1, keepdims=True)
    scaler = lax.rsqrt(jnp.mean(center * center, -1, keepdims=True) + NORM_EPS)
    normed = center * scaler
    return (normed * gain + shift, normed, scaler)


def norm_back(grad, normed, scaler, gain):
    scaled = grad * gain
    inward = scaler * (
        scaled
        - jnp.mean(scaled, -1, keepdims=True)
        - normed * jnp.mean(scaled * normed, -1, keepdims=True)
    )
    return (inward, jnp.sum(grad * normed, 0), jnp.sum(grad, 0))


def gelu_tanh(values):
    return 0.5 * values * (1.0 + jnp.tanh(GELU_C * (values + 0.044715 * values * values * values)))


def gelu_slope(values):
    tangent = jnp.tanh(GELU_C * (values + 0.044715 * values * values * values))
    return 0.5 * (1.0 + tangent) + 0.5 * values * (1.0 - tangent * tangent) * GELU_C * (
        1.0 + 3.0 * 0.044715 * values * values
    )


def positions(segment):
    codes = jnp.arange(SEGS, dtype=jnp.int32)
    starts = jnp.sum((segment[None, :] < codes[:, None]).astype(jnp.int32), 1)
    member = (segment[:, None] == codes[None, :]).astype(jnp.int32)
    return jnp.arange(segment.shape[0], dtype=jnp.int32) - jnp.sum(member * starts[None, :], 1)


def split_heads(packed):
    width = packed.shape[1] // 3
    return [packed[:, i * width : (i + 1) * width].reshape(packed.shape[0], -1, 64) for i in range(3)]


def masked_scores(queries, keys, segment):
    scores = jnp.einsum("qhd,khd->hqk", queries, keys, preferred_element_type=F32) * 0.125
    return jnp.where((segment[:, None] == segment[None, :])[None], scores, -1e30)


def attend(packed, segment):
    queries, keys, values = split_heads(packed)
    scores = masked_scores(queries, keys, segment)
    top = jnp.max(scores, -1, keepdims=True)
    expd = jnp.exp(scores - top)
    total = jnp.sum(expd, -1, keepdims=True)
    probs = (expd / total).astype(B16)
    context = jnp.einsum("hqk,khd->qhd", probs, values, preferred_element_type=F32)
    return context.reshape(packed.shape[0], -1).astype(B16), (top + jnp.log(total))[..., 0]


def attend_back(packed, segment, lse, dcontext):
    queries, keys, values = split_heads(packed)
    length = packed.shape[0]
    grads = dcontext.reshape(queries.shape)
    probs = jnp.exp(masked_scores(queries, keys, segment) - lse[..., None])
    dprobs = jnp.einsum("qhd,khd->hqk", grads, values, preferred_element_type=F32)
    inner = jnp.sum(probs * dprobs, -1, keepdims=True)
    dscore = (probs * (dprobs - inner) * 0.125).astype(B16)
    parts = (
        jnp.einsum("hqk,khd->qhd", dscore, keys, preferred_element_type=F32),
        jnp.einsum("hqk,qhd->khd", dscore, queries, preferred_element_type=F32),
        jnp.einsum("hqk,qhd->khd", probs.astype(B16), grads, preferred_element_type=F32),
    )
    return jnp.concatenate([p.reshape(length, -1) for p in parts], 1)


def layer_forward(hidden, segment, weights, gains):
    qkv_t, out_t, up_t, down_t = weights
    h_zero, normed_a, scaler_a = norm_rows(hidden, gains[0], gains[1])
    zero_b = h_zero.astype(B16)
    packed = jnp.dot(zero_b, qkv_t, preferred_element_type=F32).astype(B16)
    context_b, lse = attend(packed, segment)
    h_one, normed_b, scaler_b = norm_rows(
        h_zero + jnp.dot(context_b, out_t, preferred_element_type=F32), gains[2], gains[3]
    )
    one_b = h_one.astype(B16)
    inner = jnp.dot(one_b, up_t, preferred_element_type=F32)
    active = gelu_tanh(inner).astype(B16)
    h_two, normed_c, scaler_c = norm_rows(
        h_one + jnp.dot(active, down_t, preferred_element_type=F32), gains[4], gains[5]
    )
    kept = (normed_a, scaler_a, zero_b, packed, lse, context_b, normed_b, scaler_b, one_b, inner, active, normed_c, scaler_c)
    return (kept, h_two)


def layer_backward(dtwo, segment, weights, gains, kept):
    qkv_t, out_t, up_t, down_t = weights
    (normed_a, scaler_a, zero_b, packed, lse, context_b, normed_b, scaler_b, one_b, inner, active, normed_c, scaler_c) = kept
    dz_two, gain_c, shift_c = norm_back(dtwo, normed_c, scaler_c, gains[4])
    dbranch = dz_two.astype(B16)
    grad_down = jnp.einsum("nf,nd->fd", active, dbranch, preferred_element_type=F32)
    dinner = (jnp.dot(dbranch, down_t.T, preferred_element_type=F32) * gelu_slope(inner)).astype(B16)
    grad_up = jnp.einsum("nd,nf->df", one_b, dinner, preferred_element_type=F32)
    dh_one = dz_two + jnp.dot(dinner, up_t.T, preferred_element_type=F32)
    dz_one, gain_b, shift_b = norm_back(dh_one, normed_b, scaler_b, gains[2])
    dproj = dz_one.astype(B16)
    grad_out = jnp.einsum("nc,nd->cd", context_b, dproj, preferred_element_type=F32)
    dcontext = jnp.dot(dproj, out_t.T, preferred_element_type=F32).astype(B16)
    dpacked = attend_back(packed, segment, lse, dcontext).astype(B16)
    grad_qkv = jnp.einsum("nd,ne->de", zero_b, dpacked, preferred_element_type=F32)
    dh_zero = dz_one + jnp.dot(dpacked, qkv_t.T, preferred_element_type=F32)
    dhidden, gain_a, shift_a = norm_back(dh_zero, normed_a, scaler_a, gains[0])
    grad_gains = jnp.stack([gain_a, shift_a, gain_b, shift_b, gain_c, shift_c])
    return (dhidden, (grad_qkv, grad_out, grad_up, grad_down), grad_gains)


def adam(weight, first, second, grad, fix_one, fix_two, rate):
    first = BETA_ONE * first + (1.0 - BETA_ONE) * grad
    second = BETA_TWO * second + (1.0 - BETA_TWO) * grad * grad
    update = first / fix_one / (jnp.sqrt(second / fix_two) + ADAM_EPS)
    return (first, second, weight - rate * (update + WEIGHT_DECAY * weight))


def on_device(
    D, V,
    token_ids, segment_ids, labels, loss_mask, teacher_group, teacher_inputs, teacher_table,
    teacher_qkv, teacher_out, teacher_up, teacher_down, teacher_gains, step_count,
    embed_w, embed_m, embed_v, pos_w, pos_m, pos_v, qkv_w, qkv_m, qkv_v,
    out_w, out_m, out_v, up_w, up_m, up_v, down_w, down_m, down_v, gains_w, gains_m, gains_v,
):
    length = token_ids.shape[1]
    slice_len, columns = embed_w.shape
    width = gains_w.shape[1]
    d, v = lax.axis_index("dp"), lax.axis_index("vocab")
    segment = segment_ids[0]

    turned_table = embed_w.astype(B16).T.reshape(2, columns // 2, slice_len)
    attention = jnp.concatenate([qkv_w, out_w], 1).astype(B16)[None]
    integers = jnp.concatenate(
        [token_ids, labels, loss_mask, jnp.broadcast_to(teacher_group[:, None], (1, length)),
         jnp.zeros((4, length), jnp.int32)], 0
    )[None]
    table, attention, up_t, down_t, pos_t, integers = ring_gather(
        D, V,
        [turned_table, attention, up_w.astype(B16)[None], down_w.astype(B16)[None], pos_w.astype(B16)[None], integers],
        ((0, 0, False, "dp", 0), (0, 1, False, "dp", 1), (5, 0, True, 2, 1), (1, 0, True, 0, 0), (2, 0, True, 1, 1),
         (3, 0, True, 2, 0), (4, 0, True, 1, 0)),
        1,
    )
    table = table.reshape(width, slice_len)
    attention = attention.reshape(width, -1)
    qkv_t, out_t = attention[:, : 3 * width], attention[:, 3 * width :]
    up_t, down_t, pos_t = up_t.reshape(width, -1), down_t.reshape(-1, width), pos_t.reshape(-1, width)
    weights = (qkv_t, out_t, up_t, down_t)
    integers = integers.reshape(D, V, 8, length)
    counted = jnp.maximum(jnp.sum(integers[:, :, 2].astype(F32)), 1.0)
    group_ints = lax.dynamic_index_in_dim(integers, d, 0, False)
    offset = v * slice_len
    ids_here = (group_ints[:, 0].reshape(-1, 1) - offset)
    labels_here = (group_ints[:, 1].reshape(-1, 1) - offset)
    counts = group_ints[:, 2].reshape(-1).astype(F32)
    groups = group_ints[:, 3, 0]

    picked = pick_rows(ids_here, table).astype(B16).reshape(V, length, width)
    embedded = vocab_scatter(V, picked, 2)
    places = positions(segment)
    onehot = (places[:, None] == jnp.arange(pos_t.shape[0], dtype=jnp.int32)[None, :]).astype(B16)
    hidden = embedded + jnp.dot(onehot, pos_t, preferred_element_type=F32)
    kept, h_two = layer_forward(hidden, segment, weights, gains_w)
    two_b = h_two.astype(B16)

    (hidden_all,) = vocab_gather(V, [two_b], 3)
    hidden_all = hidden_all.reshape(V * length, width)
    turned = hidden_all.T
    stats = lax.all_gather(student_stats(hidden_all, table), "vocab")
    top = jnp.max(stats[:, 0], 0)
    student_lse = top + jnp.log(jnp.sum(stats[:, 1] * jnp.exp(stats[:, 0] - top), 0))
    weight = counts / counted
    dh_student, grad_head, pick_lanes = student_grad(
        hidden_all, turned, table, student_lse[:, None], weight[:, None], labels_here
    )

    first = jnp.concatenate([teacher_qkv, teacher_out, teacher_up], 2)
    first, second = ring_gather(
        D, V, [first, teacher_down], tuple((q, r, True, r, q) for r in range(3) for q in range(2)), 4
    )
    mine = teacher_group[0]
    tw = teacher_qkv.shape[2] // 3
    first = lax.dynamic_index_in_dim(first, mine, 0, False).reshape(tw, -1)
    second = lax.dynamic_index_in_dim(second, mine, 0, False).reshape(-1, tw)
    chosen = (first[:, : 3 * tw], first[:, 3 * tw : 4 * tw], first[:, 4 * tw :], second)
    gains_row = lax.dynamic_index_in_dim(teacher_gains, mine, 0, False)
    _, teacher_top = layer_forward(teacher_inputs[0].astype(F32), segment, chosen, gains_row)
    (teacher_hidden,) = vocab_gather(V, [teacher_top.astype(B16)], 5)

    teacher, stats = teacher_stats(groups, teacher_hidden, teacher_table)
    stats = lax.all_gather(stats, "vocab")
    top = jnp.max(stats[:, 0], 0)
    scale = jnp.exp(stats[:, 0] - top)
    tsum = jnp.sum(stats[:, 1] * scale, 0)
    tcross = jnp.sum(stats[:, 2] * scale, 0) / tsum
    teacher_lse = top + jnp.log(tsum)
    dh_teacher, grad_head = teacher_grad(
        teacher, turned, table, teacher_lse[:, None], weight[:, None], grad_head
    )
    everywhere = jnp.sum(hidden_all.astype(F32) * dh_teacher) - jnp.sum(weight[:, None] * pick_lanes)
    once = jnp.sum(weight * (MIX_ALPHA * (tcross - teacher_lse + student_lse) + student_lse))
    loss_part = everywhere + jnp.where(v == 0, once, 0.0)

    dtwo = vocab_scatter(V, (dh_student + dh_teacher).astype(B16).reshape(V, length, width), 6)
    dhidden, dense_grads, grad_gains = layer_backward(dtwo, segment, weights, gains_w, kept)
    dhidden_b = dhidden.astype(B16)
    grad_pos = lax.dot_general(onehot, dhidden_b, (((0,), (0,)), ((), ())), preferred_element_type=F32)
    (turned_grads,) = vocab_gather(V, [dhidden_b.T], 7)
    grad_embed = spread_rows(ids_here, turned_grads, grad_head)

    grad_qkv, grad_out, grad_up, grad_down = dense_grads
    owners = lambda g: g.astype(B16).reshape(D * V // 2, 2, -1, g.shape[1])
    grad_embed = grad_embed.reshape(D, 2, columns // 2, slice_len)
    sums = ring_scatter(
        D, V,
        [grad_embed[:, 0], grad_embed[:, 1], owners(jnp.concatenate([grad_qkv, grad_out], 1)), owners(grad_up),
         owners(grad_down), owners(grad_pos)],
        (("dp", 0), ("dp", 1), (0, 0), (1, 1), (2, 0), (1, 0)),
        8,
    )
    grad_embed = jnp.concatenate(sums[:2], 0)
    owned = (sums[5], sums[2][:, : 3 * width], sums[2][:, 3 * width :], sums[3], sums[4])
    squares = jnp.sum(grad_embed * grad_embed)
    for grad in (sums[2], sums[3], sums[4], sums[5]):
        squares = squares + jnp.sum(grad * grad)
    lane = lax.broadcasted_iota(jnp.int32, (2, width), 1)
    scalars = jnp.where(lane == 0, squares, jnp.where(lane == 1, loss_part, 0.0))
    totals = total_all(D, V, jnp.concatenate([grad_gains, scalars], 0), 9)
    gains_grad, squares, loss = totals[:6], totals[6, 0], totals[6, 1]

    grad_norm = jnp.sqrt(squares + jnp.sum(gains_grad * gains_grad))
    factor = CLIP_NORM / jnp.maximum(grad_norm, CLIP_NORM)
    count_f = step_count.astype(F32)
    fix_one = 1.0 - jnp.power(BETA_ONE, count_f)
    fix_two = 1.0 - jnp.power(BETA_TWO, count_f)

    def update(weight, first, second, grad, rate):
        return adam(weight, first, second, grad * factor, fix_one, fix_two, rate)

    out = [loss, grad_norm]
    out += update(embed_w, embed_m, embed_v, grad_embed.T, LEARN_RATE)
    out += update(pos_w, pos_m, pos_v, owned[0], LEARN_RATE)
    out += update(qkv_w, qkv_m, qkv_v, owned[1], LEARN_RATE)
    out += update(out_w, out_m, out_v, owned[2], LEARN_RATE)
    out += update(up_w, up_m, up_v, owned[3], LEARN_RATE)
    out += update(down_w, down_m, down_v, owned[4], LEARN_RATE)
    out += update(gains_w, gains_m, gains_v, gains_grad, GAIN_RATE)
    return tuple(out)


def solution(mesh):
    rows, whole = P(("dp", "vocab"), None), P()
    split = P(None, ("dp", "vocab"), None)
    embed = P("vocab", "dp")
    return jax.shard_map(
        functools.partial(on_device, mesh.shape["dp"], mesh.shape["vocab"]),
        mesh=mesh,
        in_specs=(rows, rows, rows, rows, P(("dp", "vocab")), P(("dp", "vocab"), None, None), P(None, None, "vocab"),
                  split, split, split, split, whole, whole)
        + (embed,) * 3 + (rows,) * 15 + (whole,) * 3,
        out_specs=(whole, whole) + (embed,) * 3 + (rows,) * 15 + (whole,) * 3,
        check_vma=False,
    )
```

```python
import functools

import jax
import jax.numpy as jnp
from jax import lax
from jax.experimental import pallas as pl
from jax.experimental.pallas import tpu as pltpu
from jax.sharding import PartitionSpec as P

SEGS = 8
NORM_EPS = 1e-05
MIX_ALPHA = 0.5
CLIP_NORM = 0.005
LEARN_RATE = 0.03
GAIN_RATE = 0.4
BETA_ONE = 0.9
BETA_TWO = 0.999
ADAM_EPS = 1e-08
WEIGHT_DECAY = 0.01
GELU_C = 0.7978845608028654
MESH = pl.DeviceIdType.MESH
F32 = jnp.float32
B16 = jnp.bfloat16
ANYWHERE = pl.BlockSpec(memory_space=pl.ANY)
IN_VMEM = pl.BlockSpec(memory_space=pltpu.VMEM)
MIB = 1 << 20

CYCLES = (
    (0, 1, 3, 2, 6, 7, 5, 9, 11, 10, 14, 15, 13, 12, 8, 4),
    (0, 1, 5, 4, 6, 10, 8, 9, 13, 12, 14, 15, 11, 7, 3, 2),
    (0, 2, 6, 7, 3, 1, 5, 9, 13, 15, 11, 10, 14, 12, 8, 4),
)


def chip_cycle(count, which):
    return CYCLES[which] if count == 16 else tuple(range(count))


def dp_cycle(count):
    return tuple(range(0, count, 2)) + tuple(range(count - 1 - count % 2, 0, -2))


def lookup(table, index):
    out = jnp.int32(table[0])
    for k in range(1, len(table)):
        out = jnp.where(index == k, table[k], out)
    return out


class Ring:
    def __init__(self, D, V, which):
        self.D, self.V = D, V
        d, v = lax.axis_index("dp"), lax.axis_index("vocab")
        self.core, self.v = lax.rem(v, 2), v
        self.over_dp = which == "dp"
        self.n = D if self.over_dp else D * V // 2
        self.table = dp_cycle(D) if self.over_dp else chip_cycle(self.n, which)
        self.me = d if self.over_dp else d * (V // 2) + v // 2
        inverse = tuple(self.table.index(k) for k in range(self.n))
        self.pos = lookup(inverse, self.me)

    def at(self, ahead):
        return lookup(self.table, lax.rem(self.pos + ahead + self.n, self.n))

    def device(self, place):
        if self.over_dp:
            return (place, self.v)
        half = self.V // 2
        return (place // half, lax.rem(place, half) * 2 + self.core)

    def hops(self, parity):
        more, less = self.n // 2, self.n - 1 - self.n // 2
        return (more, less) if parity == 0 else (less, more)


def sibling():
    v = lax.axis_index("vocab")
    return (lax.axis_index("dp"), v + 1 - 2 * lax.rem(v, 2))


def greet(devices):
    barrier = pltpu.get_barrier_semaphore()
    for device in devices:
        pl.semaphore_signal(barrier, inc=1, device_id=device, device_id_type=MESH)
    pl.semaphore_wait(barrier, len(devices))


def on_condition(condition, body):
    if condition is True:
        body()
    elif condition is not False:
        pl.when(condition)(body)


class Gather:
    def __init__(self, D, V, spec, ins, outs, sems):
        self.spec, self.ins, self.outs = spec, ins, outs
        self.ssem, self.rsem, self.xssem, self.xrsem, self.lsem = sems
        rings = {w: Ring(D, V, w) for w in dict.fromkeys(p[3] for p in spec)}
        self.core = lax.rem(lax.axis_index("vocab"), 2)
        self.sib = sibling()
        self.nexts = {w: (r.at(1), r.at(-1)) for w, r in rings.items()}
        self.neighbours = [r.device(place) for w, r in rings.items() for place in self.nexts[w]]
        if any(p[3] != "dp" for p in spec):
            self.neighbours.append(self.sib)
        self.streams = []
        for number, piece in enumerate(spec):
            ring = rings[piece[3]]
            for turn, hops in zip((0, 1), ring.hops(piece[4])):
                self.streams.append((piece, ring, turn, hops, number))
        self.longest = max(s[3] for s in self.streams)

    def dst(self, piece, slot):
        which, k, lead, _, _ = piece
        return self.outs[which].at[k, slot] if lead else self.outs[which].at[slot, k]

    def slot_of(self, ring, place):
        return place if ring.over_dp else place * 2 + self.core

    def origin(self, stream, s):
        _, ring, turn, _, _ = stream
        return self.slot_of(ring, ring.at(-s) if turn == 0 else ring.at(s))

    def remote(self, i, s, src, slot):
        piece, ring, turn, _, _ = self.streams[i]
        return pltpu.make_async_remote_copy(
            src_ref=src,
            dst_ref=self.dst(piece, slot),
            send_sem=self.ssem.at[s, i],
            recv_sem=self.rsem.at[s, i],
            device_id=ring.device(self.nexts[piece[3]][turn]),
            device_id_type=MESH,
        )

    def across(self, i, s, src, slot):
        return pltpu.make_async_remote_copy(
            src_ref=src,
            dst_ref=self.dst(self.streams[i][0], slot),
            send_sem=self.xssem.at[s, i],
            recv_sem=self.xrsem.at[s, i],
            device_id=self.sib,
            device_id_type=MESH,
        )

    def own(self, i):
        piece, ring, _, _, _ = self.streams[i]
        return self.ins[piece[0]].at[piece[1]], self.slot_of(ring, ring.me)

    def begin(self):
        for i in range(len(self.streams)):
            self.remote(i, 0, *self.own(i)).start()
        for i, stream in enumerate(self.streams):
            if stream[2] == 0:
                src, slot = self.own(i)
                pltpu.make_async_copy(src, self.dst(stream[0], slot), self.lsem.at[stream[4]]).start()
                if not stream[1].over_dp:
                    self.across(i, 0, src, slot).start()

    def within(self, s, hops):
        return True if hops == self.longest else s <= hops

    def serve(self, s):
        for i, stream in enumerate(self.streams):

            def take(i=i, stream=stream):
                slot = self.origin(stream, s)
                block = self.dst(stream[0], slot)
                self.remote(i, s - 1, block, slot).wait_recv()
                pl.when(s < stream[3])(lambda: self.remote(i, s, block, slot).start())
                if not stream[1].over_dp:
                    self.across(i, s, block, slot).start()

            on_condition(self.within(s, stream[3]), take)

    def serve_range(self, low, high):
        def body(s, carry):
            self.serve(s)
            return carry

        lax.fori_loop(low, high, body, 0)

    def finish(self):
        def last(s, carry):
            for i, stream in enumerate(self.streams):

                def end(i=i, stream=stream):
                    slot = self.origin(stream, s)
                    block = self.dst(stream[0], slot)
                    pl.when(s < stream[3])(lambda: self.remote(i, s, block, slot).wait_send())
                    if not stream[1].over_dp:

                        def crossed():
                            self.across(i, s, block, slot).wait_send()
                            theirs = slot + 1 - 2 * self.core
                            self.across(i, s, block, theirs).wait_recv()

                        on_condition(True if stream[2] == 0 else s > 0, crossed)

                on_condition(self.within(s, stream[3]), end)
            return carry

        lax.fori_loop(0, self.longest + 1, last, 0)
        for i, stream in enumerate(self.streams):
            if stream[2] == 0:
                src, slot = self.own(i)
                pltpu.make_async_copy(src, self.dst(stream[0], slot), self.lsem.at[stream[4]]).wait()


def gather_kernel(D, V, spec, count, *refs):
    gather = Gather(D, V, spec, refs[:count], refs[count : 2 * count], refs[2 * count :])
    greet(gather.neighbours)
    gather.begin()
    gather.serve_range(1, gather.longest + 1)
    gather.finish()


def gather_plan(D, V, arrays, spec):
    shapes = []
    for which, array in enumerate(arrays):
        piece = next(p for p in spec if p[0] == which)
        places = D if piece[3] == "dp" else D * V
        lead = array.shape[:1]
        shape = lead + (places,) if piece[2] else (places,) + lead
        shapes.append(jax.ShapeDtypeStruct(shape + array.shape[1:], array.dtype))
    longest = max((D if p[3] == "dp" else D * V // 2) // 2 for p in spec) + 1
    sems = pltpu.SemaphoreType.DMA((longest, 2 * len(spec)))
    return shapes, [sems] * 4 + [pltpu.SemaphoreType.DMA((len(spec),))]


def ring_gather(D, V, arrays, spec, ident):
    shapes, sems = gather_plan(D, V, arrays, spec)
    return pl.pallas_call(
        functools.partial(gather_kernel, D, V, spec, len(arrays)),
        out_shape=shapes,
        in_specs=[ANYWHERE] * len(arrays),
        out_specs=[ANYWHERE] * len(arrays),
        scratch_shapes=sems,
        compiler_params=pltpu.CompilerParams(collective_id=ident, has_side_effects=True),
    )(*arrays)


def scatter_kernel(D, V, spec, *refs):
    count = len(spec)
    ins, outs = refs[:count], refs[count : 2 * count]
    scratch = list(refs[2 * count :])
    ssem, rsem, xssem, xrsem = scratch[-4:]
    rings = {w: Ring(D, V, w) for w in dict.fromkeys(p[0] for p in spec)}
    core = lax.rem(lax.axis_index("vocab"), 2)
    sib = sibling()
    nexts = {w: (r.at(1), r.at(-1)) for w, r in rings.items()}
    crossing = any(w != "dp" for w in rings)
    greet(
        [r.device(place) for w, r in rings.items() for place in nexts[w]]
        + ([sib] if crossing else [])
    )
    sums, slots = [], []
    for number, (which, parity) in enumerate(spec):
        if which == "dp":
            sums.append(ins[number])
        else:
            sums.append(scratch.pop(0))
        slots.append((scratch.pop(0), scratch.pop(0)))
    streams = []
    for number, (which, parity) in enumerate(spec):
        for turn, hops in zip((0, 1), rings[which].hops(parity)):
            streams.append((number, rings[which], turn, hops, which))
    streams = [s for s in streams if s[3] > 0]

    def place(stream, ahead):
        return stream[1].at(ahead) if stream[2] == 0 else stream[1].at(-ahead)

    def remote(i, s, src):
        number, ring, turn, hops, which = streams[i]
        return pltpu.make_async_remote_copy(
            src_ref=src,
            dst_ref=slots[number][turn].at[s],
            send_sem=ssem.at[s, i],
            recv_sem=rsem.at[s, i],
            device_id=ring.device(nexts[which][turn]),
            device_id_type=MESH,
        )

    def across(number):
        return pltpu.make_async_remote_copy(
            src_ref=ins[number].at[:, 1 - core],
            dst_ref=sums[number],
            send_sem=xssem.at[number],
            recv_sem=xrsem.at[number],
            device_id=sib,
            device_id_type=MESH,
        )

    def first(i):
        number, _, _, hops, _ = streams[i]
        return remote(i, 0, sums[number].at[place(streams[i], hops)])

    for number, (which, _) in enumerate(spec):
        if which != "dp":
            across(number).start()
    for i, stream in enumerate(streams):
        if stream[4] == "dp":
            first(i).start()
    for number, (which, _) in enumerate(spec):
        if which != "dp":
            across(number).wait_recv()

            def add(k, carry, number=number):
                total = sums[number][k].astype(F32) + ins[number][k, core].astype(F32)
                sums[number][k] = total.astype(B16)
                return carry

            lax.fori_loop(0, rings[which].n, add, 0)
            for i, stream in enumerate(streams):
                if stream[0] == number:
                    first(i).start()
    longest = max(s[3] for s in streams)
    stride = {w: max(1, longest // max(max(r.hops(0)), 1)) for w, r in rings.items()}

    def body(s, carry):
        for i, stream in enumerate(streams):
            number, ring, turn, hops, which = stream
            by = stride[which]

            def take(i=i, stream=stream, number=number, turn=turn, hops=hops, by=by):
                step = s // by
                block = slots[number][turn].at[step - 1]
                remote(i, step - 1, block).wait_recv()

                def onward():
                    mine = sums[number].at[place(stream, hops - step)]
                    block[...] = (block[...].astype(F32) + mine[...].astype(F32)).astype(B16)
                    remote(i, step, block).start()

                pl.when(step < hops)(onward)

            condition = True
            if by > 1 or hops * by < longest:
                condition = (lax.rem(s, by) == 0) & (s // by <= hops)
            on_condition(condition, take)
        return carry

    lax.fori_loop(1, longest + 1, body, 0)
    for number, (which, parity) in enumerate(spec):
        total = sums[number][rings[which].me].astype(F32)
        for turn, hops in zip((0, 1), rings[which].hops(parity)):
            if hops > 0:
                total = total + slots[number][turn][hops - 1].astype(F32)
        outs[number][...] = total
    for i, stream in enumerate(streams):
        number, ring, turn, hops, which = stream
        first(i).wait_send()

        def sent(s, carry, i=i, number=number, turn=turn):
            remote(i, s, slots[number][turn].at[s - 1]).wait_send()
            return carry

        lax.fori_loop(1, hops, sent, 0)
    for number, (which, _) in enumerate(spec):
        if which != "dp":
            across(number).wait_send()


def ring_scatter(D, V, arrays, spec, ident):
    scratch, shapes = [], []
    for array, (which, parity) in zip(arrays, spec):
        block = array.shape[-2:]
        n = D if which == "dp" else D * V // 2
        if which != "dp":
            scratch.append(pltpu.VMEM((n,) + block, B16))
        more, less = n // 2, n - 1 - n // 2
        scratch += [pltpu.VMEM((max(k, 1),) + block, B16) for k in ((more, less), (less, more))[parity]]
        shapes.append(jax.ShapeDtypeStruct(block, F32))
    longest = max((D if w == "dp" else D * V // 2) // 2 for w, _ in spec)
    sems = pltpu.SemaphoreType.DMA((longest, 2 * len(spec)))
    single = pltpu.SemaphoreType.DMA((len(spec),))
    return pl.pallas_call(
        functools.partial(scatter_kernel, D, V, spec),
        out_shape=shapes,
        in_specs=[IN_VMEM] * len(arrays),
        out_specs=[IN_VMEM] * len(arrays),
        scratch_shapes=scratch + [sems, sems, single, single],
        compiler_params=pltpu.CompilerParams(
            collective_id=ident, has_side_effects=True, vmem_limit_bytes=56 * MIB
        ),
    )(*arrays)


def vocab_gather_kernel(V, count, *refs):
    ins, outs = refs[:count], refs[count : 2 * count]
    ssem, rsem, xssem, xrsem, lsem = refs[2 * count :]
    d, v = lax.axis_index("dp"), lax.axis_index("vocab")
    half = V // 2
    core, chip = lax.rem(v, 2), v // 2
    sib = sibling()

    def other(k):
        return lax.rem(chip + k + half, half) * 2 + core

    greet([(d, other(k)) for k in range(1, half)] + [sib])

    def send(q, k):
        return pltpu.make_async_remote_copy(
            src_ref=ins[q],
            dst_ref=outs[q].at[v],
            send_sem=ssem.at[q, k],
            recv_sem=rsem.at[q, k],
            device_id=(d, other(k)),
            device_id_type=MESH,
        )

    def across(q, k, src, slot):
        return pltpu.make_async_remote_copy(
            src_ref=src,
            dst_ref=outs[q].at[slot],
            send_sem=xssem.at[q, k],
            recv_sem=xrsem.at[q, k],
            device_id=sib,
            device_id_type=MESH,
        )

    for q in range(count):
        for k in range(1, half):
            send(q, k).start()
    for q in range(count):
        across(q, 0, ins[q], v).start()
        pltpu.make_async_copy(ins[q], outs[q].at[v], lsem.at[q]).start()
    for q in range(count):
        for k in range(1, half):
            slot = other(-k)
            send(q, k).wait_recv()
            across(q, k, outs[q].at[slot], slot).start()
    for q in range(count):
        pltpu.make_async_copy(ins[q], outs[q].at[v], lsem.at[q]).wait()
        for k in range(half):
            slot = other(-k)
            if k:
                send(q, k).wait_send()
            across(q, k, outs[q].at[slot], slot).wait_send()
            across(q, k, outs[q].at[slot], slot + 1 - 2 * core).wait_recv()


def vocab_gather(V, arrays, ident):
    count = len(arrays)
    sems = pltpu.SemaphoreType.DMA((count, V // 2))
    return pl.pallas_call(
        functools.partial(vocab_gather_kernel, V, count),
        out_shape=[jax.ShapeDtypeStruct((V,) + a.shape, a.dtype) for a in arrays],
        in_specs=[ANYWHERE] * count,
        out_specs=[ANYWHERE] * count,
        scratch_shapes=[sems] * 4 + [pltpu.SemaphoreType.DMA((count,))],
        compiler_params=pltpu.CompilerParams(collective_id=ident, has_side_effects=True),
    )(*arrays)


def vocab_scatter_kernel(V, in_ref, out_ref, sums, taken, ssem, rsem, xsem):
    d, v = lax.axis_index("dp"), lax.axis_index("vocab")
    half = V // 2
    core, chip = lax.rem(v, 2), v // 2
    sib = sibling()

    def other(k):
        return lax.rem(chip + k + half, half)

    greet([(d, other(k) * 2 + core) for k in range(1, half)] + [sib])
    across = pltpu.make_async_remote_copy(
        src_ref=in_ref.at[:, 1 - core],
        dst_ref=sums,
        send_sem=xsem.at[0],
        recv_sem=xsem.at[1],
        device_id=sib,
        device_id_type=MESH,
    )
    across.start()
    across.wait_recv()

    def send(k):
        return pltpu.make_async_remote_copy(
            src_ref=sums.at[other(k)],
            dst_ref=taken.at[k - 1],
            send_sem=ssem.at[k - 1],
            recv_sem=rsem.at[k - 1],
            device_id=(d, other(k) * 2 + core),
            device_id_type=MESH,
        )

    for k in [*range(1, half), 0]:
        to = other(k)
        total = sums[to].astype(F32) + in_ref[to, core].astype(F32)
        sums[to] = total.astype(B16)
        if k:
            send(k).start()
    total = sums[chip].astype(F32)
    for k in range(1, half):
        send(k).wait_recv()
        total = total + taken[k - 1].astype(F32)
    out_ref[...] = total
    for k in range(1, half):
        send(k).wait_send()
    across.wait_send()


def vocab_scatter(V, array, ident):
    half = V // 2
    block = array.shape[1:]
    sems = pltpu.SemaphoreType.DMA((max(half - 1, 1),))
    return pl.pallas_call(
        functools.partial(vocab_scatter_kernel, V),
        out_shape=jax.ShapeDtypeStruct(block, F32),
        in_specs=[IN_VMEM],
        out_specs=IN_VMEM,
        scratch_shapes=[
            pltpu.VMEM((half,) + block, B16),
            pltpu.VMEM((max(half - 1, 1),) + block, B16),
            sems,
            sems,
            pltpu.SemaphoreType.DMA((2,)),
        ],
        compiler_params=pltpu.CompilerParams(
            collective_id=ident, has_side_effects=True, vmem_limit_bytes=40 * MIB
        ),
    )(array.reshape((half, 2) + block))


def total_kernel(D, V, in_ref, out_ref, first, second, ssem, rsem):
    d, v = lax.axis_index("dp"), lax.axis_index("vocab")
    peers = [(d, lax.rem(v + k, V)) for k in range(1, V)]
    peers += [(lax.rem(d + k, D), v) for k in range(1, D)]
    greet(peers)

    def send(k):
        over = first if k < V - 1 else second
        mine = v if k < V - 1 else d
        return pltpu.make_async_remote_copy(
            src_ref=over.at[mine],
            dst_ref=over.at[mine],
            send_sem=ssem.at[k],
            recv_sem=rsem.at[k],
            device_id=peers[k],
            device_id_type=MESH,
        )

    def stage(slots, mine, value, low, high):
        slots[mine] = value
        for k in range(low, high):
            send(k).start()
        for k in range(low, high):
            send(k).wait_recv()
        total = slots[0]
        for k in range(1, slots.shape[0]):
            total = total + slots[k]
        return total

    total = stage(first, v, in_ref[...], 0, V - 1)
    out_ref[...] = stage(second, d, total, V - 1, V + D - 2)
    for k in range(V + D - 2):
        send(k).wait_send()


def total_all(D, V, array, ident):
    sems = pltpu.SemaphoreType.DMA((V + D - 2,))
    return pl.pallas_call(
        functools.partial(total_kernel, D, V),
        out_shape=jax.ShapeDtypeStruct(array.shape, F32),
        in_specs=[IN_VMEM],
        out_specs=IN_VMEM,
        scratch_shapes=[pltpu.VMEM((V,) + array.shape, F32), pltpu.VMEM((D,) + array.shape, F32), sems, sems],
        compiler_params=pltpu.CompilerParams(collective_id=ident, has_side_effects=True),
    )(array)


def tile_of(size, tokens=1):
    return next(t for t in (1280, 768, 640, 512, 256, 128) if size % t == 0 and (t * tokens <= 1280 * 2048 or t == 128))


def lane_fold(values, combine):
    out = values[:, :128]
    for k in range(1, values.shape[1] // 128):
        out = combine(out, values[:, k * 128 : (k + 1) * 128])
    return out


def running(values, top_ref, sum_ref, rows):
    old = top_ref[rows, :]
    top = jnp.maximum(old, lane_fold(values, jnp.maximum))
    fade = jnp.exp(old - top)
    expd = jnp.concatenate(
        [jnp.exp(values[:, k * 128 : (k + 1) * 128] - top) for k in range(values.shape[1] // 128)], 1
    )
    top_ref[rows, :] = top
    sum_ref[rows, :] = sum_ref[rows, :] * fade + lane_fold(expd, jnp.add)
    return expd, fade


def pack_rows(columns):
    lane = lax.broadcasted_iota(jnp.int32, (columns[0].shape[0], 128), 1)
    packed = jnp.zeros(lane.shape, F32)
    for k, column in enumerate(columns):
        packed = jnp.where(lane == k, column, packed)
    return packed.T[:8]


def study_kernel(D, V, spec, *refs):
    first_ref, second_ref, own_ref, table_ref, given_ref = refs[:5]
    first_out, second_out, hidden_ref, turned_out, dh_ref, grad_ref, rows_out = refs[5:12]
    top_ref, sum_ref, dl_ref, slots, hs, hr, xs, xr, ps, pr = refs[12:22]
    gather = Gather(D, V, spec, (first_ref, second_ref), (first_out, second_out), refs[22:])
    d, v = lax.axis_index("dp"), lax.axis_index("vocab")
    half = V // 2
    core, chip = lax.rem(v, 2), v // 2
    length, width = own_ref.shape
    tokens, size = V * length, table_ref.shape[1]
    tile, block = tile_of(size, tokens), min(256, length)
    tiles, blocks = size // tile, tokens // block
    peers = [(d, lax.rem(v + k, V)) for k in range(1, V)]
    greet(gather.neighbours + peers)

    def other(k):
        return lax.rem(chip + k + half, half) * 2 + core

    def place(slot):
        return hidden_ref.at[pl.ds(pl.multiple_of(slot * length, length), length)]

    def send(k):
        return pltpu.make_async_remote_copy(
            src_ref=own_ref, dst_ref=place(v), send_sem=hs.at[k], recv_sem=hr.at[k],
            device_id=(d, other(k)), device_id_type=MESH,
        )

    def across(k, src, slot):
        return pltpu.make_async_remote_copy(
            src_ref=src, dst_ref=place(slot), send_sem=xs.at[k], recv_sem=xr.at[k],
            device_id=sibling(), device_id_type=MESH,
        )

    for k in range(1, half):
        send(k).start()
    across(0, own_ref, v).start()
    gather.begin()
    place(v)[...] = own_ref[...]
    top_ref[...] = jnp.full(top_ref.shape, -jnp.inf, F32)
    sum_ref[...] = jnp.zeros(sum_ref.shape, F32)
    dh_ref[...] = jnp.zeros(dh_ref.shape, F32)
    for k in range(1, half):
        slot = other(-k)
        send(k).wait_recv()
        across(k, place(slot), slot).start()
    for k in range(half):
        across(k, place(other(-k)), other(-k) + 1 - 2 * core).wait_recv()

    def columns(t):
        return pl.ds(pl.multiple_of(t * tile, tile), tile)

    early = max(1, gather.longest // 4)
    late = gather.longest - early

    def pass_one(t, carry):
        for k in range(blocks):
            rows = slice(k * block, (k + 1) * block)
            logits = jnp.dot(hidden_ref[rows, :], table_ref[:, columns(t)], preferred_element_type=F32)
            running(logits, top_ref, sum_ref, rows)
        gather.serve_range(1 + t * early // tiles, 1 + (t + 1) * early // tiles)
        return carry

    lax.fori_loop(0, tiles, pass_one, 0)
    top = jnp.max(top_ref[...], 1, keepdims=True)
    total = jnp.sum(sum_ref[...] * jnp.exp(top_ref[...] - top), 1, keepdims=True)
    slots[v] = pack_rows([top, total])

    def tell(k):
        return pltpu.make_async_remote_copy(
            src_ref=slots.at[v], dst_ref=slots.at[v], send_sem=ps.at[k], recv_sem=pr.at[k],
            device_id=peers[k], device_id_type=MESH,
        )

    for k in range(V - 1):
        tell(k).start()
    for q in range(tokens // length):
        rows = slice(q * length, (q + 1) * length)
        turned_out[:, rows] = hidden_ref[rows, :].T
    for k in range(V - 1):
        tell(k).wait_recv()
    top = slots[0, 0:1, :]
    for k in range(1, V):
        top = jnp.maximum(top, slots[k, 0:1, :])
    total = jnp.zeros(top.shape, F32)
    for k in range(V):
        total = total + slots[k, 1:2, :] * jnp.exp(slots[k, 0:1, :] - top)
    lse = top + jnp.log(total)
    rows_out[...] = jnp.broadcast_to(lse, rows_out.shape)
    lse_ref, pick_ref = top_ref, sum_ref
    lse_ref[...] = jnp.broadcast_to(lse, (128, tokens)).T
    pick_ref[...] = jnp.zeros(pick_ref.shape, F32)

    def pass_two(t, carry):
        for k in range(blocks):
            rows = slice(k * block, (k + 1) * block)
            logits = jnp.dot(hidden_ref[rows, :], table_ref[:, columns(t)], preferred_element_type=F32)
            weight = given_ref[rows, 0:1]
            soft = jnp.exp(logits - lse_ref[rows, :1]) * ((1.0 + MIX_ALPHA) * weight)
            lane = lax.broadcasted_iota(jnp.int32, logits.shape, 1)
            hit = lane == given_ref[rows, 1:2].astype(jnp.int32) - t * tile
            dl_ref[rows, :] = jnp.where(hit, soft - weight, soft).astype(B16)
            pick_ref[rows, :] += lane_fold(jnp.where(hit, logits, 0.0), jnp.add)
        for k in range(tokens // length):
            rows = slice(k * length, (k + 1) * length)
            dh_ref[rows, :] += lax.dot_general(
                dl_ref[rows, :], table_ref[:, columns(t)], (((1,), (1,)), ((), ())), preferred_element_type=F32
            )
        grad_ref[:, columns(t)] = jnp.dot(
            turned_out[...], dl_ref[...], preferred_element_type=F32
        ).astype(B16)
        gather.serve_range(1 + early + t * late // tiles, 1 + early + (t + 1) * late // tiles)
        return carry

    lax.fori_loop(0, tiles, pass_two, 0)
    picks = pack_rows([jnp.sum(pick_ref[...], 1, keepdims=True)])
    rows_out[1:2, :] = picks[0:1]
    for k in range(1, half):
        send(k).wait_send()
    for k in range(half):
        across(k, place(other(-k)), other(-k)).wait_send()
    for k in range(V - 1):
        tell(k).wait_send()
    gather.finish()


def study(D, V, first, second, own, table, given, ident):
    spec = tuple((q, r, True, r, q) for r in range(3) for q in range(2))
    shapes, sems = gather_plan(D, V, [first, second], spec)
    length, width = own.shape
    tokens, size = V * length, table.shape[1]
    tile = tile_of(size, tokens)
    halves, singles = pltpu.SemaphoreType.DMA((V // 2,)), pltpu.SemaphoreType.DMA((V,))
    column = pltpu.VMEM((tokens, 128), F32)
    return pl.pallas_call(
        functools.partial(study_kernel, D, V, spec),
        out_shape=shapes
        + [
            jax.ShapeDtypeStruct((tokens, width), B16),
            jax.ShapeDtypeStruct((width, tokens), B16),
            jax.ShapeDtypeStruct((tokens, width), F32),
            jax.ShapeDtypeStruct((width, size), B16),
            jax.ShapeDtypeStruct((8, tokens), F32),
        ],
        in_specs=[ANYWHERE] * 2 + [IN_VMEM] * 3,
        out_specs=[ANYWHERE] * 2 + [IN_VMEM] * 5,
        scratch_shapes=[column] * 2
        + [pltpu.VMEM((tokens, tile), B16), pltpu.VMEM((V, 8, tokens), F32)]
        + [halves] * 4
        + [singles] * 2
        + sems,
        compiler_params=pltpu.CompilerParams(
            collective_id=ident, has_side_effects=True, vmem_limit_bytes=60 * MIB
        ),
    )(first, second, own, table, given)


def teacher_stats_kernel(group_ref, hidden_ref, table_ref, out_ref, stats_ref, top_ref, sum_ref, cross_ref):
    step, row = pl.program_id(0), pl.program_id(1)
    length = hidden_ref.shape[1]
    rows = pl.ds(pl.multiple_of(row * length, length), length)

    @pl.when(step == 0)
    def _():
        top_ref[rows, :] = jnp.full((length, 128), -jnp.inf, F32)
        sum_ref[rows, :] = jnp.zeros((length, 128), F32)
        cross_ref[rows, :] = jnp.zeros((length, 128), F32)

    rounded = jnp.dot(hidden_ref[0], table_ref[0], preferred_element_type=F32).astype(B16)
    out_ref[0] = rounded
    values = rounded.astype(F32)
    expd, fade = running(values, top_ref, sum_ref, rows)
    cross_ref[rows, :] = cross_ref[rows, :] * fade + lane_fold(expd * values, jnp.add)

    @pl.when((step == pl.num_programs(0) - 1) & (row == pl.num_programs(1) - 1))
    def _():
        top = jnp.max(top_ref[...], 1, keepdims=True)
        scale = jnp.exp(top_ref[...] - top)
        total = jnp.sum(sum_ref[...] * scale, 1, keepdims=True)
        cross = jnp.sum(cross_ref[...] * scale, 1, keepdims=True)
        stats_ref[...] = pack_rows([top, total, cross])


def teacher_stats(groups, hidden, tables):
    count, length, width = hidden.shape
    size = tables.shape[2]
    tile = tile_of(size)
    tokens = count * length
    return pl.pallas_call(
        teacher_stats_kernel,
        grid_spec=pltpu.PrefetchScalarGridSpec(
            num_scalar_prefetch=1,
            grid=(size // tile, count),
            in_specs=[
                pl.BlockSpec((1, length, width), lambda j, r, g: (r, 0, 0)),
                pl.BlockSpec((1, width, tile), lambda j, r, g: (g[r], 0, j)),
            ],
            out_specs=[
                pl.BlockSpec((1, length, tile), lambda j, r, g: (r, 0, j)),
                pl.BlockSpec((8, tokens), lambda j, r, g: (0, 0)),
            ],
            scratch_shapes=[pltpu.VMEM((tokens, 128), F32)] * 3,
        ),
        out_shape=[
            jax.ShapeDtypeStruct((count, length, size), B16),
            jax.ShapeDtypeStruct((8, tokens), F32),
        ],
        compiler_params=pltpu.CompilerParams(vmem_limit_bytes=48 * MIB),
    )(groups, hidden, tables)


def teacher_grad_kernel(teacher_ref, turned_ref, table_ref, lse_ref, weight_ref, gradin_ref, dh_ref, grad_ref):
    step = pl.program_id(0)
    count, length = teacher_ref.shape[:2]

    @pl.when(step == 0)
    def _():
        dh_ref[...] = jnp.zeros(dh_ref.shape, F32)

    grad_ref[...] = gradin_ref[...].astype(F32)

    def one(k, carry):
        rows = pl.ds(pl.multiple_of(k * length, length), length)
        target = jnp.exp(teacher_ref[k].astype(F32) - lse_ref[rows, :])
        dlogits = ((-MIX_ALPHA * weight_ref[rows, :]) * target).astype(B16)
        dh_ref[rows, :] += lax.dot_general(
            dlogits, table_ref[...], (((1,), (1,)), ((), ())), preferred_element_type=F32
        )
        grad_ref[...] += jnp.dot(turned_ref[:, rows], dlogits, preferred_element_type=F32)
        return carry

    lax.fori_loop(0, count, one, 0)


def teacher_grad(teacher, turned, table, lse, weight, grad):
    count, length, size = teacher.shape
    width, tokens = turned.shape
    tile = tile_of(size)
    whole = lambda *shape: pl.BlockSpec(shape, lambda j: (0, 0))
    return pl.pallas_call(
        teacher_grad_kernel,
        grid=(size // tile,),
        out_shape=[jax.ShapeDtypeStruct((tokens, width), F32), jax.ShapeDtypeStruct((width, size), F32)],
        in_specs=[
            pl.BlockSpec((count, length, tile), lambda j: (0, 0, j)),
            whole(width, tokens),
            pl.BlockSpec((width, tile), lambda j: (0, j)),
            whole(tokens, 1),
            whole(tokens, 1),
            pl.BlockSpec((width, tile), lambda j: (0, j)),
        ],
        out_specs=[whole(tokens, width), pl.BlockSpec((width, tile), lambda j: (0, j))],
        compiler_params=pltpu.CompilerParams(vmem_limit_bytes=60 * MIB),
    )(teacher, turned, table, lse, weight, grad)


def pick_kernel(block, ids_ref, table_ref, out_ref):
    step = pl.program_id(0)
    tile = table_ref.shape[1]

    @pl.when(step == 0)
    def _():
        out_ref[...] = jnp.zeros(out_ref.shape, F32)

    def one(k, carry):
        rows = pl.ds(pl.multiple_of(k * block, block), block)
        lane = lax.broadcasted_iota(jnp.int32, (block, tile), 1)
        hit = jnp.where(lane == ids_ref[rows, :] - step * tile, 1.0, 0.0).astype(B16)
        out_ref[rows, :] += lax.dot_general(
            hit, table_ref[...], (((1,), (1,)), ((), ())), preferred_element_type=F32
        )
        return carry

    lax.fori_loop(0, ids_ref.shape[0] // block, one, 0)


def pick_rows(ids, table):
    tokens = ids.shape[0]
    width, size = table.shape
    tile = tile_of(size)
    return pl.pallas_call(
        functools.partial(pick_kernel, 512),
        grid=(size // tile,),
        out_shape=jax.ShapeDtypeStruct((tokens, width), F32),
        in_specs=[
            pl.BlockSpec((tokens, 1), lambda j: (0, 0)),
            pl.BlockSpec((width, tile), lambda j: (0, j)),
        ],
        out_specs=pl.BlockSpec((tokens, width), lambda j: (0, 0)),
        compiler_params=pltpu.CompilerParams(vmem_limit_bytes=48 * MIB),
    )(ids, table)


def spread_kernel(ids_ref, turned_ref, grad_ref, out_ref):
    step = pl.program_id(0)
    tile = grad_ref.shape[1]
    count, _, length = turned_ref.shape

    def one(k, total):
        rows = pl.ds(pl.multiple_of(k * length, length), length)
        lane = lax.broadcasted_iota(jnp.int32, (length, tile), 1)
        hit = jnp.where(lane == ids_ref[rows, :] - step * tile, 1.0, 0.0).astype(B16)
        return total + jnp.dot(turned_ref[k], hit, preferred_element_type=F32)

    out_ref[...] = lax.fori_loop(0, count, one, grad_ref[...]).astype(B16)


def spread_rows(ids, turned, grad):
    tokens = ids.shape[0]
    width, size = grad.shape
    tile = tile_of(size)
    return pl.pallas_call(
        spread_kernel,
        grid=(size // tile,),
        out_shape=jax.ShapeDtypeStruct((width, size), B16),
        in_specs=[
            pl.BlockSpec((tokens, 1), lambda j: (0, 0)),
            pl.BlockSpec(turned.shape, lambda j: (0, 0, 0)),
            pl.BlockSpec((width, tile), lambda j: (0, j)),
        ],
        out_specs=pl.BlockSpec((width, tile), lambda j: (0, j)),
        compiler_params=pltpu.CompilerParams(vmem_limit_bytes=48 * MIB),
    )(ids, turned, grad)


def norm_rows(values, gain, shift):
    center = values - jnp.mean(values, -1, keepdims=True)
    scaler = lax.rsqrt(jnp.mean(center * center, -1, keepdims=True) + NORM_EPS)
    normed = center * scaler
    return (normed * gain + shift, normed, scaler)


def norm_back(grad, normed, scaler, gain):
    scaled = grad * gain
    inward = scaler * (
        scaled
        - jnp.mean(scaled, -1, keepdims=True)
        - normed * jnp.mean(scaled * normed, -1, keepdims=True)
    )
    return (inward, jnp.sum(grad * normed, 0), jnp.sum(grad, 0))


def gelu_tanh(values):
    return 0.5 * values * (1.0 + jnp.tanh(GELU_C * (values + 0.044715 * values * values * values)))


def gelu_slope(values):
    tangent = jnp.tanh(GELU_C * (values + 0.044715 * values * values * values))
    return 0.5 * (1.0 + tangent) + 0.5 * values * (1.0 - tangent * tangent) * GELU_C * (
        1.0 + 3.0 * 0.044715 * values * values
    )


def positions(segment):
    codes = jnp.arange(SEGS, dtype=jnp.int32)
    starts = jnp.sum((segment[None, :] < codes[:, None]).astype(jnp.int32), 1)
    member = (segment[:, None] == codes[None, :]).astype(jnp.int32)
    return jnp.arange(segment.shape[0], dtype=jnp.int32) - jnp.sum(member * starts[None, :], 1)


def split_heads(packed):
    width = packed.shape[1] // 3
    return [packed[:, i * width : (i + 1) * width].reshape(packed.shape[0], -1, 64) for i in range(3)]


def masked_scores(queries, keys, segment):
    scores = jnp.einsum("qhd,khd->hqk", queries, keys, preferred_element_type=F32) * 0.125
    return jnp.where((segment[:, None] == segment[None, :])[None], scores, -1e30)


def attend(packed, segment):
    queries, keys, values = split_heads(packed)
    scores = masked_scores(queries, keys, segment)
    top = jnp.max(scores, -1, keepdims=True)
    expd = jnp.exp(scores - top)
    total = jnp.sum(expd, -1, keepdims=True)
    probs = (expd / total).astype(B16)
    context = jnp.einsum("hqk,khd->qhd", probs, values, preferred_element_type=F32)
    return context.reshape(packed.shape[0], -1).astype(B16), (top + jnp.log(total))[..., 0]


def attend_back(packed, segment, lse, dcontext):
    queries, keys, values = split_heads(packed)
    length = packed.shape[0]
    grads = dcontext.reshape(queries.shape)
    probs = jnp.exp(masked_scores(queries, keys, segment) - lse[..., None])
    dprobs = jnp.einsum("qhd,khd->hqk", grads, values, preferred_element_type=F32)
    inner = jnp.sum(probs * dprobs, -1, keepdims=True)
    dscore = (probs * (dprobs - inner) * 0.125).astype(B16)
    parts = (
        jnp.einsum("hqk,khd->qhd", dscore, keys, preferred_element_type=F32),
        jnp.einsum("hqk,qhd->khd", dscore, queries, preferred_element_type=F32),
        jnp.einsum("hqk,qhd->khd", probs.astype(B16), grads, preferred_element_type=F32),
    )
    return jnp.concatenate([p.reshape(length, -1) for p in parts], 1)


def layer_forward(hidden, segment, weights, gains):
    qkv_t, out_t, up_t, down_t = weights
    h_zero, normed_a, scaler_a = norm_rows(hidden, gains[0], gains[1])
    zero_b = h_zero.astype(B16)
    packed = jnp.dot(zero_b, qkv_t, preferred_element_type=F32).astype(B16)
    context_b, lse = attend(packed, segment)
    h_one, normed_b, scaler_b = norm_rows(
        h_zero + jnp.dot(context_b, out_t, preferred_element_type=F32), gains[2], gains[3]
    )
    one_b = h_one.astype(B16)
    inner = jnp.dot(one_b, up_t, preferred_element_type=F32)
    active = gelu_tanh(inner).astype(B16)
    h_two, normed_c, scaler_c = norm_rows(
        h_one + jnp.dot(active, down_t, preferred_element_type=F32), gains[4], gains[5]
    )
    kept = (normed_a, scaler_a, zero_b, packed, lse, context_b, normed_b, scaler_b, one_b, inner, active, normed_c, scaler_c)
    return (kept, h_two)


def layer_backward(dtwo, segment, weights, gains, kept):
    qkv_t, out_t, up_t, down_t = weights
    (normed_a, scaler_a, zero_b, packed, lse, context_b, normed_b, scaler_b, one_b, inner, active, normed_c, scaler_c) = kept
    dz_two, gain_c, shift_c = norm_back(dtwo, normed_c, scaler_c, gains[4])
    dbranch = dz_two.astype(B16)
    grad_down = jnp.einsum("nf,nd->fd", active, dbranch, preferred_element_type=F32)
    dinner = (jnp.dot(dbranch, down_t.T, preferred_element_type=F32) * gelu_slope(inner)).astype(B16)
    grad_up = jnp.einsum("nd,nf->df", one_b, dinner, preferred_element_type=F32)
    dh_one = dz_two + jnp.dot(dinner, up_t.T, preferred_element_type=F32)
    dz_one, gain_b, shift_b = norm_back(dh_one, normed_b, scaler_b, gains[2])
    dproj = dz_one.astype(B16)
    grad_out = jnp.einsum("nc,nd->cd", context_b, dproj, preferred_element_type=F32)
    dcontext = jnp.dot(dproj, out_t.T, preferred_element_type=F32).astype(B16)
    dpacked = attend_back(packed, segment, lse, dcontext).astype(B16)
    grad_qkv = jnp.einsum("nd,ne->de", zero_b, dpacked, preferred_element_type=F32)
    dh_zero = dz_one + jnp.dot(dpacked, qkv_t.T, preferred_element_type=F32)
    dhidden, gain_a, shift_a = norm_back(dh_zero, normed_a, scaler_a, gains[0])
    grad_gains = jnp.stack([gain_a, shift_a, gain_b, shift_b, gain_c, shift_c])
    return (dhidden, (grad_qkv, grad_out, grad_up, grad_down), grad_gains)


def adam(weight, first, second, grad, fix_one, fix_two, rate):
    first = BETA_ONE * first + (1.0 - BETA_ONE) * grad
    second = BETA_TWO * second + (1.0 - BETA_TWO) * grad * grad
    update = first / fix_one / (jnp.sqrt(second / fix_two) + ADAM_EPS)
    return (first, second, weight - rate * (update + WEIGHT_DECAY * weight))


def on_device(
    D, V,
    token_ids, segment_ids, labels, loss_mask, teacher_group, teacher_inputs, teacher_table,
    teacher_qkv, teacher_out, teacher_up, teacher_down, teacher_gains, step_count,
    embed_w, embed_m, embed_v, pos_w, pos_m, pos_v, qkv_w, qkv_m, qkv_v,
    out_w, out_m, out_v, up_w, up_m, up_v, down_w, down_m, down_v, gains_w, gains_m, gains_v,
):
    length = token_ids.shape[1]
    slice_len, columns = embed_w.shape
    width = gains_w.shape[1]
    d, v = lax.axis_index("dp"), lax.axis_index("vocab")
    segment = segment_ids[0]

    turned_table = embed_w.astype(B16).T.reshape(2, columns // 2, slice_len)
    attention = jnp.concatenate([qkv_w, out_w], 1).astype(B16)[None]
    integers = jnp.concatenate(
        [token_ids, labels, loss_mask, jnp.broadcast_to(teacher_group[:, None], (1, length)),
         jnp.zeros((4, length), jnp.int32)], 0
    )[None]
    table, attention, up_t, down_t, pos_t, integers = ring_gather(
        D, V,
        [turned_table, attention, up_w.astype(B16)[None], down_w.astype(B16)[None], pos_w.astype(B16)[None], integers],
        ((0, 0, False, "dp", 0), (0, 1, False, "dp", 1), (5, 0, True, 2, 1), (1, 0, True, 0, 0), (2, 0, True, 1, 1),
         (3, 0, True, 2, 0), (4, 0, True, 1, 0)),
        1,
    )
    table = table.reshape(width, slice_len)
    attention = attention.reshape(width, -1)
    qkv_t, out_t = attention[:, : 3 * width], attention[:, 3 * width :]
    up_t, down_t, pos_t = up_t.reshape(width, -1), down_t.reshape(-1, width), pos_t.reshape(-1, width)
    weights = (qkv_t, out_t, up_t, down_t)
    integers = integers.reshape(D, V, 8, length)
    counted = jnp.maximum(jnp.sum(integers[:, :, 2].astype(F32)), 1.0)
    group_ints = lax.dynamic_index_in_dim(integers, d, 0, False)
    offset = v * slice_len
    ids_here = (group_ints[:, 0].reshape(-1, 1) - offset)
    labels_here = (group_ints[:, 1].reshape(-1, 1) - offset)
    counts = group_ints[:, 2].reshape(-1).astype(F32)
    groups = group_ints[:, 3, 0]

    picked = pick_rows(ids_here, table).astype(B16).reshape(V, length, width)
    embedded = vocab_scatter(V, picked, 2)
    places = positions(segment)
    onehot = (places[:, None] == jnp.arange(pos_t.shape[0], dtype=jnp.int32)[None, :]).astype(B16)
    hidden = embedded + jnp.dot(onehot, pos_t, preferred_element_type=F32)
    kept, h_two = layer_forward(hidden, segment, weights, gains_w)
    two_b = h_two.astype(B16)

    weight = counts / counted
    given = jnp.concatenate([weight[:, None], labels_here.astype(F32)], 1)
    first = jnp.concatenate([teacher_qkv, teacher_out, teacher_up], 2)
    first, second, hidden_all, turned, dh_student, grad_head, told = study(
        D, V, first, teacher_down, two_b, table, given, 4
    )
    student_lse, picked = told[0], told[1]
    mine = teacher_group[0]
    tw = teacher_qkv.shape[2] // 3
    first = lax.dynamic_index_in_dim(first, mine, 0, False).reshape(tw, -1)
    second = lax.dynamic_index_in_dim(second, mine, 0, False).reshape(-1, tw)
    chosen = (first[:, : 3 * tw], first[:, 3 * tw : 4 * tw], first[:, 4 * tw :], second)
    gains_row = lax.dynamic_index_in_dim(teacher_gains, mine, 0, False)
    _, teacher_top = layer_forward(teacher_inputs[0].astype(F32), segment, chosen, gains_row)
    (teacher_hidden,) = vocab_gather(V, [teacher_top.astype(B16)], 5)

    teacher, stats = teacher_stats(groups, teacher_hidden, teacher_table)
    stats = lax.all_gather(stats, "vocab")
    top = jnp.max(stats[:, 0], 0)
    scale = jnp.exp(stats[:, 0] - top)
    tsum = jnp.sum(stats[:, 1] * scale, 0)
    tcross = jnp.sum(stats[:, 2] * scale, 0) / tsum
    teacher_lse = top + jnp.log(tsum)
    dh_teacher, grad_head = teacher_grad(
        teacher, turned, table, teacher_lse[:, None], weight[:, None], grad_head
    )
    everywhere = jnp.sum(hidden_all.astype(F32) * dh_teacher) - jnp.sum(weight * picked)
    once = jnp.sum(weight * (MIX_ALPHA * (tcross - teacher_lse + student_lse) + student_lse))
    loss_part = everywhere + jnp.where(v == 0, once, 0.0)

    dtwo = vocab_scatter(V, (dh_student + dh_teacher).astype(B16).reshape(V, length, width), 6)
    dhidden, dense_grads, grad_gains = layer_backward(dtwo, segment, weights, gains_w, kept)
    dhidden_b = dhidden.astype(B16)
    grad_pos = lax.dot_general(onehot, dhidden_b, (((0,), (0,)), ((), ())), preferred_element_type=F32)
    (turned_grads,) = vocab_gather(V, [dhidden_b.T], 7)
    grad_embed = spread_rows(ids_here, turned_grads, grad_head)

    grad_qkv, grad_out, grad_up, grad_down = dense_grads
    owners = lambda g: g.astype(B16).reshape(D * V // 2, 2, -1, g.shape[1])
    grad_embed = grad_embed.reshape(D, 2, columns // 2, slice_len)
    sums = ring_scatter(
        D, V,
        [grad_embed[:, 0], grad_embed[:, 1], owners(jnp.concatenate([grad_qkv, grad_out], 1)), owners(grad_up),
         owners(grad_down), owners(grad_pos)],
        (("dp", 0), ("dp", 1), (0, 0), (1, 1), (2, 0), (1, 0)),
        8,
    )
    grad_embed = jnp.concatenate(sums[:2], 0)
    owned = (sums[5], sums[2][:, : 3 * width], sums[2][:, 3 * width :], sums[3], sums[4])
    squares = jnp.sum(grad_embed * grad_embed)
    for grad in (sums[2], sums[3], sums[4], sums[5]):
        squares = squares + jnp.sum(grad * grad)
    lane = lax.broadcasted_iota(jnp.int32, (2, width), 1)
    scalars = jnp.where(lane == 0, squares, jnp.where(lane == 1, loss_part, 0.0))
    totals = total_all(D, V, jnp.concatenate([grad_gains, scalars], 0), 9)
    gains_grad, squares, loss = totals[:6], totals[6, 0], totals[6, 1]

    grad_norm = jnp.sqrt(squares + jnp.sum(gains_grad * gains_grad))
    factor = CLIP_NORM / jnp.maximum(grad_norm, CLIP_NORM)
    count_f = step_count.astype(F32)
    fix_one = 1.0 - jnp.power(BETA_ONE, count_f)
    fix_two = 1.0 - jnp.power(BETA_TWO, count_f)

    def update(weight, first, second, grad, rate):
        return adam(weight, first, second, grad * factor, fix_one, fix_two, rate)

    out = [loss, grad_norm]
    out += update(embed_w, embed_m, embed_v, grad_embed.T, LEARN_RATE)
    out += update(pos_w, pos_m, pos_v, owned[0], LEARN_RATE)
    out += update(qkv_w, qkv_m, qkv_v, owned[1], LEARN_RATE)
    out += update(out_w, out_m, out_v, owned[2], LEARN_RATE)
    out += update(up_w, up_m, up_v, owned[3], LEARN_RATE)
    out += update(down_w, down_m, down_v, owned[4], LEARN_RATE)
    out += update(gains_w, gains_m, gains_v, gains_grad, GAIN_RATE)
    return tuple(out)


def solution(mesh):
    rows, whole = P(("dp", "vocab"), None), P()
    split = P(None, ("dp", "vocab"), None)
    embed = P("vocab", "dp")
    return jax.shard_map(
        functools.partial(on_device, mesh.shape["dp"], mesh.shape["vocab"]),
        mesh=mesh,
        in_specs=(rows, rows, rows, rows, P(("dp", "vocab")), P(("dp", "vocab"), None, None), P(None, None, "vocab"),
                  split, split, split, split, whole, whole)
        + (embed,) * 3 + (rows,) * 15 + (whole,) * 3,
        out_specs=(whole, whole) + (embed,) * 3 + (rows,) * 15 + (whole,) * 3,
        check_vma=False,
    )
```

```python
import functools

import jax
import jax.numpy as jnp
from jax import lax
from jax.experimental import pallas as pl
from jax.experimental.pallas import tpu as pltpu
from jax.sharding import PartitionSpec as P

SEGS = 8
NORM_EPS = 1e-05
MIX_ALPHA = 0.5
CLIP_NORM = 0.005
LEARN_RATE = 0.03
GAIN_RATE = 0.4
BETA_ONE = 0.9
BETA_TWO = 0.999
ADAM_EPS = 1e-08
WEIGHT_DECAY = 0.01
GELU_C = 0.7978845608028654
MESH = pl.DeviceIdType.MESH
F32 = jnp.float32
B16 = jnp.bfloat16
ANYWHERE = pl.BlockSpec(memory_space=pl.ANY)
IN_VMEM = pl.BlockSpec(memory_space=pltpu.VMEM)
MIB = 1 << 20

CYCLES = (
    (0, 1, 3, 2, 6, 7, 5, 9, 11, 10, 14, 15, 13, 12, 8, 4),
    (0, 1, 5, 4, 6, 10, 8, 9, 13, 12, 14, 15, 11, 7, 3, 2),
    (0, 2, 6, 7, 3, 1, 5, 9, 13, 15, 11, 10, 14, 12, 8, 4),
)


def chip_cycle(count, which):
    return CYCLES[which] if count == 16 else tuple(range(count))


def dp_cycle(count):
    return tuple(range(0, count, 2)) + tuple(range(count - 1 - count % 2, 0, -2))


def lookup(table, index):
    out = jnp.int32(table[0])
    for k in range(1, len(table)):
        out = jnp.where(index == k, table[k], out)
    return out


class Ring:
    def __init__(self, D, V, which):
        self.D, self.V = D, V
        d, v = lax.axis_index("dp"), lax.axis_index("vocab")
        self.core, self.v = lax.rem(v, 2), v
        self.over_dp = which == "dp"
        self.n = D if self.over_dp else D * V // 2
        self.table = dp_cycle(D) if self.over_dp else chip_cycle(self.n, which)
        self.me = d if self.over_dp else d * (V // 2) + v // 2
        inverse = tuple(self.table.index(k) for k in range(self.n))
        self.pos = lookup(inverse, self.me)

    def at(self, ahead):
        return lookup(self.table, lax.rem(self.pos + ahead + self.n, self.n))

    def device(self, place):
        if self.over_dp:
            return (place, self.v)
        half = self.V // 2
        return (place // half, lax.rem(place, half) * 2 + self.core)

    def hops(self, parity):
        more, less = self.n // 2, self.n - 1 - self.n // 2
        return (more, less) if parity == 0 else (less, more)


def sibling():
    v = lax.axis_index("vocab")
    return (lax.axis_index("dp"), v + 1 - 2 * lax.rem(v, 2))


def greet(devices):
    barrier = pltpu.get_barrier_semaphore()
    for device in devices:
        pl.semaphore_signal(barrier, inc=1, device_id=device, device_id_type=MESH)
    pl.semaphore_wait(barrier, len(devices))


def on_condition(condition, body):
    if condition is True:
        body()
    elif condition is not False:
        pl.when(condition)(body)


class Gather:
    def __init__(self, D, V, spec, ins, outs, sems):
        self.spec, self.ins, self.outs = spec, ins, outs
        self.ssem, self.rsem, self.xssem, self.xrsem, self.lsem = sems
        rings = {w: Ring(D, V, w) for w in dict.fromkeys(p[3] for p in spec)}
        self.core = lax.rem(lax.axis_index("vocab"), 2)
        self.sib = sibling()
        self.nexts = {w: (r.at(1), r.at(-1)) for w, r in rings.items()}
        self.neighbours = [r.device(place) for w, r in rings.items() for place in self.nexts[w]]
        if any(p[3] != "dp" for p in spec):
            self.neighbours.append(self.sib)
        self.streams = []
        for number, piece in enumerate(spec):
            ring = rings[piece[3]]
            for turn, hops in zip((0, 1), ring.hops(piece[4])):
                self.streams.append((piece, ring, turn, hops, number))
        self.longest = max(s[3] for s in self.streams)
        most = {w: max(r.hops(0)) for w, r in rings.items()}
        self.every = {w: max(1, self.longest // max(m, 1)) for w, m in most.items()}

    def dst(self, piece, slot):
        which, k, lead, _, _ = piece
        return self.outs[which].at[k, slot] if lead else self.outs[which].at[slot, k]

    def slot_of(self, ring, place):
        return place if ring.over_dp else place * 2 + self.core

    def origin(self, stream, s):
        _, ring, turn, _, _ = stream
        return self.slot_of(ring, ring.at(-s) if turn == 0 else ring.at(s))

    def remote(self, i, s, src, slot):
        piece, ring, turn, _, _ = self.streams[i]
        return pltpu.make_async_remote_copy(
            src_ref=src,
            dst_ref=self.dst(piece, slot),
            send_sem=self.ssem.at[s, i],
            recv_sem=self.rsem.at[s, i],
            device_id=ring.device(self.nexts[piece[3]][turn]),
            device_id_type=MESH,
        )

    def across(self, i, s, src, slot):
        return pltpu.make_async_remote_copy(
            src_ref=src,
            dst_ref=self.dst(self.streams[i][0], slot),
            send_sem=self.xssem.at[s, i],
            recv_sem=self.xrsem.at[s, i],
            device_id=self.sib,
            device_id_type=MESH,
        )

    def own(self, i):
        piece, ring, _, _, _ = self.streams[i]
        return self.ins[piece[0]].at[piece[1]], self.slot_of(ring, ring.me)

    def begin(self):
        for i in range(len(self.streams)):
            self.remote(i, 0, *self.own(i)).start()
        for i, stream in enumerate(self.streams):
            if stream[2] == 0:
                src, slot = self.own(i)
                pltpu.make_async_copy(src, self.dst(stream[0], slot), self.lsem.at[stream[4]]).start()
                if not stream[1].over_dp:
                    self.across(i, 0, src, slot).start()

    def within(self, s, hops):
        return True if hops == self.longest else s <= hops

    def serve(self, step):
        for i, stream in enumerate(self.streams):
            every = self.every[stream[0][3]]
            s = step // every

            def take(i=i, stream=stream, s=s):
                slot = self.origin(stream, s)
                block = self.dst(stream[0], slot)
                self.remote(i, s - 1, block, slot).wait_recv()
                pl.when(s < stream[3])(lambda: self.remote(i, s, block, slot).start())
                if not stream[1].over_dp:
                    self.across(i, s, block, slot).start()

            condition = self.within(s, stream[3])
            if every > 1:
                condition = (lax.rem(step, every) == 0) & (s <= stream[3])
            on_condition(condition, take)

    def serve_range(self, low, high):
        def body(s, carry):
            self.serve(s)
            return carry

        lax.fori_loop(low, high, body, 0)

    def finish(self):
        def last(s, carry):
            for i, stream in enumerate(self.streams):

                def end(i=i, stream=stream):
                    slot = self.origin(stream, s)
                    block = self.dst(stream[0], slot)
                    pl.when(s < stream[3])(lambda: self.remote(i, s, block, slot).wait_send())
                    if not stream[1].over_dp:

                        def crossed():
                            self.across(i, s, block, slot).wait_send()
                            theirs = slot + 1 - 2 * self.core
                            self.across(i, s, block, theirs).wait_recv()

                        on_condition(True if stream[2] == 0 else s > 0, crossed)

                on_condition(self.within(s, stream[3]), end)
            return carry

        lax.fori_loop(0, self.longest + 1, last, 0)
        for i, stream in enumerate(self.streams):
            if stream[2] == 0:
                src, slot = self.own(i)
                pltpu.make_async_copy(src, self.dst(stream[0], slot), self.lsem.at[stream[4]]).wait()


def gather_kernel(D, V, spec, count, *refs):
    gather = Gather(D, V, spec, refs[:count], refs[count : 2 * count], refs[2 * count :])
    greet(gather.neighbours)
    gather.begin()
    gather.serve_range(1, gather.longest + 1)
    gather.finish()


def gather_plan(D, V, arrays, spec):
    shapes = []
    for which, array in enumerate(arrays):
        piece = next(p for p in spec if p[0] == which)
        places = D if piece[3] == "dp" else D * V
        lead = array.shape[:1]
        shape = lead + (places,) if piece[2] else (places,) + lead
        shapes.append(jax.ShapeDtypeStruct(shape + array.shape[1:], array.dtype))
    longest = max((D if p[3] == "dp" else D * V // 2) // 2 for p in spec) + 1
    sems = pltpu.SemaphoreType.DMA((longest, 2 * len(spec)))
    return shapes, [sems] * 4 + [pltpu.SemaphoreType.DMA((len(spec),))]


def ring_gather(D, V, arrays, spec, ident):
    shapes, sems = gather_plan(D, V, arrays, spec)
    return pl.pallas_call(
        functools.partial(gather_kernel, D, V, spec, len(arrays)),
        out_shape=shapes,
        in_specs=[ANYWHERE] * len(arrays),
        out_specs=[ANYWHERE] * len(arrays),
        scratch_shapes=sems,
        compiler_params=pltpu.CompilerParams(collective_id=ident, has_side_effects=True),
    )(*arrays)


class Scatter:
    def __init__(self, pieces, sems):
        self.pieces = pieces
        self.ssem, self.rsem = sems
        self.streams = []
        for number, (ring, parity, _, _) in enumerate(pieces):
            for turn, hops in zip((0, 1), ring.hops(parity)):
                if hops:
                    self.streams.append((number, ring, turn, hops))
        self.longest = max(s[3] for s in self.streams)

    def place(self, stream, ahead):
        return stream[1].at(ahead) if stream[2] == 0 else stream[1].at(-ahead)

    def slots(self, stream):
        return self.pieces[stream[0]][3][stream[2]]

    def remote(self, i, s, src):
        stream = self.streams[i]
        return pltpu.make_async_remote_copy(
            src_ref=src,
            dst_ref=self.slots(stream).at[s],
            send_sem=self.ssem.at[s, i],
            recv_sem=self.rsem.at[s, i],
            device_id=stream[1].device(self.place(stream, 1)),
            device_id_type=MESH,
        )

    def first(self, i):
        stream = self.streams[i]
        return self.remote(i, 0, self.pieces[stream[0]][2].at[self.place(stream, stream[3])])

    def begin(self, number):
        for i, stream in enumerate(self.streams):
            if stream[0] == number:
                self.first(i).start()

    def serve(self, s):
        for i, stream in enumerate(self.streams):
            hops = stream[3]

            def take(i=i, stream=stream, hops=hops):
                block = self.slots(stream).at[s - 1]
                self.remote(i, s - 1, block).wait_recv()

                def onward():
                    mine = self.pieces[stream[0]][2].at[self.place(stream, hops - s)]
                    block[...] = (block[...].astype(F32) + mine[...].astype(F32)).astype(B16)
                    self.remote(i, s, block).start()

                pl.when(s < hops)(onward)

            on_condition(True if hops == self.longest else s <= hops, take)

    def serve_range(self, low, high):
        def body(s, carry):
            self.serve(s)
            return carry

        lax.fori_loop(low, high, body, 0)

    def total(self, number):
        ring, parity, terms, slots = self.pieces[number]
        total = terms[ring.me].astype(F32)
        for turn, hops in zip((0, 1), ring.hops(parity)):
            if hops:
                total = total + slots[turn][hops - 1].astype(F32)
        return total

    def finish(self):
        for i, stream in enumerate(self.streams):
            self.first(i).wait_send()

            def sent(s, carry, i=i, stream=stream):
                self.remote(i, s, self.slots(stream).at[s - 1]).wait_send()
                return carry

            lax.fori_loop(1, stream[3], sent, 0)


def settle_kernel(D, V, rings, *refs):
    count = len(rings)
    table_in, dx_ref, ids_ref, gains_ref = refs[:4]
    dense_in, refs = refs[4 : 4 + count], refs[4 + count :]
    table_out, totals_out = refs[:2]
    dense_out, refs = refs[2 : 2 + count], refs[2 + count :]
    dx_all, table_sums, table_slots, first, second = refs[:5]
    dense_sums, refs = refs[5 : 5 + count], refs[5 + count :]
    dense_slots, refs = refs[: 2 * count], refs[2 * count :]
    ts, tr, ds, dr, cs, cr, hs, hr, xs, xr, ns, nr = refs
    d, v = lax.axis_index("dp"), lax.axis_index("vocab")
    half = V // 2
    core, chip = lax.rem(v, 2), v // 2
    sib = sibling()
    width, length = dx_ref.shape
    chunks, _, columns, tile = table_sums.shape
    over_dp = Ring(D, V, "dp")
    chips = {w: Ring(D, V, w) for w in dict.fromkeys(rings)}
    more, less = over_dp.hops(0)
    table = Scatter(
        [
            (over_dp, c % 2, table_sums.at[c], (table_slots.at[c], table_slots.at[c, pl.ds(over_dp.hops(c % 2)[0], over_dp.hops(c % 2)[1])]))
            for c in range(chunks)
        ],
        (ts, tr),
    )
    dense = Scatter(
        [
            (chips[w], k % 2, dense_sums[k], (dense_slots[2 * k], dense_slots[2 * k + 1]))
            for k, w in enumerate(rings)
        ],
        (ds, dr),
    )
    peers = [(d, lax.rem(v + k, V)) for k in range(1, V)]
    peers += [(lax.rem(d + k, D), v) for k in range(1, D)]
    near = [r.device(r.at(k)) for r in (over_dp, *chips.values()) for k in (1, -1)]
    greet(near + peers)

    def other(k):
        return lax.rem(chip + k + half, half) * 2 + core

    def send(k):
        return pltpu.make_async_remote_copy(
            src_ref=dx_ref, dst_ref=dx_all.at[v], send_sem=hs.at[k], recv_sem=hr.at[k],
            device_id=(d, other(k)), device_id_type=MESH,
        )

    def across(k, src, slot):
        return pltpu.make_async_remote_copy(
            src_ref=src, dst_ref=dx_all.at[slot], send_sem=xs.at[k], recv_sem=xr.at[k],
            device_id=sib, device_id_type=MESH,
        )

    def crossing(k):
        return pltpu.make_async_remote_copy(
            src_ref=dense_in[k].at[:, 1 - core], dst_ref=dense_sums[k], send_sem=cs.at[k], recv_sem=cr.at[k],
            device_id=sib, device_id_type=MESH,
        )

    for k in range(1, half):
        send(k).start()
    for k in range(count):
        crossing(k).start()
    across(0, dx_ref, v).start()
    dx_all[v] = dx_ref[...]
    for k in range(count):
        crossing(k).wait_recv()

        def add(place, carry, k=k):
            total = dense_sums[k][place].astype(F32) + dense_in[k][place, core].astype(F32)
            dense_sums[k][place] = total.astype(B16)
            return carry

        lax.fori_loop(0, D * half, add, 0)
        dense.begin(k)
    for k in range(1, half):
        slot = other(-k)
        send(k).wait_recv()
        across(k, dx_all.at[slot], slot).start()
    for k in range(half):
        across(k, dx_ref, other(-k) + 1 - 2 * core).wait_recv()

    for c in range(chunks):
        grad = table_in[:, c * tile : (c + 1) * tile].astype(F32)
        lane = lax.broadcasted_iota(jnp.int32, (length, tile), 1) + c * tile
        for k in range(V):
            hit = jnp.where(lane == ids_ref[k * length : (k + 1) * length, :], 1.0, 0.0).astype(B16)
            grad = grad + mm(dx_all[k], hit)
        table_sums[c] = grad.astype(B16).reshape(D, columns, tile)
        table.begin(c)
        dense.serve_range(1 + c * dense.longest // chunks, 1 + (c + 1) * dense.longest // chunks)
    squares = jnp.zeros((1, 1), F32)
    for k in range(count):
        total = dense.total(k)
        dense_out[k][...] = total
        squares += jnp.sum(jnp.sum(total * total, 1, keepdims=True), 0, keepdims=True)
    table.serve_range(1, table.longest + 1)
    for c in range(chunks):
        total = table.total(c)
        table_out[:, c * tile : (c + 1) * tile] = total
        squares += jnp.sum(jnp.sum(total * total, 1, keepdims=True), 0, keepdims=True)
    row = lax.broadcasted_iota(jnp.int32, gains_ref.shape, 0)
    lane = lax.broadcasted_iota(jnp.int32, gains_ref.shape, 1)
    local = jnp.where((row == gains_ref.shape[0] - 1) & (lane == 0), squares, gains_ref[...])

    def tell(k):
        over, mine = (first, v) if k < V - 1 else (second, d)
        return pltpu.make_async_remote_copy(
            src_ref=over.at[mine], dst_ref=over.at[mine], send_sem=ns.at[k], recv_sem=nr.at[k],
            device_id=peers[k], device_id_type=MESH,
        )

    def stage(slots, mine, value, low, high):
        slots[mine] = value
        for k in range(low, high):
            tell(k).start()
        for k in range(low, high):
            tell(k).wait_recv()
        total = slots[0]
        for k in range(1, slots.shape[0]):
            total = total + slots[k]
        return total

    local = stage(first, v, local, 0, V - 1)
    totals_out[...] = stage(second, d, local, V - 1, V + D - 2)
    for k in range(V + D - 2):
        tell(k).wait_send()
    for k in range(1, half):
        send(k).wait_send()
    for k in range(half):
        across(k, dx_ref, v).wait_send()
    for k in range(count):
        crossing(k).wait_send()
    dense.finish()
    table.finish()


def settle(D, V, grad, dx, ids, gains, dense, rings, ident):
    width, size = grad.shape
    length = dx.shape[1]
    tile = tile_of(size, V * length)
    chunks, columns = size // tile, width // D
    n = D * V // 2
    count = len(dense)
    blocks = [a.shape[-2:] for a in dense]
    more, less = n // 2, n - 1 - n // 2
    slots = []
    for k, block in enumerate(blocks):
        slots += [pltpu.VMEM((h,) + block, B16) for h in ((more, less), (less, more))[k % 2]]
    sems = lambda *shape: pltpu.SemaphoreType.DMA(shape)
    return pl.pallas_call(
        functools.partial(settle_kernel, D, V, rings),
        out_shape=[jax.ShapeDtypeStruct((columns, size), F32), jax.ShapeDtypeStruct(gains.shape, F32)]
        + [jax.ShapeDtypeStruct(block, F32) for block in blocks],
        in_specs=[IN_VMEM] * (4 + count),
        out_specs=[IN_VMEM] * (2 + count),
        scratch_shapes=[
            pltpu.VMEM((V, width, length), B16),
            pltpu.VMEM((chunks, D, columns, tile), B16),
            pltpu.VMEM((chunks, D - 1, columns, tile), B16),
            pltpu.VMEM((V,) + gains.shape, F32),
            pltpu.VMEM((D,) + gains.shape, F32),
        ]
        + [pltpu.VMEM((n,) + block, B16) for block in blocks]
        + slots
        + [sems(D // 2, 2 * chunks)] * 2
        + [sems(n // 2, 2 * count)] * 2
        + [sems(count)] * 2
        + [sems(V // 2)] * 4
        + [sems(V + D - 2)] * 2,
        compiler_params=pltpu.CompilerParams(
            collective_id=ident, has_side_effects=True, vmem_limit_bytes=62 * MIB
        ),
    )(grad, dx, ids, gains, *dense)


def vocab_gather_kernel(V, count, *refs):
    ins, outs = refs[:count], refs[count : 2 * count]
    ssem, rsem, xssem, xrsem, lsem = refs[2 * count :]
    d, v = lax.axis_index("dp"), lax.axis_index("vocab")
    half = V // 2
    core, chip = lax.rem(v, 2), v // 2
    sib = sibling()

    def other(k):
        return lax.rem(chip + k + half, half) * 2 + core

    greet([(d, other(k)) for k in range(1, half)] + [sib])

    def send(q, k):
        return pltpu.make_async_remote_copy(
            src_ref=ins[q],
            dst_ref=outs[q].at[v],
            send_sem=ssem.at[q, k],
            recv_sem=rsem.at[q, k],
            device_id=(d, other(k)),
            device_id_type=MESH,
        )

    def across(q, k, src, slot):
        return pltpu.make_async_remote_copy(
            src_ref=src,
            dst_ref=outs[q].at[slot],
            send_sem=xssem.at[q, k],
            recv_sem=xrsem.at[q, k],
            device_id=sib,
            device_id_type=MESH,
        )

    for q in range(count):
        for k in range(1, half):
            send(q, k).start()
    for q in range(count):
        across(q, 0, ins[q], v).start()
        pltpu.make_async_copy(ins[q], outs[q].at[v], lsem.at[q]).start()
    for q in range(count):
        for k in range(1, half):
            slot = other(-k)
            send(q, k).wait_recv()
            across(q, k, outs[q].at[slot], slot).start()
    for q in range(count):
        pltpu.make_async_copy(ins[q], outs[q].at[v], lsem.at[q]).wait()
        for k in range(half):
            slot = other(-k)
            if k:
                send(q, k).wait_send()
            across(q, k, outs[q].at[slot], slot).wait_send()
            across(q, k, outs[q].at[slot], slot + 1 - 2 * core).wait_recv()


def vocab_gather(V, arrays, ident):
    count = len(arrays)
    sems = pltpu.SemaphoreType.DMA((count, V // 2))
    return pl.pallas_call(
        functools.partial(vocab_gather_kernel, V, count),
        out_shape=[jax.ShapeDtypeStruct((V,) + a.shape, a.dtype) for a in arrays],
        in_specs=[ANYWHERE] * count,
        out_specs=[ANYWHERE] * count,
        scratch_shapes=[sems] * 4 + [pltpu.SemaphoreType.DMA((count,))],
        compiler_params=pltpu.CompilerParams(collective_id=ident, has_side_effects=True),
    )(*arrays)


def vocab_scatter_kernel(V, in_ref, out_ref, sums, taken, ssem, rsem, xsem):
    d, v = lax.axis_index("dp"), lax.axis_index("vocab")
    half = V // 2
    core, chip = lax.rem(v, 2), v // 2
    sib = sibling()

    def other(k):
        return lax.rem(chip + k + half, half)

    greet([(d, other(k) * 2 + core) for k in range(1, half)] + [sib])
    across = pltpu.make_async_remote_copy(
        src_ref=in_ref.at[:, 1 - core],
        dst_ref=sums,
        send_sem=xsem.at[0],
        recv_sem=xsem.at[1],
        device_id=sib,
        device_id_type=MESH,
    )
    across.start()
    across.wait_recv()

    def send(k):
        return pltpu.make_async_remote_copy(
            src_ref=sums.at[other(k)],
            dst_ref=taken.at[k - 1],
            send_sem=ssem.at[k - 1],
            recv_sem=rsem.at[k - 1],
            device_id=(d, other(k) * 2 + core),
            device_id_type=MESH,
        )

    for k in [*range(1, half), 0]:
        to = other(k)
        total = sums[to].astype(F32) + in_ref[to, core].astype(F32)
        sums[to] = total.astype(B16)
        if k:
            send(k).start()
    total = sums[chip].astype(F32)
    for k in range(1, half):
        send(k).wait_recv()
        total = total + taken[k - 1].astype(F32)
    out_ref[...] = total
    for k in range(1, half):
        send(k).wait_send()
    across.wait_send()


def vocab_scatter(V, array, ident):
    half = V // 2
    block = array.shape[1:]
    sems = pltpu.SemaphoreType.DMA((max(half - 1, 1),))
    return pl.pallas_call(
        functools.partial(vocab_scatter_kernel, V),
        out_shape=jax.ShapeDtypeStruct(block, F32),
        in_specs=[IN_VMEM],
        out_specs=IN_VMEM,
        scratch_shapes=[
            pltpu.VMEM((half,) + block, B16),
            pltpu.VMEM((max(half - 1, 1),) + block, B16),
            sems,
            sems,
            pltpu.SemaphoreType.DMA((2,)),
        ],
        compiler_params=pltpu.CompilerParams(
            collective_id=ident, has_side_effects=True, vmem_limit_bytes=40 * MIB
        ),
    )(array.reshape((half, 2) + block))


def tile_of(size, tokens=1):
    return next(t for t in (1280, 768, 640, 512, 256, 128) if size % t == 0 and (t * tokens <= 1280 * 2048 or t == 128))


def lane_fold(values, combine):
    out = values[:, :128]
    for k in range(1, values.shape[1] // 128):
        out = combine(out, values[:, k * 128 : (k + 1) * 128])
    return out


def running(values, top_ref, sum_ref, rows):
    old = top_ref[rows, :]
    top = jnp.maximum(old, lane_fold(values, jnp.maximum))
    fade = jnp.exp(old - top)
    expd = jnp.concatenate(
        [jnp.exp(values[:, k * 128 : (k + 1) * 128] - top) for k in range(values.shape[1] // 128)], 1
    )
    top_ref[rows, :] = top
    sum_ref[rows, :] = sum_ref[rows, :] * fade + lane_fold(expd, jnp.add)
    return expd, fade


def pack_rows(columns):
    lane = lax.broadcasted_iota(jnp.int32, (columns[0].shape[0], 128), 1)
    packed = jnp.zeros(lane.shape, F32)
    for k, column in enumerate(columns):
        packed = jnp.where(lane == k, column, packed)
    return packed.T[:8]


def study_kernel(D, V, spec, *refs):
    first_ref, second_ref, own_ref, table_ref, given_ref = refs[:5]
    first_out, second_out, hidden_ref, turned_out, dh_ref, grad_ref, rows_out = refs[5:12]
    top_ref, sum_ref, dl_ref, slots, hs, hr, xs, xr, ps, pr = refs[12:22]
    gather = Gather(D, V, spec, (first_ref, second_ref), (first_out, second_out), refs[22:])
    d, v = lax.axis_index("dp"), lax.axis_index("vocab")
    half = V // 2
    core, chip = lax.rem(v, 2), v // 2
    length, width = own_ref.shape
    tokens, size = V * length, table_ref.shape[1]
    tile, block = tile_of(size, tokens), min(256, length)
    tiles, blocks = size // tile, tokens // block
    peers = [(d, lax.rem(v + k, V)) for k in range(1, V)]
    greet(gather.neighbours + peers)

    def other(k):
        return lax.rem(chip + k + half, half) * 2 + core

    def place(slot):
        return hidden_ref.at[pl.ds(pl.multiple_of(slot * length, length), length)]

    def send(k):
        return pltpu.make_async_remote_copy(
            src_ref=own_ref, dst_ref=place(v), send_sem=hs.at[k], recv_sem=hr.at[k],
            device_id=(d, other(k)), device_id_type=MESH,
        )

    def across(k, src, slot):
        return pltpu.make_async_remote_copy(
            src_ref=src, dst_ref=place(slot), send_sem=xs.at[k], recv_sem=xr.at[k],
            device_id=sibling(), device_id_type=MESH,
        )

    for k in range(1, half):
        send(k).start()
    across(0, own_ref, v).start()
    gather.begin()
    place(v)[...] = own_ref[...]
    top_ref[...] = jnp.full(top_ref.shape, -jnp.inf, F32)
    sum_ref[...] = jnp.zeros(sum_ref.shape, F32)
    dh_ref[...] = jnp.zeros(dh_ref.shape, F32)
    for k in range(1, half):
        slot = other(-k)
        send(k).wait_recv()
        across(k, place(slot), slot).start()
    for k in range(half):
        across(k, place(other(-k)), other(-k) + 1 - 2 * core).wait_recv()

    def columns(t):
        return pl.ds(pl.multiple_of(t * tile, tile), tile)

    early = max(1, gather.longest // 4)
    late = gather.longest - early

    def pass_one(t, carry):
        for k in range(blocks):
            rows = slice(k * block, (k + 1) * block)
            logits = jnp.dot(hidden_ref[rows, :], table_ref[:, columns(t)], preferred_element_type=F32)
            running(logits, top_ref, sum_ref, rows)
        gather.serve_range(1 + t * early // tiles, 1 + (t + 1) * early // tiles)
        return carry

    lax.fori_loop(0, tiles, pass_one, 0)
    top = jnp.max(top_ref[...], 1, keepdims=True)
    total = jnp.sum(sum_ref[...] * jnp.exp(top_ref[...] - top), 1, keepdims=True)
    slots[v] = pack_rows([top, total])

    def tell(k):
        return pltpu.make_async_remote_copy(
            src_ref=slots.at[v], dst_ref=slots.at[v], send_sem=ps.at[k], recv_sem=pr.at[k],
            device_id=peers[k], device_id_type=MESH,
        )

    for k in range(V - 1):
        tell(k).start()
    for q in range(tokens // length):
        rows = slice(q * length, (q + 1) * length)
        turned_out[:, rows] = hidden_ref[rows, :].T
    for k in range(V - 1):
        tell(k).wait_recv()
    top = slots[0, 0:1, :]
    for k in range(1, V):
        top = jnp.maximum(top, slots[k, 0:1, :])
    total = jnp.zeros(top.shape, F32)
    for k in range(V):
        total = total + slots[k, 1:2, :] * jnp.exp(slots[k, 0:1, :] - top)
    lse = top + jnp.log(total)
    rows_out[...] = jnp.broadcast_to(lse, rows_out.shape)
    lse_ref, pick_ref = top_ref, sum_ref
    lse_ref[...] = jnp.broadcast_to(lse, (128, tokens)).T
    pick_ref[...] = jnp.zeros(pick_ref.shape, F32)

    def pass_two(t, carry):
        for k in range(blocks):
            rows = slice(k * block, (k + 1) * block)
            logits = jnp.dot(hidden_ref[rows, :], table_ref[:, columns(t)], preferred_element_type=F32)
            weight = given_ref[rows, 0:1]
            soft = jnp.exp(logits - lse_ref[rows, :1]) * ((1.0 + MIX_ALPHA) * weight)
            lane = lax.broadcasted_iota(jnp.int32, logits.shape, 1)
            hit = lane == given_ref[rows, 1:2].astype(jnp.int32) - t * tile
            dl_ref[rows, :] = jnp.where(hit, soft - weight, soft).astype(B16)
            pick_ref[rows, :] += lane_fold(jnp.where(hit, logits, 0.0), jnp.add)
        for k in range(tokens // length):
            rows = slice(k * length, (k + 1) * length)
            dh_ref[rows, :] += lax.dot_general(
                dl_ref[rows, :], table_ref[:, columns(t)], (((1,), (1,)), ((), ())), preferred_element_type=F32
            )
        grad_ref[:, columns(t)] = jnp.dot(
            turned_out[...], dl_ref[...], preferred_element_type=F32
        ).astype(B16)
        gather.serve_range(1 + early + t * late // tiles, 1 + early + (t + 1) * late // tiles)
        return carry

    lax.fori_loop(0, tiles, pass_two, 0)
    picks = pack_rows([jnp.sum(pick_ref[...], 1, keepdims=True)])
    rows_out[1:2, :] = picks[0:1]
    for k in range(1, half):
        send(k).wait_send()
    for k in range(half):
        across(k, place(other(-k)), other(-k)).wait_send()
    for k in range(V - 1):
        tell(k).wait_send()
    gather.finish()


def study(D, V, first, second, own, table, given, ident):
    spec = tuple((q, r, True, r, q) for r in range(3) for q in range(2))
    shapes, sems = gather_plan(D, V, [first, second], spec)
    length, width = own.shape
    tokens, size = V * length, table.shape[1]
    tile = tile_of(size, tokens)
    halves, singles = pltpu.SemaphoreType.DMA((V // 2,)), pltpu.SemaphoreType.DMA((V,))
    column = pltpu.VMEM((tokens, 128), F32)
    return pl.pallas_call(
        functools.partial(study_kernel, D, V, spec),
        out_shape=shapes
        + [
            jax.ShapeDtypeStruct((tokens, width), B16),
            jax.ShapeDtypeStruct((width, tokens), B16),
            jax.ShapeDtypeStruct((tokens, width), F32),
            jax.ShapeDtypeStruct((width, size), B16),
            jax.ShapeDtypeStruct((8, tokens), F32),
        ],
        in_specs=[ANYWHERE] * 2 + [IN_VMEM] * 3,
        out_specs=[ANYWHERE] * 2 + [IN_VMEM] * 5,
        scratch_shapes=[column] * 2
        + [pltpu.VMEM((tokens, tile), B16), pltpu.VMEM((V, 8, tokens), F32)]
        + [halves] * 4
        + [singles] * 2
        + sems,
        compiler_params=pltpu.CompilerParams(
            collective_id=ident, has_side_effects=True, vmem_limit_bytes=60 * MIB
        ),
    )(first, second, own, table, given)


def teacher_stats_kernel(group_ref, hidden_ref, table_ref, out_ref, stats_ref, top_ref, sum_ref, cross_ref):
    step = pl.program_id(0)
    count, length = hidden_ref.shape[:2]
    block = min(256, length)

    @pl.when(step == 0)
    def _():
        top_ref[...] = jnp.full(top_ref.shape, -jnp.inf, F32)
        sum_ref[...] = jnp.zeros(sum_ref.shape, F32)
        cross_ref[...] = jnp.zeros(cross_ref.shape, F32)

    for row in range(count):
        table = table_ref[group_ref[row]]
        for k in range(length // block):
            inside = slice(k * block, (k + 1) * block)
            rows = slice(row * length + k * block, row * length + (k + 1) * block)
            rounded = mm(hidden_ref[row, inside, :], table).astype(B16)
            out_ref[row, inside, :] = rounded
            values = rounded.astype(F32)
            expd, fade = running(values, top_ref, sum_ref, rows)
            cross_ref[rows, :] = cross_ref[rows, :] * fade + lane_fold(expd * values, jnp.add)

    @pl.when(step == pl.num_programs(0) - 1)
    def _():
        top = jnp.max(top_ref[...], 1, keepdims=True)
        scale = jnp.exp(top_ref[...] - top)
        total = jnp.sum(sum_ref[...] * scale, 1, keepdims=True)
        cross = jnp.sum(cross_ref[...] * scale, 1, keepdims=True)
        stats_ref[...] = pack_rows([top, total, cross])


def teacher_stats(groups, hidden, tables):
    count, length, width = hidden.shape
    kinds, _, size = tables.shape
    tokens = count * length
    tile = tile_of(size, tokens)
    return pl.pallas_call(
        teacher_stats_kernel,
        grid_spec=pltpu.PrefetchScalarGridSpec(
            num_scalar_prefetch=1,
            grid=(size // tile,),
            in_specs=[
                pl.BlockSpec((count, length, width), lambda j, g: (0, 0, 0)),
                pl.BlockSpec((kinds, width, tile), lambda j, g: (0, 0, j)),
            ],
            out_specs=[
                pl.BlockSpec((count, length, tile), lambda j, g: (0, 0, j)),
                pl.BlockSpec((8, tokens), lambda j, g: (0, 0)),
            ],
            scratch_shapes=[pltpu.VMEM((tokens, 128), F32)] * 3,
        ),
        out_shape=[
            jax.ShapeDtypeStruct((count, length, size), B16),
            jax.ShapeDtypeStruct((8, tokens), F32),
        ],
        compiler_params=pltpu.CompilerParams(vmem_limit_bytes=60 * MIB),
    )(groups, hidden, tables)


def teacher_grad_kernel(
    teacher_ref, turned_ref, hidden_ref, table_ref, given_ref, dhin_ref, gradin_ref,
    dh_ref, grad_ref, cross_ref, dl_ref, sum_ref,
):
    step = pl.program_id(0)
    count, length = teacher_ref.shape[:2]
    block = min(256, length)

    @pl.when(step == 0)
    def _():
        sum_ref[...] = dhin_ref[...]

    for row in range(count):
        for k in range(length // block):
            inside = slice(k * block, (k + 1) * block)
            rows = slice(row * length + k * block, row * length + (k + 1) * block)
            target = jnp.exp(teacher_ref[row, inside, :].astype(F32) - given_ref[rows, 1:2])
            dl_ref[rows, :] = ((-MIX_ALPHA * given_ref[rows, 0:1]) * target).astype(B16)
        rows = slice(row * length, (row + 1) * length)
        sum_ref[rows, :] += mm(dl_ref[rows, :], table_ref[...], (1, 1))
    grad_ref[...] = (gradin_ref[...].astype(F32) + mm(turned_ref[...], dl_ref[...])).astype(grad_ref.dtype)

    @pl.when(step == pl.num_programs(0) - 1)
    def _():
        dh_ref[...] = sum_ref[...].astype(B16)
        part = jnp.sum(hidden_ref[...].astype(F32) * (sum_ref[...] - dhin_ref[...]), 1, keepdims=True)
        cross_ref[...] = jnp.broadcast_to(jnp.sum(part, 0, keepdims=True), cross_ref.shape)


def teacher_grad(teacher, turned, hidden, table, given, dh, grad):
    count, length, size = teacher.shape
    width, tokens = turned.shape
    tile = tile_of(size, tokens)
    whole = lambda *shape: pl.BlockSpec(shape, lambda j: (0, 0))
    striped = pl.BlockSpec((width, tile), lambda j: (0, j))
    return pl.pallas_call(
        teacher_grad_kernel,
        grid=(size // tile,),
        out_shape=[
            jax.ShapeDtypeStruct((tokens, width), B16),
            jax.ShapeDtypeStruct((width, size), B16),
            jax.ShapeDtypeStruct((8, 128), F32),
        ],
        in_specs=[
            pl.BlockSpec((count, length, tile), lambda j: (0, 0, j)),
            whole(width, tokens), whole(tokens, width), striped, whole(tokens, 2), whole(tokens, width), striped,
        ],
        out_specs=[whole(tokens, width), striped, whole(8, 128)],
        scratch_shapes=[pltpu.VMEM((tokens, tile), B16), pltpu.VMEM((tokens, width), F32)],
        compiler_params=pltpu.CompilerParams(vmem_limit_bytes=60 * MIB),
    )(teacher, turned, hidden, table, given, dh, grad)


def pick_kernel(block, ids_ref, table_ref, out_ref):
    step = pl.program_id(0)
    tile = table_ref.shape[1]

    @pl.when(step == 0)
    def _():
        out_ref[...] = jnp.zeros(out_ref.shape, F32)

    def one(k, carry):
        rows = pl.ds(pl.multiple_of(k * block, block), block)
        lane = lax.broadcasted_iota(jnp.int32, (block, tile), 1)
        hit = jnp.where(lane == ids_ref[rows, :] - step * tile, 1.0, 0.0).astype(B16)
        out_ref[rows, :] += lax.dot_general(
            hit, table_ref[...], (((1,), (1,)), ((), ())), preferred_element_type=F32
        )
        return carry

    lax.fori_loop(0, ids_ref.shape[0] // block, one, 0, unroll=True)


def pick_rows(ids, table):
    tokens = ids.shape[0]
    width, size = table.shape
    tile = tile_of(size)
    return pl.pallas_call(
        functools.partial(pick_kernel, 512),
        grid=(size // tile,),
        out_shape=jax.ShapeDtypeStruct((tokens, width), F32),
        in_specs=[
            pl.BlockSpec((tokens, 1), lambda j: (0, 0)),
            pl.BlockSpec((width, tile), lambda j: (0, j)),
        ],
        out_specs=pl.BlockSpec((tokens, width), lambda j: (0, 0)),
        compiler_params=pltpu.CompilerParams(vmem_limit_bytes=48 * MIB),
    )(ids, table)


def mm(a, b, over=(1, 0)):
    return lax.dot_general(a, b, (((over[0],), (over[1],)), ((), ())), preferred_element_type=F32)


def norm_rows(values, gain, shift):
    center = values - jnp.mean(values, -1, keepdims=True)
    scaler = lax.rsqrt(jnp.mean(center * center, -1, keepdims=True) + NORM_EPS)
    normed = center * scaler
    return (normed * gain + shift, normed, scaler)


def norm_back(grad, normed, scaler, gain):
    scaled = grad * gain
    inward = scaler * (
        scaled
        - jnp.mean(scaled, -1, keepdims=True)
        - normed * jnp.mean(scaled * normed, -1, keepdims=True)
    )
    return (inward, jnp.sum(grad * normed, 0, keepdims=True), jnp.sum(grad, 0, keepdims=True))


def gelu_both(values):
    square = values * values
    tangent = jnp.tanh(GELU_C * values * (1.0 + 0.044715 * square))
    half = 0.5 * (1.0 + tangent)
    slope = half + 0.5 * values * (1.0 - tangent * tangent) * (GELU_C * (1.0 + 3.0 * 0.044715 * square))
    return values * half, slope


def bias_of(segment_ref, bias_ref):
    length = segment_ref.shape[1]
    row = segment_ref[...]
    column = jnp.broadcast_to(row, (128, length)).T[:, :1]
    bias_ref[...] = jnp.where(column == row, 0.0, -1e30)
    place = lax.broadcasted_iota(jnp.int32, (length, 1), 0)
    for code in range(SEGS):
        start = jnp.sum((row < code).astype(jnp.int32), 1, keepdims=True)
        place = place - jnp.where(column == code, start, 0)
    return place


def softmax(queries, keys, bias):
    scores = mm(queries, keys, (1, 1)) * 0.125 + bias
    expd = jnp.exp(scores - jnp.max(scores, -1, keepdims=True))
    return expd / jnp.sum(expd, -1, keepdims=True)


def pair_of(ref, part, pair, width):
    return ref[:, pl.ds(pl.multiple_of(part * width + pair * 128, 128), 128)]


def layer_forward(x, weights, gains_ref, bias_ref, packed_ref, context_ref):
    qkv_ref, out_ref, up_ref, down_ref = weights
    length, width = x.shape
    gain = lambda k: gains_ref[k : k + 1, :]
    h_zero, normed_a, scaler_a = norm_rows(x, gain(0), gain(1))
    packed_ref[...] = mm(h_zero.astype(B16), qkv_ref[...]).astype(B16)
    low = lax.broadcasted_iota(jnp.int32, (length, 128), 1) < 64

    def heads(pair, carry):
        queries, keys, values = (pair_of(packed_ref, part, pair, width) for part in range(3))
        none = jnp.zeros_like(queries)
        parts = []
        for picked in (jnp.where(low, queries, none), jnp.where(low, none, queries)):
            parts.append(mm(softmax(picked, keys, bias_ref[...]).astype(B16), values))
        context_ref[:, pl.ds(pl.multiple_of(pair * 128, 128), 128)] = jnp.where(low, *parts).astype(B16)
        return carry

    lax.fori_loop(0, width // 128, heads, 0)
    h_one, normed_b, scaler_b = norm_rows(h_zero + mm(context_ref[...], out_ref[...]), gain(2), gain(3))
    one_b = h_one.astype(B16)
    total = h_one
    chunk = 512
    for c in range(up_ref.shape[1] // chunk):
        part = slice(c * chunk, (c + 1) * chunk)
        active = gelu_both(mm(one_b, up_ref[:, part]))[0].astype(B16)
        total = total + mm(active, down_ref[part, :])
    h_two, normed_c, scaler_c = norm_rows(total, gain(4), gain(5))
    return h_two, (normed_a, normed_b, normed_c), (scaler_a, scaler_b, scaler_c)


def teach_kernel(group_ref, x_ref, segment_ref, first_ref, second_ref, gains_ref, top_ref, bias_ref, packed_ref, context_ref):
    width = x_ref.shape[2]
    bias_of(segment_ref, bias_ref)
    first, second = first_ref.at[0], second_ref.at[0]
    weights = (first.at[:, : 3 * width], first.at[:, 3 * width : 4 * width], first.at[:, 4 * width :], second)
    h_two, _, _ = layer_forward(
        x_ref[0].astype(F32), weights, gains_ref.at[0], bias_ref, packed_ref, context_ref
    )
    top_ref[...] = h_two.astype(B16)


def teach(group, x, segment, first, second, gains):
    _, length, width = x.shape
    chosen = lambda shape: pl.BlockSpec((1,) + shape[1:], lambda i, g: (g[0], 0, 0))
    return pl.pallas_call(
        teach_kernel,
        grid_spec=pltpu.PrefetchScalarGridSpec(
            num_scalar_prefetch=1,
            grid=(1,),
            in_specs=[
                pl.BlockSpec((1, length, width), lambda i, g: (0, 0, 0)),
                pl.BlockSpec((1, length), lambda i, g: (0, 0)),
                chosen(first.shape),
                chosen(second.shape),
                chosen(gains.shape),
            ],
            out_specs=pl.BlockSpec((length, width), lambda i, g: (0, 0)),
            scratch_shapes=[
                pltpu.VMEM((length, length), F32),
                pltpu.VMEM((length, 3 * width), B16),
                pltpu.VMEM((length, width), B16),
            ],
        ),
        out_shape=jax.ShapeDtypeStruct((length, width), B16),
        compiler_params=pltpu.CompilerParams(vmem_limit_bytes=60 * MIB),
    )(group, x, segment, first, second, gains)


def learn_kernel(
    rows_ref, segment_ref, pos_ref, attention_ref, up_ref, down_ref, gains_ref,
    top_ref, na_ref, nb_ref, nc_ref, scalers_ref, packed_ref, context_ref, bias_ref,
):
    length, width = rows_ref.shape
    place = bias_of(segment_ref, bias_ref)
    lane = lax.broadcasted_iota(jnp.int32, (length, pos_ref.shape[0]), 1)
    onehot = jnp.where(lane == place, 1.0, 0.0).astype(B16)
    x = rows_ref[...] + mm(onehot, pos_ref[...])
    weights = (attention_ref.at[:, : 3 * width], attention_ref.at[:, 3 * width :], up_ref, down_ref)
    h_two, normed, scalers = layer_forward(x, weights, gains_ref, bias_ref, packed_ref, context_ref)
    top_ref[...] = h_two.astype(B16)
    for ref, value in zip((na_ref, nb_ref, nc_ref), normed):
        ref[...] = value
    lane = lax.broadcasted_iota(jnp.int32, (length, 128), 1)
    scalers_ref[...] = jnp.where(lane == 0, scalers[0], jnp.where(lane == 1, scalers[1], scalers[2]))


def learn(rows, segment, pos, attention, up, down, gains):
    length, width = rows.shape
    square = jax.ShapeDtypeStruct((length, width), F32)
    half = jax.ShapeDtypeStruct((length, width), B16)
    return pl.pallas_call(
        learn_kernel,
        in_specs=[IN_VMEM] * 7,
        out_specs=[IN_VMEM] * 7,
        out_shape=[
            half, square, square, square,
            jax.ShapeDtypeStruct((length, 128), F32),
            jax.ShapeDtypeStruct((length, 3 * width), B16),
            half,
        ],
        scratch_shapes=[pltpu.VMEM((length, length), F32)],
        compiler_params=pltpu.CompilerParams(vmem_limit_bytes=56 * MIB),
    )(rows, segment, pos, attention, up, down, gains)


def back_kernel(
    dtwo_ref, segment_ref, attention_ref, up_ref, down_ref, gains_ref,
    na_ref, nb_ref, nc_ref, scalers_ref, packed_ref, context_ref,
    dx_ref, dattention_ref, dup_ref, ddown_ref, dpos_ref, dgains_ref, bias_ref, dpacked_ref, dcontext_ref,
):
    length, width = dtwo_ref.shape
    gain = lambda k: gains_ref[k : k + 1, :]
    place = bias_of(segment_ref, bias_ref)
    dz_two, gain_c, shift_c = norm_back(dtwo_ref[...], nc_ref[...], scalers_ref[:, 2:3], gain(4))
    dbranch = dz_two.astype(B16)
    one_b = (nb_ref[...] * gain(2) + gain(3)).astype(B16)
    dh_one = dz_two
    chunk = 512
    for c in range(up_ref.shape[1] // chunk):
        part = slice(c * chunk, (c + 1) * chunk)
        active, slope = gelu_both(mm(one_b, up_ref[:, part]))
        ddown_ref[part, :] = mm(active.astype(B16), dbranch, (0, 0)).astype(B16)
        dinner = (mm(dbranch, down_ref[part, :], (1, 1)) * slope).astype(B16)
        dup_ref[:, part] = mm(one_b, dinner, (0, 0)).astype(B16)
        dh_one = dh_one + mm(dinner, up_ref[:, part], (1, 1))
    dz_one, gain_b, shift_b = norm_back(dh_one, nb_ref[...], scalers_ref[:, 1:2], gain(2))
    dproj = dz_one.astype(B16)
    dattention_ref[:, 3 * width :] = mm(context_ref[...], dproj, (0, 0)).astype(B16)
    dcontext_ref[...] = mm(dproj, attention_ref[:, 3 * width :], (1, 1)).astype(B16)
    low = lax.broadcasted_iota(jnp.int32, (length, 128), 1) < 64

    def heads(pair, carry):
        queries, keys, values = (pair_of(packed_ref, part, pair, width) for part in range(3))
        grads = pair_of(dcontext_ref, 0, pair, width)
        none = jnp.zeros_like(queries)
        parts = []
        for first in (True, False):
            pick = lambda a: jnp.where(low, a, none) if first else jnp.where(low, none, a)
            probs = softmax(pick(queries), keys, bias_ref[...])
            dprobs = mm(pick(grads), values, (1, 1))
            inner = jnp.sum(probs * dprobs, -1, keepdims=True)
            dscore = (probs * (dprobs - inner) * 0.125).astype(B16)
            parts.append(
                (mm(dscore, keys), mm(dscore, queries, (0, 0)), mm(probs.astype(B16), grads, (0, 0)))
            )
        for part in range(3):
            columns = pl.ds(pl.multiple_of(part * width + pair * 128, 128), 128)
            dpacked_ref[:, columns] = jnp.where(low, parts[0][part], parts[1][part]).astype(B16)
        return carry

    lax.fori_loop(0, width // 128, heads, 0)
    zero_b = (na_ref[...] * gain(0) + gain(1)).astype(B16)
    dattention_ref[:, : 3 * width] = mm(zero_b, dpacked_ref[...], (0, 0)).astype(B16)
    dh_zero = dz_one + mm(dpacked_ref[...], attention_ref[:, : 3 * width], (1, 1))
    dx, gain_a, shift_a = norm_back(dh_zero, na_ref[...], scalers_ref[:, 0:1], gain(0))
    dx_b = dx.astype(B16)
    lane = lax.broadcasted_iota(jnp.int32, (length, dpos_ref.shape[0]), 1)
    onehot = jnp.where(lane == place, 1.0, 0.0).astype(B16)
    dpos_ref[...] = mm(onehot, dx_b, (0, 0)).astype(B16)
    dx_ref[...] = dx_b.T
    for k, row in enumerate((gain_a, shift_a, gain_b, shift_b, gain_c, shift_c)):
        dgains_ref[k : k + 1, :] = row


def back(dtwo, segment, pos_count, attention, up, down, gains, kept):
    length, width = dtwo.shape
    inputs = (dtwo, segment, attention, up, down, gains) + tuple(kept)
    half = lambda *shape: jax.ShapeDtypeStruct(shape, B16)
    return pl.pallas_call(
        back_kernel,
        in_specs=[IN_VMEM] * len(inputs),
        out_specs=[IN_VMEM] * 6,
        out_shape=[
            half(width, length), half(*attention.shape), half(*up.shape), half(*down.shape),
            half(pos_count, width), jax.ShapeDtypeStruct(gains.shape, F32),
        ],
        scratch_shapes=[
            pltpu.VMEM((length, length), F32),
            pltpu.VMEM((length, 3 * width), B16),
            pltpu.VMEM((length, width), B16),
        ],
        compiler_params=pltpu.CompilerParams(vmem_limit_bytes=60 * MIB),
    )(*inputs)


def adam(weight, first, second, grad, fix_one, fix_two, rate):
    first = BETA_ONE * first + (1.0 - BETA_ONE) * grad
    second = BETA_TWO * second + (1.0 - BETA_TWO) * grad * grad
    update = first / fix_one / (jnp.sqrt(second / fix_two) + ADAM_EPS)
    return (first, second, weight - rate * (update + WEIGHT_DECAY * weight))


def on_device(
    D, V,
    token_ids, segment_ids, labels, loss_mask, teacher_group, teacher_inputs, teacher_table,
    teacher_qkv, teacher_out, teacher_up, teacher_down, teacher_gains, step_count,
    embed_w, embed_m, embed_v, pos_w, pos_m, pos_v, qkv_w, qkv_m, qkv_v,
    out_w, out_m, out_v, up_w, up_m, up_v, down_w, down_m, down_v, gains_w, gains_m, gains_v,
):
    length = token_ids.shape[1]
    slice_len, columns = embed_w.shape
    width = gains_w.shape[1]
    d, v = lax.axis_index("dp"), lax.axis_index("vocab")

    turned_table = embed_w.astype(B16).T.reshape(2, columns // 2, slice_len)
    attention = jnp.concatenate([qkv_w, out_w], 1).astype(B16)[None]
    integers = jnp.concatenate(
        [token_ids, labels, loss_mask, jnp.broadcast_to(teacher_group[:, None], (1, length)),
         jnp.zeros((4, length), jnp.int32)], 0
    )[None]
    table, attention, up_t, down_t, pos_t, integers = ring_gather(
        D, V,
        [turned_table, attention, up_w.astype(B16)[None], down_w.astype(B16)[None], pos_w.astype(B16)[None], integers],
        ((0, 0, False, "dp", 0), (0, 1, False, "dp", 1), (5, 0, True, 2, 1), (1, 0, True, 0, 0), (2, 0, True, 1, 1),
         (3, 0, True, 2, 0), (4, 0, True, 1, 0)),
        1,
    )
    table = table.reshape(width, slice_len)
    attention = attention.reshape(width, -1)
    up_t, down_t, pos_t = up_t.reshape(width, -1), down_t.reshape(-1, width), pos_t.reshape(-1, width)
    integers = integers.reshape(D, V, 8, length)
    counted = jnp.maximum(jnp.sum(integers[:, :, 2].astype(F32)), 1.0)
    group_ints = lax.dynamic_index_in_dim(integers, d, 0, False)
    offset = v * slice_len
    ids_here = (group_ints[:, 0].reshape(-1, 1) - offset)
    labels_here = (group_ints[:, 1].reshape(-1, 1) - offset)
    counts = group_ints[:, 2].reshape(-1).astype(F32)
    groups = group_ints[:, 3, 0]

    picked = pick_rows(ids_here, table).astype(B16).reshape(V, length, width)
    embedded = vocab_scatter(V, picked, 2)
    two_b, *kept = learn(embedded, segment_ids, pos_t, attention, up_t, down_t, gains_w)

    weight = counts / counted
    given = jnp.concatenate([weight[:, None], labels_here.astype(F32)], 1)
    first = jnp.concatenate([teacher_qkv, teacher_out, teacher_up], 2)
    first, second, hidden_all, turned, dh_student, grad_head, told = study(
        D, V, first, teacher_down, two_b, table, given, 4
    )
    student_lse, picked = told[0], told[1]
    tw = teacher_gains.shape[2]
    top = teach(
        teacher_group, teacher_inputs, segment_ids, first.reshape(3, tw, -1), second.reshape(3, -1, tw), teacher_gains
    )
    (teacher_hidden,) = vocab_gather(V, [top], 5)

    teacher, stats = teacher_stats(groups, teacher_hidden, teacher_table)
    stats = lax.all_gather(stats, "vocab")
    top = jnp.max(stats[:, 0], 0)
    scale = jnp.exp(stats[:, 0] - top)
    tsum = jnp.sum(stats[:, 1] * scale, 0)
    tcross = jnp.sum(stats[:, 2] * scale, 0) / tsum
    teacher_lse = top + jnp.log(tsum)
    given = jnp.concatenate([weight[:, None], teacher_lse[:, None]], 1)
    dh, grad_head, cross = teacher_grad(teacher, turned, hidden_all, table, given, dh_student, grad_head)
    once = jnp.sum(weight * (MIX_ALPHA * (tcross - teacher_lse + student_lse) + student_lse))
    loss_part = cross[0, 0] - jnp.sum(weight * picked) + jnp.where(v == 0, once, 0.0)

    dtwo = vocab_scatter(V, dh.reshape(V, length, width), 6)
    turned_dx, grad_attention, grad_up, grad_down, grad_pos, grad_gains = back(
        dtwo, segment_ids, pos_t.shape[0], attention, up_t, down_t, gains_w, kept
    )

    lane = lax.broadcasted_iota(jnp.int32, (2, width), 1)
    scalars = jnp.where(lane == 1, loss_part, 0.0)
    owners = lambda g: g.reshape(D * V // 2, 2, -1, g.shape[1])
    grad_embed, totals, owned_attention, owned_up, owned_down, owned_pos = settle(
        D, V, grad_head, turned_dx, ids_here, jnp.concatenate([grad_gains, scalars], 0),
        [owners(grad_attention), owners(grad_up), owners(grad_down), owners(grad_pos)], (0, 1, 2, 1), 7,
    )
    owned = (owned_pos, owned_attention[:, : 3 * width], owned_attention[:, 3 * width :], owned_up, owned_down)
    gains_grad, squares, loss = totals[:6], totals[7, 0], totals[7, 1]

    grad_norm = jnp.sqrt(squares + jnp.sum(gains_grad * gains_grad))
    factor = CLIP_NORM / jnp.maximum(grad_norm, CLIP_NORM)
    count_f = step_count.astype(F32)
    fix_one = 1.0 - jnp.power(BETA_ONE, count_f)
    fix_two = 1.0 - jnp.power(BETA_TWO, count_f)

    def update(weight, first, second, grad, rate):
        return adam(weight, first, second, grad * factor, fix_one, fix_two, rate)

    out = [loss, grad_norm]
    out += update(embed_w, embed_m, embed_v, grad_embed.T, LEARN_RATE)
    out += update(pos_w, pos_m, pos_v, owned[0], LEARN_RATE)
    out += update(qkv_w, qkv_m, qkv_v, owned[1], LEARN_RATE)
    out += update(out_w, out_m, out_v, owned[2], LEARN_RATE)
    out += update(up_w, up_m, up_v, owned[3], LEARN_RATE)
    out += update(down_w, down_m, down_v, owned[4], LEARN_RATE)
    out += update(gains_w, gains_m, gains_v, gains_grad, GAIN_RATE)
    return tuple(out)


def solution(mesh):
    rows, whole = P(("dp", "vocab"), None), P()
    split = P(None, ("dp", "vocab"), None)
    embed = P("vocab", "dp")
    return jax.shard_map(
        functools.partial(on_device, mesh.shape["dp"], mesh.shape["vocab"]),
        mesh=mesh,
        in_specs=(rows, rows, rows, rows, P(("dp", "vocab")), P(("dp", "vocab"), None, None), P(None, None, "vocab"),
                  split, split, split, split, whole, whole)
        + (embed,) * 3 + (rows,) * 15 + (whole,) * 3,
        out_specs=(whole, whole) + (embed,) * 3 + (rows,) * 15 + (whole,) * 3,
        check_vma=False,
    )
```

```python
import functools

import jax
import jax.numpy as jnp
from jax import lax
from jax.experimental import pallas as pl
from jax.experimental.pallas import tpu as pltpu
from jax.sharding import PartitionSpec as P

SEGS = 8
NORM_EPS = 1e-05
MIX_ALPHA = 0.5
CLIP_NORM = 0.005
LEARN_RATE = 0.03
GAIN_RATE = 0.4
BETA_ONE = 0.9
BETA_TWO = 0.999
ADAM_EPS = 1e-08
WEIGHT_DECAY = 0.01
GELU_C = 0.7978845608028654
MESH = pl.DeviceIdType.MESH
F32 = jnp.float32
B16 = jnp.bfloat16
ANYWHERE = pl.BlockSpec(memory_space=pl.ANY)
IN_VMEM = pl.BlockSpec(memory_space=pltpu.VMEM)
MIB = 1 << 20

CYCLES = (
    (0, 1, 3, 2, 6, 7, 5, 9, 11, 10, 14, 15, 13, 12, 8, 4),
    (0, 1, 5, 4, 6, 10, 8, 9, 13, 12, 14, 15, 11, 7, 3, 2),
    (0, 2, 6, 7, 3, 1, 5, 9, 13, 15, 11, 10, 14, 12, 8, 4),
)


def chip_cycle(count, which):
    return CYCLES[which] if count == 16 else tuple(range(count))


def dp_cycle(count):
    return tuple(range(0, count, 2)) + tuple(range(count - 1 - count % 2, 0, -2))


def lookup(table, index):
    out = jnp.int32(table[0])
    for k in range(1, len(table)):
        out = jnp.where(index == k, table[k], out)
    return out


class Ring:
    def __init__(self, D, V, which):
        self.D, self.V = D, V
        d, v = lax.axis_index("dp"), lax.axis_index("vocab")
        self.core, self.v = lax.rem(v, 2), v
        self.over_dp = which == "dp"
        self.n = D if self.over_dp else D * V // 2
        self.table = dp_cycle(D) if self.over_dp else chip_cycle(self.n, which)
        self.me = d if self.over_dp else d * (V // 2) + v // 2
        inverse = tuple(self.table.index(k) for k in range(self.n))
        self.pos = lookup(inverse, self.me)

    def at(self, ahead):
        return lookup(self.table, lax.rem(self.pos + ahead + self.n, self.n))

    def device(self, place):
        if self.over_dp:
            return (place, self.v)
        half = self.V // 2
        return (place // half, lax.rem(place, half) * 2 + self.core)

    def hops(self, parity):
        more, less = self.n // 2, self.n - 1 - self.n // 2
        return (more, less) if parity == 0 else (less, more)


def sibling():
    v = lax.axis_index("vocab")
    return (lax.axis_index("dp"), v + 1 - 2 * lax.rem(v, 2))


def greet(devices):
    barrier = pltpu.get_barrier_semaphore()
    for device in devices:
        pl.semaphore_signal(barrier, inc=1, device_id=device, device_id_type=MESH)
    pl.semaphore_wait(barrier, len(devices))


def on_condition(condition, body):
    if condition is True:
        body()
    elif condition is not False:
        pl.when(condition)(body)


class Gather:
    def __init__(self, D, V, spec, ins, outs, sems, staggered=False):
        self.spec, self.ins, self.outs = spec, ins, outs
        self.ssem, self.rsem, self.xssem, self.xrsem, self.lsem = sems
        rings = {w: Ring(D, V, w) for w in dict.fromkeys(p[3] for p in spec)}
        self.core = lax.rem(lax.axis_index("vocab"), 2)
        self.sib = sibling()
        self.nexts = {w: (r.at(1), r.at(-1)) for w, r in rings.items()}
        self.neighbours = [r.device(place) for w, r in rings.items() for place in self.nexts[w]]
        if any(p[3] != "dp" for p in spec):
            self.neighbours.append(self.sib)
        self.streams = []
        for number, piece in enumerate(spec):
            ring = rings[piece[3]]
            for turn, hops in zip((0, 1), ring.hops(piece[4])):
                self.streams.append((piece, ring, turn, hops, number))
        self.longest = max(s[3] for s in self.streams)
        most = {w: max(r.hops(0)) for w, r in rings.items()}
        self.every = {w: max(1, self.longest // max(m, 1)) for w, m in most.items()}
        self.groups = len(ins) if staggered else 1
        self.units = self.longest * self.groups

    def dst(self, piece, slot):
        which, k, lead, _, _ = piece
        return self.outs[which].at[k, slot] if lead else self.outs[which].at[slot, k]

    def slot_of(self, ring, place):
        return place if ring.over_dp else place * 2 + self.core

    def origin(self, stream, s):
        _, ring, turn, _, _ = stream
        return self.slot_of(ring, ring.at(-s) if turn == 0 else ring.at(s))

    def remote(self, i, s, src, slot):
        piece, ring, turn, _, _ = self.streams[i]
        return pltpu.make_async_remote_copy(
            src_ref=src,
            dst_ref=self.dst(piece, slot),
            send_sem=self.ssem.at[s, i],
            recv_sem=self.rsem.at[s, i],
            device_id=ring.device(self.nexts[piece[3]][turn]),
            device_id_type=MESH,
        )

    def across(self, i, s, src, slot):
        return pltpu.make_async_remote_copy(
            src_ref=src,
            dst_ref=self.dst(self.streams[i][0], slot),
            send_sem=self.xssem.at[s, i],
            recv_sem=self.xrsem.at[s, i],
            device_id=self.sib,
            device_id_type=MESH,
        )

    def own(self, i):
        piece, ring, _, _, _ = self.streams[i]
        return self.ins[piece[0]].at[piece[1]], self.slot_of(ring, ring.me)

    def begin(self, group=None):
        wanted = [i for i, stream in enumerate(self.streams) if group in (None, stream[0][0])]
        for i in wanted:
            self.remote(i, 0, *self.own(i)).start()
        for i in wanted:
            stream = self.streams[i]
            if stream[2] == 0:
                src, slot = self.own(i)
                pltpu.make_async_copy(src, self.dst(stream[0], slot), self.lsem.at[stream[4]]).start()
                if not stream[1].over_dp:
                    self.across(i, 0, src, slot).start()

    def within(self, s, hops):
        return True if hops == self.longest else s <= hops

    def serve(self, unit):
        step = unit // self.groups + 1
        for i, stream in enumerate(self.streams):
            every = self.every[stream[0][3]]
            s = step // every

            def take(i=i, stream=stream, s=s):
                slot = self.origin(stream, s)
                block = self.dst(stream[0], slot)
                self.remote(i, s - 1, block, slot).wait_recv()
                pl.when(s < stream[3])(lambda: self.remote(i, s, block, slot).start())
                if not stream[1].over_dp:
                    self.across(i, s, block, slot).start()

            condition = self.within(s, stream[3])
            if every > 1:
                condition = (lax.rem(step, every) == 0) & (s <= stream[3])
            if self.groups > 1:
                turn = lax.rem(unit, self.groups) == stream[0][0]
                condition = turn if condition is True else turn & condition
            on_condition(condition, take)

    def serve_range(self, low, high):
        def body(s, carry):
            self.serve(s)
            return carry

        lax.fori_loop(low, high, body, 0)

    def finish(self):
        def last(s, carry):
            for i, stream in enumerate(self.streams):

                def end(i=i, stream=stream):
                    slot = self.origin(stream, s)
                    block = self.dst(stream[0], slot)
                    pl.when(s < stream[3])(lambda: self.remote(i, s, block, slot).wait_send())
                    if not stream[1].over_dp:

                        def crossed():
                            self.across(i, s, block, slot).wait_send()
                            theirs = slot + 1 - 2 * self.core
                            self.across(i, s, block, theirs).wait_recv()

                        on_condition(True if stream[2] == 0 else s > 0, crossed)

                on_condition(self.within(s, stream[3]), end)
            return carry

        lax.fori_loop(0, self.longest + 1, last, 0)
        for i, stream in enumerate(self.streams):
            if stream[2] == 0:
                src, slot = self.own(i)
                pltpu.make_async_copy(src, self.dst(stream[0], slot), self.lsem.at[stream[4]]).wait()


def gather_kernel(D, V, spec, count, *refs):
    gather = Gather(D, V, spec, refs[:count], refs[count : 2 * count], refs[2 * count :])
    greet(gather.neighbours)
    gather.begin()
    gather.serve_range(0, gather.units)
    gather.finish()


def gather_plan(D, V, arrays, spec):
    shapes = []
    for which, array in enumerate(arrays):
        piece = next(p for p in spec if p[0] == which)
        places = D if piece[3] == "dp" else D * V
        lead = array.shape[:1]
        shape = lead + (places,) if piece[2] else (places,) + lead
        shapes.append(jax.ShapeDtypeStruct(shape + array.shape[1:], array.dtype))
    longest = max((D if p[3] == "dp" else D * V // 2) // 2 for p in spec) + 1
    sems = pltpu.SemaphoreType.DMA((longest, 2 * len(spec)))
    return shapes, [sems] * 4 + [pltpu.SemaphoreType.DMA((len(spec),))]


def ring_gather(D, V, arrays, spec, ident):
    shapes, sems = gather_plan(D, V, arrays, spec)
    return pl.pallas_call(
        functools.partial(gather_kernel, D, V, spec, len(arrays)),
        out_shape=shapes,
        in_specs=[ANYWHERE] * len(arrays),
        out_specs=[ANYWHERE] * len(arrays),
        scratch_shapes=sems,
        compiler_params=pltpu.CompilerParams(collective_id=ident, has_side_effects=True),
    )(*arrays)


class Scatter:
    def __init__(self, pieces, sems):
        self.pieces = pieces
        self.ssem, self.rsem = sems
        self.streams = []
        for number, (ring, parity, _, _) in enumerate(pieces):
            for turn, hops in zip((0, 1), ring.hops(parity)):
                if hops:
                    self.streams.append((number, ring, turn, hops))
        self.longest = max(s[3] for s in self.streams)

    def place(self, stream, ahead):
        return stream[1].at(ahead) if stream[2] == 0 else stream[1].at(-ahead)

    def slots(self, stream):
        return self.pieces[stream[0]][3][stream[2]]

    def remote(self, i, s, src):
        stream = self.streams[i]
        return pltpu.make_async_remote_copy(
            src_ref=src,
            dst_ref=self.slots(stream).at[s],
            send_sem=self.ssem.at[s, i],
            recv_sem=self.rsem.at[s, i],
            device_id=stream[1].device(self.place(stream, 1)),
            device_id_type=MESH,
        )

    def first(self, i):
        stream = self.streams[i]
        return self.remote(i, 0, self.pieces[stream[0]][2].at[self.place(stream, stream[3])])

    def begin(self, number):
        for i, stream in enumerate(self.streams):
            if stream[0] == number:
                self.first(i).start()

    def serve(self, s):
        for i, stream in enumerate(self.streams):
            hops = stream[3]

            def take(i=i, stream=stream, hops=hops):
                block = self.slots(stream).at[s - 1]
                self.remote(i, s - 1, block).wait_recv()

                def onward():
                    mine = self.pieces[stream[0]][2].at[self.place(stream, hops - s)]
                    block[...] = (block[...].astype(F32) + mine[...].astype(F32)).astype(B16)
                    self.remote(i, s, block).start()

                pl.when(s < hops)(onward)

            on_condition(True if hops == self.longest else s <= hops, take)

    def serve_range(self, low, high):
        def body(s, carry):
            self.serve(s)
            return carry

        lax.fori_loop(low, high, body, 0)

    def total(self, number):
        ring, parity, terms, slots = self.pieces[number]
        total = terms[ring.me].astype(F32)
        for turn, hops in zip((0, 1), ring.hops(parity)):
            if hops:
                total = total + slots[turn][hops - 1].astype(F32)
        return total

    def finish(self):
        for i, stream in enumerate(self.streams):
            self.first(i).wait_send()

            def sent(s, carry, i=i, stream=stream):
                self.remote(i, s, self.slots(stream).at[s - 1]).wait_send()
                return carry

            lax.fori_loop(1, stream[3], sent, 0)


def settle_kernel(D, V, rings, *refs):
    count = len(rings)
    table_in, dx_ref, ids_ref, gains_ref = refs[:4]
    dense_in, refs = refs[4 : 4 + count], refs[4 + count :]
    table_out, totals_out = refs[:2]
    dense_out, refs = refs[2 : 2 + count], refs[2 + count :]
    dx_all, table_sums, table_slots, first, second = refs[:5]
    dense_sums, refs = refs[5 : 5 + count], refs[5 + count :]
    dense_slots, refs = refs[: 2 * count], refs[2 * count :]
    ts, tr, ds, dr, cs, cr, hs, hr, xs, xr, ns, nr = refs
    d, v = lax.axis_index("dp"), lax.axis_index("vocab")
    half = V // 2
    core, chip = lax.rem(v, 2), v // 2
    sib = sibling()
    width, length = dx_ref.shape
    chunks, _, columns, tile = table_sums.shape
    over_dp = Ring(D, V, "dp")
    chips = {w: Ring(D, V, w) for w in dict.fromkeys(rings)}
    more, less = over_dp.hops(0)
    table = Scatter(
        [
            (over_dp, c % 2, table_sums.at[c], (table_slots.at[c], table_slots.at[c, pl.ds(over_dp.hops(c % 2)[0], over_dp.hops(c % 2)[1])]))
            for c in range(chunks)
        ],
        (ts, tr),
    )
    dense = Scatter(
        [
            (chips[w], k % 2, dense_sums[k], (dense_slots[2 * k], dense_slots[2 * k + 1]))
            for k, w in enumerate(rings)
        ],
        (ds, dr),
    )
    peers = [(d, lax.rem(v + k, V)) for k in range(1, V)]
    peers += [(lax.rem(d + k, D), v) for k in range(1, D)]
    near = [r.device(r.at(k)) for r in (over_dp, *chips.values()) for k in (1, -1)]
    greet(near + peers)

    def other(k):
        return lax.rem(chip + k + half, half) * 2 + core

    def send(k):
        return pltpu.make_async_remote_copy(
            src_ref=dx_ref, dst_ref=dx_all.at[v], send_sem=hs.at[k], recv_sem=hr.at[k],
            device_id=(d, other(k)), device_id_type=MESH,
        )

    def across(k, src, slot):
        return pltpu.make_async_remote_copy(
            src_ref=src, dst_ref=dx_all.at[slot], send_sem=xs.at[k], recv_sem=xr.at[k],
            device_id=sib, device_id_type=MESH,
        )

    def crossing(k):
        return pltpu.make_async_remote_copy(
            src_ref=dense_in[k].at[:, 1 - core], dst_ref=dense_sums[k], send_sem=cs.at[k], recv_sem=cr.at[k],
            device_id=sib, device_id_type=MESH,
        )

    for k in range(1, half):
        send(k).start()
    for k in range(count):
        crossing(k).start()
    across(0, dx_ref, v).start()
    dx_all[v] = dx_ref[...]
    for k in range(count):
        crossing(k).wait_recv()

        def add(place, carry, k=k):
            total = dense_sums[k][place].astype(F32) + dense_in[k][place, core].astype(F32)
            dense_sums[k][place] = total.astype(B16)
            return carry

        lax.fori_loop(0, D * half, add, 0)
        dense.begin(k)
    for k in range(1, half):
        slot = other(-k)
        send(k).wait_recv()
        across(k, dx_all.at[slot], slot).start()
    for k in range(half):
        across(k, dx_ref, other(-k) + 1 - 2 * core).wait_recv()

    for c in range(chunks):
        grad = table_in[:, c * tile : (c + 1) * tile].astype(F32)
        lane = lax.broadcasted_iota(jnp.int32, (length, tile), 1) + c * tile
        for k in range(V):
            hit = jnp.where(lane == ids_ref[k * length : (k + 1) * length, :], 1.0, 0.0).astype(B16)
            grad = grad + mm(dx_all[k], hit)
        table_sums[c] = grad.astype(B16).reshape(D, columns, tile)
        table.begin(c)
        dense.serve_range(1 + c * dense.longest // chunks, 1 + (c + 1) * dense.longest // chunks)
    squares = jnp.zeros((1, 1), F32)
    for k in range(count):
        total = dense.total(k)
        dense_out[k][...] = total
        squares += jnp.sum(jnp.sum(total * total, 1, keepdims=True), 0, keepdims=True)
    table.serve_range(1, table.longest + 1)
    for c in range(chunks):
        total = table.total(c)
        table_out[:, c * tile : (c + 1) * tile] = total
        squares += jnp.sum(jnp.sum(total * total, 1, keepdims=True), 0, keepdims=True)
    row = lax.broadcasted_iota(jnp.int32, gains_ref.shape, 0)
    lane = lax.broadcasted_iota(jnp.int32, gains_ref.shape, 1)
    local = jnp.where((row == gains_ref.shape[0] - 1) & (lane == 0), squares, gains_ref[...])

    def tell(k):
        over, mine = (first, v) if k < V - 1 else (second, d)
        return pltpu.make_async_remote_copy(
            src_ref=over.at[mine], dst_ref=over.at[mine], send_sem=ns.at[k], recv_sem=nr.at[k],
            device_id=peers[k], device_id_type=MESH,
        )

    def stage(slots, mine, value, low, high):
        slots[mine] = value
        for k in range(low, high):
            tell(k).start()
        for k in range(low, high):
            tell(k).wait_recv()
        total = slots[0]
        for k in range(1, slots.shape[0]):
            total = total + slots[k]
        return total

    local = stage(first, v, local, 0, V - 1)
    totals_out[...] = stage(second, d, local, V - 1, V + D - 2)
    for k in range(V + D - 2):
        tell(k).wait_send()
    for k in range(1, half):
        send(k).wait_send()
    for k in range(half):
        across(k, dx_ref, v).wait_send()
    for k in range(count):
        crossing(k).wait_send()
    dense.finish()
    table.finish()


def settle(D, V, grad, dx, ids, gains, dense, rings, ident):
    width, size = grad.shape
    length = dx.shape[1]
    tile = tile_of(size, V * length)
    chunks, columns = size // tile, width // D
    n = D * V // 2
    count = len(dense)
    blocks = [a.shape[-2:] for a in dense]
    more, less = n // 2, n - 1 - n // 2
    slots = []
    for k, block in enumerate(blocks):
        slots += [pltpu.VMEM((h,) + block, B16) for h in ((more, less), (less, more))[k % 2]]
    sems = lambda *shape: pltpu.SemaphoreType.DMA(shape)
    return pl.pallas_call(
        functools.partial(settle_kernel, D, V, rings),
        out_shape=[jax.ShapeDtypeStruct((columns, size), F32), jax.ShapeDtypeStruct(gains.shape, F32)]
        + [jax.ShapeDtypeStruct(block, F32) for block in blocks],
        in_specs=[IN_VMEM] * (4 + count),
        out_specs=[IN_VMEM] * (2 + count),
        scratch_shapes=[
            pltpu.VMEM((V, width, length), B16),
            pltpu.VMEM((chunks, D, columns, tile), B16),
            pltpu.VMEM((chunks, D - 1, columns, tile), B16),
            pltpu.VMEM((V,) + gains.shape, F32),
            pltpu.VMEM((D,) + gains.shape, F32),
        ]
        + [pltpu.VMEM((n,) + block, B16) for block in blocks]
        + slots
        + [sems(D // 2, 2 * chunks)] * 2
        + [sems(n // 2, 2 * count)] * 2
        + [sems(count)] * 2
        + [sems(V // 2)] * 4
        + [sems(V + D - 2)] * 2,
        compiler_params=pltpu.CompilerParams(
            collective_id=ident, has_side_effects=True, vmem_limit_bytes=62 * MIB
        ),
    )(grad, dx, ids, gains, *dense)


def tile_of(size, tokens=1):
    return next(t for t in (1280, 768, 640, 512, 256, 128) if size % t == 0 and (t * tokens <= 1280 * 2048 or t == 128))


def lane_fold(values, combine):
    out = values[:, :128]
    for k in range(1, values.shape[1] // 128):
        out = combine(out, values[:, k * 128 : (k + 1) * 128])
    return out


def running(values, top_ref, sum_ref, rows):
    old = top_ref[rows, :]
    top = jnp.maximum(old, lane_fold(values, jnp.maximum))
    fade = jnp.exp(old - top)
    expd = jnp.concatenate(
        [jnp.exp(values[:, k * 128 : (k + 1) * 128] - top) for k in range(values.shape[1] // 128)], 1
    )
    top_ref[rows, :] = top
    sum_ref[rows, :] = sum_ref[rows, :] * fade + lane_fold(expd, jnp.add)
    return expd, fade


def pack_rows(columns):
    lane = lax.broadcasted_iota(jnp.int32, (columns[0].shape[0], 128), 1)
    packed = jnp.zeros(lane.shape, F32)
    for k, column in enumerate(columns):
        packed = jnp.where(lane == k, column, packed)
    return packed.T[:8]


def study_kernel(D, V, spec, *refs):
    first_ref, mid_ref, second_ref, table_ref, given_ref, segment_ref, pos_ref, attention_ref, up_ref, down_ref, gains_ref = refs[:11]
    first_out, mid_out, second_out, hidden_ref, turned_out, rows_out = refs[11:17]
    kept, refs = refs[17:23], refs[23:]
    top_ref, sum_ref, pick_ref, dh_ref, dl_ref, slots, own_ref, bias_ref, sums, taken = refs[:10]
    hs, hr, xs, xr, es, er, fs, fr, ps, pr = refs[10:20]
    gather = Gather(D, V, spec, (first_ref, mid_ref, second_ref), (first_out, mid_out, second_out), refs[20:], True)
    d, v = lax.axis_index("dp"), lax.axis_index("vocab")
    half = V // 2
    core, chip = lax.rem(v, 2), v // 2
    length, width = own_ref.shape
    tokens, size = V * length, table_ref.shape[1]
    tile, block = tile_of(size, tokens), min(256, length)
    tiles, blocks = size // tile, tokens // block
    peers = [(d, lax.rem(v + k, V)) for k in range(1, V)]
    greet(gather.neighbours + peers)
    marks = [k * gather.units // 24 for k in range(25)]
    gather.begin(0)

    def other(k):
        return lax.rem(chip + k + half, half) * 2 + core

    def columns(t):
        return pl.ds(pl.multiple_of(t * tile, tile), tile)

    def rows_of(slot, part=0, size=length):
        return pl.ds(pl.multiple_of(slot * length + part * size, size), size)

    dh_ref[...] = jnp.zeros(dh_ref.shape, F32)

    def pick_for(k, low, high):
        slots_of = [other(k) - core + c for c in range(2)]

        def pick(t, carry):
            for slot in slots_of:
                lane = lax.broadcasted_iota(jnp.int32, (length, tile), 1)
                hit = lane == given_ref[rows_of(slot), 2:3].astype(jnp.int32) - t * tile
                hit = jnp.where(hit, 1.0, 0.0).astype(B16)
                dh_ref[rows_of(slot), :] += mm(hit, table_ref[:, columns(t)], (1, 1))
            return carry

        lax.fori_loop(low, high, pick, 0)
        if high == tiles:
            for slot in slots_of:
                dl_ref[rows_of(slot), :] = dh_ref[rows_of(slot), :].astype(B16)

    def slab(slot):
        return dl_ref.at[rows_of(slot)]

    def swap(k):
        to = other(k)
        return pltpu.make_async_remote_copy(
            src_ref=slab(to + 1 - 2 * core), dst_ref=sums.at[to // 2], send_sem=es.at[k], recv_sem=er.at[k],
            device_id=sibling(), device_id_type=MESH,
        )

    def pass_on(k):
        return pltpu.make_async_remote_copy(
            src_ref=sums.at[other(k) // 2], dst_ref=taken.at[k - 1], send_sem=fs.at[k], recv_sem=fr.at[k],
            device_id=(d, other(k)), device_id_type=MESH,
        )

    def join(k):
        swap(k).wait()
        to = other(k)
        sums[to // 2] = (sums[to // 2].astype(F32) + slab(to)[...].astype(F32)).astype(B16)

    for k in range(1, half):
        pick_for(k, 0, tiles)
        swap(k).start()
    gather.begin(1)
    gather.serve_range(marks[0], marks[1])
    for k in range(1, half):
        join(k)
        pass_on(k).start()
    pick_for(0, 0, tiles // 2)
    gather.begin(2)
    pick_for(0, tiles // 2, tiles)
    swap(0).start()
    gather.serve_range(marks[1], marks[3])
    join(0)
    x = sums[chip].astype(F32)
    for k in range(1, half):
        pass_on(k).wait_recv()
        x = x + taken[k - 1].astype(F32)
    place_of = bias_of(segment_ref, bias_ref)
    lane = lax.broadcasted_iota(jnp.int32, (length, pos_ref.shape[0]), 1)
    x = x + mm(jnp.where(lane == place_of, 1.0, 0.0).astype(B16), pos_ref[...])
    gather.serve_range(marks[3], marks[4])
    between = lambda: gather.serve_range(marks[4], marks[6])
    learn(x, attention_ref, up_ref, down_ref, gains_ref, bias_ref, own_ref, kept, between)
    gather.serve_range(marks[6], marks[7])

    def place(slot):
        return hidden_ref.at[pl.ds(pl.multiple_of(slot * length, length), length)]

    def send(k):
        return pltpu.make_async_remote_copy(
            src_ref=own_ref, dst_ref=place(v), send_sem=hs.at[k], recv_sem=hr.at[k],
            device_id=(d, other(k)), device_id_type=MESH,
        )

    def across(k, src, slot):
        return pltpu.make_async_remote_copy(
            src_ref=src, dst_ref=place(slot), send_sem=xs.at[k], recv_sem=xr.at[k],
            device_id=sibling(), device_id_type=MESH,
        )

    for k in range(1, half):
        send(k).start()
    across(0, own_ref, v).start()
    place(v)[...] = own_ref[...]
    top_ref[...] = jnp.full(top_ref.shape, -jnp.inf, F32)
    sum_ref[...] = jnp.zeros(sum_ref.shape, F32)
    pick_ref[...] = jnp.zeros(pick_ref.shape, F32)
    across(0, own_ref, v + 1 - 2 * core).wait_recv()

    def due(t, parts, low, high):
        return low + t * (high - low) // parts

    def pass_one(u, carry):
        near = lax.rem(chip + u // tiles, half) * 2
        t = lax.rem(u, tiles)
        for slot in (near, near + 1):
            for k in range(length // block):
                rows = rows_of(slot, k, block)
                logits = mm(hidden_ref[rows, :], table_ref[:, columns(t)])
                running(logits, top_ref, sum_ref, rows)
                lane = lax.broadcasted_iota(jnp.int32, logits.shape, 1)
                hit = lane == given_ref[rows, 1:2].astype(jnp.int32) - t * tile
                pick_ref[rows, :] += lane_fold(jnp.where(hit, logits, 0.0), jnp.add)
        parts = half * tiles
        gather.serve_range(due(u, parts, marks[7], marks[19]), due(u + 1, parts, marks[7], marks[19]))
        return carry

    lax.fori_loop(0, tiles, pass_one, 0)
    for k in range(1, half):
        slot = other(-k)
        send(k).wait_recv()
        across(k, place(slot), slot).start()
    for k in range(1, half):
        across(k, place(other(-k)), other(-k) + 1 - 2 * core).wait_recv()
    lax.fori_loop(tiles, half * tiles, pass_one, 0)
    top = jnp.max(top_ref[...], 1, keepdims=True)
    total = jnp.sum(sum_ref[...] * jnp.exp(top_ref[...] - top), 1, keepdims=True)
    picked = jnp.sum(pick_ref[...], 1, keepdims=True)
    slots[v] = pack_rows([top, total, picked])

    def tell(k):
        return pltpu.make_async_remote_copy(
            src_ref=slots.at[v], dst_ref=slots.at[v], send_sem=ps.at[k], recv_sem=pr.at[k],
            device_id=peers[k], device_id_type=MESH,
        )

    for k in range(V - 1):
        tell(k).start()
    for q in range(tokens // length):
        rows = slice(q * length, (q + 1) * length)
        turned_out[:, rows] = hidden_ref[rows, :].T
    for k in range(V - 1):
        tell(k).wait_recv()
    top = slots[0, 0:1, :]
    for k in range(1, V):
        top = jnp.maximum(top, slots[k, 0:1, :])
    total, picked = jnp.zeros(top.shape, F32), jnp.zeros(top.shape, F32)
    for k in range(V):
        total = total + slots[k, 1:2, :] * jnp.exp(slots[k, 0:1, :] - top)
        picked = picked + slots[k, 2:3, :]
    rows_out[...] = jnp.broadcast_to(top + jnp.log(total), rows_out.shape)
    rows_out[1:2, :] = picked
    gather.serve_range(marks[19], marks[24])
    for k in range(1, half):
        pass_on(k).wait_send()
        send(k).wait_send()
    for k in range(half):
        across(k, place(other(-k)), other(-k)).wait_send()
    for k in range(V - 1):
        tell(k).wait_send()
    gather.finish()


def study(D, V, layers, table, given, segment, pos, attention, up, down, gains, ident):
    spec = tuple((q, r, True, r, (q + r) % 2) for r in range(3) for q in range(3))
    shapes, sems = gather_plan(D, V, layers, spec)
    length, width = segment.shape[1], gains.shape[1]
    tokens, size = V * length, table.shape[1]
    tile = tile_of(size, tokens)
    halves, singles = pltpu.SemaphoreType.DMA((V // 2,)), pltpu.SemaphoreType.DMA((V,))
    column = pltpu.VMEM((tokens, 128), F32)
    square, half = jax.ShapeDtypeStruct((length, width), F32), jax.ShapeDtypeStruct((length, width), B16)
    return pl.pallas_call(
        functools.partial(study_kernel, D, V, spec),
        out_shape=shapes
        + [
            jax.ShapeDtypeStruct((tokens, width), B16),
            jax.ShapeDtypeStruct((width, tokens), B16),
            jax.ShapeDtypeStruct((8, tokens), F32),
            square, square, square,
            jax.ShapeDtypeStruct((length, 128), F32),
            jax.ShapeDtypeStruct((length, 3 * width), B16),
            half,
        ],
        in_specs=[ANYWHERE] * 3 + [IN_VMEM] * 8,
        out_specs=[ANYWHERE] * 3 + [IN_VMEM] * 9,
        scratch_shapes=[column] * 3
        + [
            pltpu.VMEM((tokens, width), F32),
            pltpu.VMEM((tokens, width), B16),
            pltpu.VMEM((V, 8, tokens), F32),
            pltpu.VMEM((length, width), B16),
            pltpu.VMEM((length, length), F32),
            pltpu.VMEM((V // 2, length, width), B16),
            pltpu.VMEM((max(V // 2 - 1, 1), length, width), B16),
        ]
        + [halves] * 8
        + [singles] * 2
        + sems,
        compiler_params=pltpu.CompilerParams(
            collective_id=ident, has_side_effects=True, vmem_limit_bytes=63 * MIB
        ),
    )(*layers, table, given, segment, pos, attention, up, down, gains)


def share_rows(V, slots, values, send, recv):
    d, v = lax.axis_index("dp"), lax.axis_index("vocab")

    def tell(k):
        return pltpu.make_async_remote_copy(
            src_ref=slots.at[v], dst_ref=slots.at[v], send_sem=send.at[k], recv_sem=recv.at[k],
            device_id=(d, lax.rem(v + k + 1, V)), device_id_type=MESH,
        )

    slots[v] = values
    for k in range(V - 1):
        tell(k).start()
    for k in range(V - 1):
        tell(k).wait()


def teacher_stats_kernel(
    V, group_ref, own_ref, table_ref, out_ref, rows_ref,
    hidden_ref, top_ref, sum_ref, cross_ref, slots, hs, hr, xs, xr, ps, pr,
):
    step = pl.program_id(0)
    half = V // 2
    tiles = pl.num_programs(0) // half
    d, v = lax.axis_index("dp"), lax.axis_index("vocab")
    core, chip = lax.rem(v, 2), v // 2
    length = own_ref.shape[0]
    block = min(256, length)

    def other(k):
        return lax.rem(chip + k + half, half) * 2 + core

    def send(k):
        return pltpu.make_async_remote_copy(
            src_ref=own_ref, dst_ref=hidden_ref.at[v], send_sem=hs.at[k], recv_sem=hr.at[k],
            device_id=(d, other(k)), device_id_type=MESH,
        )

    def across(k, src, slot):
        return pltpu.make_async_remote_copy(
            src_ref=src, dst_ref=hidden_ref.at[slot], send_sem=xs.at[k], recv_sem=xr.at[k],
            device_id=sibling(), device_id_type=MESH,
        )

    @pl.when(step == 0)
    def _():
        greet([(d, lax.rem(v + k, V)) for k in range(1, V)])
        for k in range(1, half):
            send(k).start()
        across(0, own_ref, v).start()
        hidden_ref[v] = own_ref[...]
        top_ref[...] = jnp.full(top_ref.shape, -jnp.inf, F32)
        sum_ref[...] = jnp.zeros(sum_ref.shape, F32)
        cross_ref[...] = jnp.zeros(cross_ref.shape, F32)
        across(0, own_ref, v + 1 - 2 * core).wait_recv()

    for part in range(1, half):
        k = half - part

        @pl.when(step == part * tiles)
        def _(k=k):
            slot = other(-k)
            send(k).wait_recv()
            across(k, hidden_ref.at[slot], slot).start()
            across(k, hidden_ref.at[slot], slot + 1 - 2 * core).wait_recv()

    for c in range(2):
        slot = lax.rem(chip + step // tiles, half) * 2 + c
        table = table_ref[group_ref[slot]]
        for k in range(length // block):
            inside = slice(k * block, (k + 1) * block)
            rows = pl.ds(pl.multiple_of(slot * length + k * block, block), block)
            rounded = mm(hidden_ref[slot, inside, :], table).astype(B16)
            out_ref[c, inside, :] = rounded
            values = rounded.astype(F32)
            expd, fade = running(values, top_ref, sum_ref, rows)
            cross_ref[rows, :] = cross_ref[rows, :] * fade + lane_fold(expd * values, jnp.add)

    @pl.when(step == pl.num_programs(0) - 1)
    def _():
        top = jnp.max(top_ref[...], 1, keepdims=True)
        scale = jnp.exp(top_ref[...] - top)
        total = jnp.sum(sum_ref[...] * scale, 1, keepdims=True)
        cross = jnp.sum(cross_ref[...] * scale, 1, keepdims=True)
        share_rows(V, slots, pack_rows([top, total, cross]), ps, pr)
        top = slots[0, 0:1, :]
        for k in range(1, V):
            top = jnp.maximum(top, slots[k, 0:1, :])
        total, cross = jnp.zeros(top.shape, F32), jnp.zeros(top.shape, F32)
        for k in range(V):
            scale = jnp.exp(slots[k, 0:1, :] - top)
            total = total + slots[k, 1:2, :] * scale
            cross = cross + slots[k, 2:3, :] * scale
        rows_ref[...] = jnp.broadcast_to(top + jnp.log(total), rows_ref.shape)
        rows_ref[1:2, :] = cross / total
        for k in range(1, half):
            send(k).wait_send()
        for k in range(half):
            across(k, own_ref, v).wait_send()


def teacher_stats(V, groups, own, tables, ident):
    length, width = own.shape
    kinds, _, size = tables.shape
    tokens = V * length
    tile = tile_of(size, tokens)
    tiles = size // tile
    halves = pltpu.SemaphoreType.DMA((V // 2,))
    singles = pltpu.SemaphoreType.DMA((V,))
    return pl.pallas_call(
        functools.partial(teacher_stats_kernel, V),
        grid=(V // 2 * tiles,),
        in_specs=[
            pl.BlockSpec(memory_space=pltpu.SMEM),
            pl.BlockSpec((length, width), lambda i: (0, 0)),
            pl.BlockSpec((kinds, width, tile), lambda i: (0, 0, i % tiles)),
        ],
        out_specs=[
            pl.BlockSpec((2, length, tile), lambda i: (i // tiles, 0, i % tiles)),
            pl.BlockSpec((8, tokens), lambda i: (0, 0)),
        ],
        out_shape=[
            jax.ShapeDtypeStruct((V, length, size), B16),
            jax.ShapeDtypeStruct((8, tokens), F32),
        ],
        scratch_shapes=[pltpu.VMEM((V, length, width), B16)]
        + [pltpu.VMEM((tokens, 128), F32)] * 3
        + [pltpu.VMEM((V, 8, tokens), F32)]
        + [halves] * 4
        + [singles] * 2,
        compiler_params=pltpu.CompilerParams(
            collective_id=ident, has_side_effects=True, vmem_limit_bytes=60 * MIB
        ),
    )(groups, own, tables)


def head_grad_kernel(
    V, teacher_ref, hidden_ref, turned_ref, table_ref, given_ref, dtwo_ref, grad_ref, rows_ref,
    dl_ref, sum_ref, cross_ref, dh_ref, sums, taken, es, er, fs, fr,
):
    step = pl.program_id(0)
    tile = table_ref.shape[1]
    half = V // 2
    d, v = lax.axis_index("dp"), lax.axis_index("vocab")
    core, chip = lax.rem(v, 2), v // 2

    def other(k):
        return lax.rem(chip + k + half, half) * 2 + core
    count, length = teacher_ref.shape[:2]
    block = min(256, length)

    @pl.when(step == 0)
    def _():
        greet([(d, other(k)) for k in range(1, half)] + [sibling()])
        sum_ref[...] = jnp.zeros(sum_ref.shape, F32)
        cross_ref[...] = jnp.zeros(cross_ref.shape, F32)

    for row in range(count):
        near = lax.rem(row // 2 - chip + half, half) * 2 + row % 2
        for k in range(length // block):
            inside = slice(k * block, (k + 1) * block)
            rows = slice(row * length + k * block, row * length + (k + 1) * block)
            logits = mm(hidden_ref[rows, :], table_ref[...])
            weight = given_ref[rows, 0:1]
            target = jnp.exp(teacher_ref[near, inside, :].astype(F32) - given_ref[rows, 3:4])
            soft = jnp.exp(logits - given_ref[rows, 2:3])
            cross_ref[rows, :] += lane_fold(target * logits, jnp.add)
            lane = lax.broadcasted_iota(jnp.int32, logits.shape, 1)
            hit = lane == given_ref[rows, 1:2].astype(jnp.int32) - step * tile
            both = soft * ((1.0 + MIX_ALPHA) * weight) - target * (MIX_ALPHA * weight)
            dl_ref[rows, :] = jnp.where(hit, both - weight, both).astype(B16)
        rows = slice(row * length, (row + 1) * length)
        sum_ref[rows, :] += mm(dl_ref[rows, :], table_ref[...], (1, 1))
    grad_ref[...] = mm(turned_ref[...], dl_ref[...]).astype(B16)

    @pl.when(step == pl.num_programs(0) - 1)
    def _():
        dh_ref[...] = sum_ref[...].astype(B16)

        def slab(slot):
            return dh_ref.at[pl.ds(pl.multiple_of(slot * length, length), length)]

        def swap(k):
            to = other(k)
            return pltpu.make_async_remote_copy(
                src_ref=slab(to + 1 - 2 * core), dst_ref=sums.at[to // 2], send_sem=es.at[k], recv_sem=er.at[k],
                device_id=sibling(), device_id_type=MESH,
            )

        def pass_on(k):
            return pltpu.make_async_remote_copy(
                src_ref=sums.at[other(k) // 2], dst_ref=taken.at[k - 1], send_sem=fs.at[k], recv_sem=fr.at[k],
                device_id=(d, other(k)), device_id_type=MESH,
            )

        order = [*range(1, half), 0]
        for k in order:
            swap(k).start()
        for k in order:
            swap(k).wait()
            to = other(k)
            sums[to // 2] = (sums[to // 2].astype(F32) + slab(to)[...].astype(F32)).astype(B16)
            if k:
                pass_on(k).start()
        rows_ref[...] = pack_rows([jnp.sum(cross_ref[...], 1, keepdims=True)])
        total = sums[chip].astype(F32)
        for k in range(1, half):
            pass_on(k).wait_recv()
            total = total + taken[k - 1].astype(F32)
        dtwo_ref[...] = total
        for k in range(1, half):
            pass_on(k).wait_send()


def head_grad(V, teacher, hidden, turned, table, given, ident):
    count, length, size = teacher.shape
    width, tokens = turned.shape
    tile = tile_of(size, tokens)
    whole = lambda *shape: pl.BlockSpec(shape, lambda j: (0, 0))
    striped = pl.BlockSpec((width, tile), lambda j: (0, j))
    return pl.pallas_call(
        functools.partial(head_grad_kernel, V),
        grid=(size // tile,),
        out_shape=[
            jax.ShapeDtypeStruct((length, width), F32),
            jax.ShapeDtypeStruct((width, size), B16),
            jax.ShapeDtypeStruct((8, tokens), F32),
        ],
        in_specs=[
            pl.BlockSpec((count, length, tile), lambda j: (0, 0, j)),
            whole(tokens, width), whole(width, tokens), striped, whole(tokens, 4),
        ],
        out_specs=[whole(length, width), striped, whole(8, tokens)],
        scratch_shapes=[
            pltpu.VMEM((tokens, tile), B16),
            pltpu.VMEM((tokens, width), F32),
            pltpu.VMEM((tokens, 128), F32),
            pltpu.VMEM((tokens, width), B16),
            pltpu.VMEM((V // 2, length, width), B16),
            pltpu.VMEM((max(V // 2 - 1, 1), length, width), B16),
        ]
        + [pltpu.SemaphoreType.DMA((V // 2,))] * 4,
        compiler_params=pltpu.CompilerParams(
            collective_id=ident, has_side_effects=True, vmem_limit_bytes=62 * MIB
        ),
    )(teacher, hidden, turned, table, given)


def mm(a, b, over=(1, 0)):
    return lax.dot_general(a, b, (((over[0],), (over[1],)), ((), ())), preferred_element_type=F32)


def norm_rows(values, gain, shift):
    center = values - jnp.mean(values, -1, keepdims=True)
    scaler = lax.rsqrt(jnp.mean(center * center, -1, keepdims=True) + NORM_EPS)
    normed = center * scaler
    return (normed * gain + shift, normed, scaler)


def norm_back(grad, normed, scaler, gain):
    scaled = grad * gain
    inward = scaler * (
        scaled
        - jnp.mean(scaled, -1, keepdims=True)
        - normed * jnp.mean(scaled * normed, -1, keepdims=True)
    )
    return (inward, jnp.sum(grad * normed, 0, keepdims=True), jnp.sum(grad, 0, keepdims=True))


def gelu_both(values):
    square = values * values
    tangent = jnp.tanh(GELU_C * values * (1.0 + 0.044715 * square))
    half = 0.5 * (1.0 + tangent)
    slope = half + 0.5 * values * (1.0 - tangent * tangent) * (GELU_C * (1.0 + 3.0 * 0.044715 * square))
    return values * half, slope


def bias_of(segment_ref, bias_ref):
    length = segment_ref.shape[1]
    row = segment_ref[...]
    column = jnp.broadcast_to(row, (128, length)).T[:, :1]
    bias_ref[...] = jnp.where(column == row, 0.0, -1e30)
    place = lax.broadcasted_iota(jnp.int32, (length, 1), 0)
    for code in range(SEGS):
        start = jnp.sum((row < code).astype(jnp.int32), 1, keepdims=True)
        place = place - jnp.where(column == code, start, 0)
    return place


def softmax(queries, keys, bias):
    scores = mm(queries, keys, (1, 1)) * 0.125 + bias
    expd = jnp.exp(scores - jnp.max(scores, -1, keepdims=True))
    return expd / jnp.sum(expd, -1, keepdims=True)


def pair_of(ref, part, pair, width):
    return ref[:, pl.ds(pl.multiple_of(part * width + pair * 128, 128), 128)]


def layer_forward(x, weights, gains_ref, bias_ref, packed_ref, context_ref, between=lambda: None):
    qkv_ref, out_ref, up_ref, down_ref = weights
    length, width = x.shape
    gain = lambda k: gains_ref[k : k + 1, :]
    h_zero, normed_a, scaler_a = norm_rows(x, gain(0), gain(1))
    packed_ref[...] = mm(h_zero.astype(B16), qkv_ref[...]).astype(B16)
    low = lax.broadcasted_iota(jnp.int32, (length, 128), 1) < 64

    def heads(pair, carry):
        queries, keys, values = (pair_of(packed_ref, part, pair, width) for part in range(3))
        none = jnp.zeros_like(queries)
        parts = []
        for picked in (jnp.where(low, queries, none), jnp.where(low, none, queries)):
            parts.append(mm(softmax(picked, keys, bias_ref[...]).astype(B16), values))
        context_ref[:, pl.ds(pl.multiple_of(pair * 128, 128), 128)] = jnp.where(low, *parts).astype(B16)
        return carry

    lax.fori_loop(0, width // 128, heads, 0)
    between()
    h_one, normed_b, scaler_b = norm_rows(h_zero + mm(context_ref[...], out_ref[...]), gain(2), gain(3))
    one_b = h_one.astype(B16)
    total = h_one
    chunk = 512
    for c in range(up_ref.shape[1] // chunk):
        part = slice(c * chunk, (c + 1) * chunk)
        active = gelu_both(mm(one_b, up_ref[:, part]))[0].astype(B16)
        total = total + mm(active, down_ref[part, :])
    h_two, normed_c, scaler_c = norm_rows(total, gain(4), gain(5))
    return h_two, (normed_a, normed_b, normed_c), (scaler_a, scaler_b, scaler_c)


def teach_kernel(group_ref, x_ref, segment_ref, first_ref, mid_ref, second_ref, gains_ref, top_ref, bias_ref, packed_ref, context_ref):
    width = x_ref.shape[2]
    bias_of(segment_ref, bias_ref)
    first, second = first_ref.at[0], second_ref.at[0]
    weights = (first.at[:, : 3 * width], first.at[:, 3 * width :], mid_ref.at[0], second)
    h_two, _, _ = layer_forward(
        x_ref[0].astype(F32), weights, gains_ref.at[0], bias_ref, packed_ref, context_ref
    )
    top_ref[...] = h_two.astype(B16)


def teach(group, x, segment, first, mid, second, gains):
    _, length, width = x.shape
    chosen = lambda shape: pl.BlockSpec((1,) + shape[1:], lambda i, g: (g[0], 0, 0))
    return pl.pallas_call(
        teach_kernel,
        grid_spec=pltpu.PrefetchScalarGridSpec(
            num_scalar_prefetch=1,
            grid=(1,),
            in_specs=[
                pl.BlockSpec((1, length, width), lambda i, g: (0, 0, 0)),
                pl.BlockSpec((1, length), lambda i, g: (0, 0)),
                chosen(first.shape),
                chosen(mid.shape),
                chosen(second.shape),
                chosen(gains.shape),
            ],
            out_specs=pl.BlockSpec((length, width), lambda i, g: (0, 0)),
            scratch_shapes=[
                pltpu.VMEM((length, length), F32),
                pltpu.VMEM((length, 3 * width), B16),
                pltpu.VMEM((length, width), B16),
            ],
        ),
        out_shape=jax.ShapeDtypeStruct((length, width), B16),
        compiler_params=pltpu.CompilerParams(vmem_limit_bytes=60 * MIB),
    )(group, x, segment, first, mid, second, gains)


def learn(x, attention_ref, up_ref, down_ref, gains_ref, bias_ref, own_ref, kept, between):
    length, width = x.shape
    weights = (attention_ref.at[:, : 3 * width], attention_ref.at[:, 3 * width :], up_ref, down_ref)
    h_two, normed, scalers = layer_forward(x, weights, gains_ref, bias_ref, kept[4], kept[5], between)
    own_ref[...] = h_two.astype(B16)
    for ref, value in zip(kept, normed):
        ref[...] = value
    lane = lax.broadcasted_iota(jnp.int32, (length, 128), 1)
    kept[3][...] = jnp.where(lane == 0, scalers[0], jnp.where(lane == 1, scalers[1], scalers[2]))


def back_kernel(
    dtwo_ref, segment_ref, attention_ref, up_ref, down_ref, gains_ref,
    na_ref, nb_ref, nc_ref, scalers_ref, packed_ref, context_ref,
    dx_ref, dattention_ref, dup_ref, ddown_ref, dpos_ref, dgains_ref, bias_ref, dpacked_ref, dcontext_ref,
):
    length, width = dtwo_ref.shape
    gain = lambda k: gains_ref[k : k + 1, :]
    place = bias_of(segment_ref, bias_ref)
    dz_two, gain_c, shift_c = norm_back(dtwo_ref[...], nc_ref[...], scalers_ref[:, 2:3], gain(4))
    dbranch = dz_two.astype(B16)
    one_b = (nb_ref[...] * gain(2) + gain(3)).astype(B16)
    dh_one = dz_two
    chunk = 512
    for c in range(up_ref.shape[1] // chunk):
        part = slice(c * chunk, (c + 1) * chunk)
        active, slope = gelu_both(mm(one_b, up_ref[:, part]))
        ddown_ref[part, :] = mm(active.astype(B16), dbranch, (0, 0)).astype(B16)
        dinner = (mm(dbranch, down_ref[part, :], (1, 1)) * slope).astype(B16)
        dup_ref[:, part] = mm(one_b, dinner, (0, 0)).astype(B16)
        dh_one = dh_one + mm(dinner, up_ref[:, part], (1, 1))
    dz_one, gain_b, shift_b = norm_back(dh_one, nb_ref[...], scalers_ref[:, 1:2], gain(2))
    dproj = dz_one.astype(B16)
    dattention_ref[:, 3 * width :] = mm(context_ref[...], dproj, (0, 0)).astype(B16)
    dcontext_ref[...] = mm(dproj, attention_ref[:, 3 * width :], (1, 1)).astype(B16)
    low = lax.broadcasted_iota(jnp.int32, (length, 128), 1) < 64

    def heads(pair, carry):
        queries, keys, values = (pair_of(packed_ref, part, pair, width) for part in range(3))
        grads = pair_of(dcontext_ref, 0, pair, width)
        none = jnp.zeros_like(queries)
        parts = []
        for first in (True, False):
            pick = lambda a: jnp.where(low, a, none) if first else jnp.where(low, none, a)
            probs = softmax(pick(queries), keys, bias_ref[...])
            dprobs = mm(pick(grads), values, (1, 1))
            inner = jnp.sum(probs * dprobs, -1, keepdims=True)
            dscore = (probs * (dprobs - inner) * 0.125).astype(B16)
            parts.append(
                (mm(dscore, keys), mm(dscore, queries, (0, 0)), mm(probs.astype(B16), grads, (0, 0)))
            )
        for part in range(3):
            columns = pl.ds(pl.multiple_of(part * width + pair * 128, 128), 128)
            dpacked_ref[:, columns] = jnp.where(low, parts[0][part], parts[1][part]).astype(B16)
        return carry

    lax.fori_loop(0, width // 128, heads, 0)
    zero_b = (na_ref[...] * gain(0) + gain(1)).astype(B16)
    dattention_ref[:, : 3 * width] = mm(zero_b, dpacked_ref[...], (0, 0)).astype(B16)
    dh_zero = dz_one + mm(dpacked_ref[...], attention_ref[:, : 3 * width], (1, 1))
    dx, gain_a, shift_a = norm_back(dh_zero, na_ref[...], scalers_ref[:, 0:1], gain(0))
    dx_b = dx.astype(B16)
    lane = lax.broadcasted_iota(jnp.int32, (length, dpos_ref.shape[0]), 1)
    onehot = jnp.where(lane == place, 1.0, 0.0).astype(B16)
    dpos_ref[...] = mm(onehot, dx_b, (0, 0)).astype(B16)
    dx_ref[...] = dx_b.T
    for k, row in enumerate((gain_a, shift_a, gain_b, shift_b, gain_c, shift_c)):
        dgains_ref[k : k + 1, :] = row


def back(dtwo, segment, pos_count, attention, up, down, gains, kept):
    length, width = dtwo.shape
    inputs = (dtwo, segment, attention, up, down, gains) + tuple(kept)
    half = lambda *shape: jax.ShapeDtypeStruct(shape, B16)
    return pl.pallas_call(
        back_kernel,
        in_specs=[IN_VMEM] * len(inputs),
        out_specs=[IN_VMEM] * 6,
        out_shape=[
            half(width, length), half(*attention.shape), half(*up.shape), half(*down.shape),
            half(pos_count, width), jax.ShapeDtypeStruct(gains.shape, F32),
        ],
        scratch_shapes=[
            pltpu.VMEM((length, length), F32),
            pltpu.VMEM((length, 3 * width), B16),
            pltpu.VMEM((length, width), B16),
        ],
        compiler_params=pltpu.CompilerParams(vmem_limit_bytes=60 * MIB),
    )(*inputs)


def adam(weight, first, second, grad, fix_one, fix_two, rate):
    first = BETA_ONE * first + (1.0 - BETA_ONE) * grad
    second = BETA_TWO * second + (1.0 - BETA_TWO) * grad * grad
    update = first / fix_one / (jnp.sqrt(second / fix_two) + ADAM_EPS)
    return (first, second, weight - rate * (update + WEIGHT_DECAY * weight))


def on_device(
    D, V,
    token_ids, segment_ids, labels, loss_mask, teacher_group, teacher_inputs, teacher_table,
    teacher_qkv, teacher_out, teacher_up, teacher_down, teacher_gains, step_count,
    embed_w, embed_m, embed_v, pos_w, pos_m, pos_v, qkv_w, qkv_m, qkv_v,
    out_w, out_m, out_v, up_w, up_m, up_v, down_w, down_m, down_v, gains_w, gains_m, gains_v,
):
    length = token_ids.shape[1]
    slice_len, columns = embed_w.shape
    width = gains_w.shape[1]
    d, v = lax.axis_index("dp"), lax.axis_index("vocab")

    turned_table = embed_w.astype(B16).T.reshape(2, columns // 2, slice_len)
    attention = jnp.concatenate([qkv_w, out_w], 1).astype(B16)[None]
    integers = jnp.concatenate(
        [token_ids, labels, loss_mask, jnp.broadcast_to(teacher_group[:, None], (1, length)),
         jnp.zeros((4, length), jnp.int32)], 0
    )[None]
    table, attention, up_t, down_t, pos_t, integers = ring_gather(
        D, V,
        [turned_table, attention, up_w.astype(B16)[None], down_w.astype(B16)[None], pos_w.astype(B16)[None], integers],
        ((0, 0, False, "dp", 0), (0, 1, False, "dp", 1), (5, 0, True, 2, 1), (1, 0, True, 0, 0), (2, 0, True, 1, 1),
         (3, 0, True, 2, 0), (4, 0, True, 1, 0)),
        1,
    )
    table = table.reshape(width, slice_len)
    attention = attention.reshape(width, -1)
    up_t, down_t, pos_t = up_t.reshape(width, -1), down_t.reshape(-1, width), pos_t.reshape(-1, width)
    integers = integers.reshape(D, V, 8, length)
    counted = jnp.maximum(jnp.sum(integers[:, :, 2].astype(F32)), 1.0)
    group_ints = lax.dynamic_index_in_dim(integers, d, 0, False)
    offset = v * slice_len
    ids_here = (group_ints[:, 0].reshape(-1, 1) - offset)
    labels_here = (group_ints[:, 1].reshape(-1, 1) - offset)
    counts = group_ints[:, 2].reshape(-1).astype(F32)
    groups = group_ints[:, 3, 0]

    weight = counts / counted
    given = jnp.concatenate([weight[:, None], labels_here.astype(F32), ids_here.astype(F32)], 1)
    layers = [jnp.concatenate([teacher_qkv, teacher_out], 2), teacher_up, teacher_down]
    first, mid, second, hidden_all, turned, told, *kept = study(
        D, V, layers, table, given, segment_ids, pos_t, attention, up_t, down_t, gains_w, 4
    )
    student_lse, picked = told[0], told[1]
    tw = teacher_gains.shape[2]
    top = teach(
        teacher_group, teacher_inputs, segment_ids, first.reshape(3, tw, -1), mid.reshape(3, tw, -1),
        second.reshape(3, -1, tw), teacher_gains,
    )

    teacher, told = teacher_stats(V, groups, top, teacher_table, 5)
    teacher_lse, tcross = told[0], told[1]
    given = jnp.stack([weight, labels_here[:, 0].astype(F32), student_lse, teacher_lse], 1)
    dtwo, grad_head, cross = head_grad(V, teacher, hidden_all, turned, table, given, 6)
    once = jnp.sum(weight * (MIX_ALPHA * (tcross - teacher_lse + student_lse) + student_lse - picked))
    loss_part = jnp.where(v == 0, once, 0.0) - MIX_ALPHA * jnp.sum(weight * cross[0])

    turned_dx, grad_attention, grad_up, grad_down, grad_pos, grad_gains = back(
        dtwo, segment_ids, pos_t.shape[0], attention, up_t, down_t, gains_w, kept
    )

    lane = lax.broadcasted_iota(jnp.int32, (2, width), 1)
    scalars = jnp.where(lane == 1, loss_part, 0.0)
    owners = lambda g: g.reshape(D * V // 2, 2, -1, g.shape[1])
    grad_embed, totals, owned_attention, owned_up, owned_down, owned_pos = settle(
        D, V, grad_head, turned_dx, ids_here, jnp.concatenate([grad_gains, scalars], 0),
        [owners(grad_attention), owners(grad_up), owners(grad_down), owners(grad_pos)], (0, 1, 2, 1), 7,
    )
    owned = (owned_pos, owned_attention[:, : 3 * width], owned_attention[:, 3 * width :], owned_up, owned_down)
    gains_grad, squares, loss = totals[:6], totals[7, 0], totals[7, 1]

    grad_norm = jnp.sqrt(squares + jnp.sum(gains_grad * gains_grad))
    factor = CLIP_NORM / jnp.maximum(grad_norm, CLIP_NORM)
    count_f = step_count.astype(F32)
    fix_one = 1.0 - jnp.power(BETA_ONE, count_f)
    fix_two = 1.0 - jnp.power(BETA_TWO, count_f)

    def update(weight, first, second, grad, rate):
        return adam(weight, first, second, grad * factor, fix_one, fix_two, rate)

    out = [loss, grad_norm]
    out += update(embed_w, embed_m, embed_v, grad_embed.T, LEARN_RATE)
    out += update(pos_w, pos_m, pos_v, owned[0], LEARN_RATE)
    out += update(qkv_w, qkv_m, qkv_v, owned[1], LEARN_RATE)
    out += update(out_w, out_m, out_v, owned[2], LEARN_RATE)
    out += update(up_w, up_m, up_v, owned[3], LEARN_RATE)
    out += update(down_w, down_m, down_v, owned[4], LEARN_RATE)
    out += update(gains_w, gains_m, gains_v, gains_grad, GAIN_RATE)
    return tuple(out)


def solution(mesh):
    rows, whole = P(("dp", "vocab"), None), P()
    split = P(None, ("dp", "vocab"), None)
    embed = P("vocab", "dp")
    return jax.shard_map(
        functools.partial(on_device, mesh.shape["dp"], mesh.shape["vocab"]),
        mesh=mesh,
        in_specs=(rows, rows, rows, rows, P(("dp", "vocab")), P(("dp", "vocab"), None, None), P(None, None, "vocab"),
                  split, split, split, split, whole, whole)
        + (embed,) * 3 + (rows,) * 15 + (whole,) * 3,
        out_specs=(whole, whole) + (embed,) * 3 + (rows,) * 15 + (whole,) * 3,
        check_vma=False,
    )
```

```python
import functools

import jax
import jax.numpy as jnp
from jax import lax
from jax.experimental import pallas as pl
from jax.experimental.pallas import tpu as pltpu
from jax.sharding import PartitionSpec as P

SEGS = 8
NORM_EPS = 1e-05
MIX_ALPHA = 0.5
CLIP_NORM = 0.005
LEARN_RATE = 0.03
GAIN_RATE = 0.4
BETA_ONE = 0.9
BETA_TWO = 0.999
ADAM_EPS = 1e-08
WEIGHT_DECAY = 0.01
GELU_C = 0.7978845608028654
MESH = pl.DeviceIdType.MESH
F32 = jnp.float32
B16 = jnp.bfloat16
ANYWHERE = pl.BlockSpec(memory_space=pl.ANY)
IN_VMEM = pl.BlockSpec(memory_space=pltpu.VMEM)
MIB = 1 << 20

CYCLES = (
    (0, 1, 3, 2, 6, 7, 5, 9, 11, 10, 14, 15, 13, 12, 8, 4),
    (0, 1, 5, 4, 6, 10, 8, 9, 13, 12, 14, 15, 11, 7, 3, 2),
    (0, 2, 6, 7, 3, 1, 5, 9, 13, 15, 11, 10, 14, 12, 8, 4),
)


def chip_cycle(count, which):
    return CYCLES[which] if count == 16 else tuple(range(count))


def dp_cycle(count):
    return tuple(range(0, count, 2)) + tuple(range(count - 1 - count % 2, 0, -2))


def lookup(table, index):
    out = jnp.int32(table[0])
    for k in range(1, len(table)):
        out = jnp.where(index == k, table[k], out)
    return out


class Ring:
    def __init__(self, D, V, which):
        self.D, self.V = D, V
        d, v = lax.axis_index("dp"), lax.axis_index("vocab")
        self.core, self.v = lax.rem(v, 2), v
        self.over_dp = which == "dp"
        self.n = D if self.over_dp else D * V // 2
        self.table = dp_cycle(D) if self.over_dp else chip_cycle(self.n, which)
        self.me = d if self.over_dp else d * (V // 2) + v // 2
        inverse = tuple(self.table.index(k) for k in range(self.n))
        self.pos = lookup(inverse, self.me)

    def at(self, ahead):
        return lookup(self.table, lax.rem(self.pos + ahead + self.n, self.n))

    def device(self, place):
        if self.over_dp:
            return (place, self.v)
        half = self.V // 2
        return (place // half, lax.rem(place, half) * 2 + self.core)

    def hops(self, parity):
        more, less = self.n // 2, self.n - 1 - self.n // 2
        return (more, less) if parity == 0 else (less, more)


def sibling():
    v = lax.axis_index("vocab")
    return (lax.axis_index("dp"), v + 1 - 2 * lax.rem(v, 2))


def greet(devices):
    barrier = pltpu.get_barrier_semaphore()
    for device in devices:
        pl.semaphore_signal(barrier, inc=1, device_id=device, device_id_type=MESH)
    pl.semaphore_wait(barrier, len(devices))


def on_condition(condition, body):
    if condition is True:
        body()
    elif condition is not False:
        pl.when(condition)(body)


class Gather:
    def __init__(self, D, V, spec, ins, outs, sems, staggered=False):
        self.spec, self.ins, self.outs = spec, ins, outs
        self.ssem, self.rsem, self.xssem, self.xrsem, self.lsem = sems
        rings = {w: Ring(D, V, w) for w in dict.fromkeys(p[3] for p in spec)}
        self.core = lax.rem(lax.axis_index("vocab"), 2)
        self.sib = sibling()
        self.nexts = {w: (r.at(1), r.at(-1)) for w, r in rings.items()}
        self.neighbours = [r.device(place) for w, r in rings.items() for place in self.nexts[w]]
        if any(p[3] != "dp" for p in spec):
            self.neighbours.append(self.sib)
        self.streams = []
        for number, piece in enumerate(spec):
            ring = rings[piece[3]]
            for turn, hops in zip((0, 1), ring.hops(piece[4])):
                self.streams.append((piece, ring, turn, hops, number))
        self.longest = max(s[3] for s in self.streams)
        most = {w: max(r.hops(0)) for w, r in rings.items()}
        self.every = {w: max(1, self.longest // max(m, 1)) for w, m in most.items()}
        self.groups = len(ins) if staggered else 1
        self.units = self.longest * self.groups

    def dst(self, piece, slot):
        which, k, lead, _, _ = piece
        return self.outs[which].at[k, slot] if lead else self.outs[which].at[slot, k]

    def slot_of(self, ring, place):
        return place if ring.over_dp else place * 2 + self.core

    def origin(self, stream, s):
        _, ring, turn, _, _ = stream
        return self.slot_of(ring, ring.at(-s) if turn == 0 else ring.at(s))

    def remote(self, i, s, src, slot):
        piece, ring, turn, _, _ = self.streams[i]
        return pltpu.make_async_remote_copy(
            src_ref=src,
            dst_ref=self.dst(piece, slot),
            send_sem=self.ssem.at[s, i],
            recv_sem=self.rsem.at[s, i],
            device_id=ring.device(self.nexts[piece[3]][turn]),
            device_id_type=MESH,
        )

    def across(self, i, s, src, slot):
        return pltpu.make_async_remote_copy(
            src_ref=src,
            dst_ref=self.dst(self.streams[i][0], slot),
            send_sem=self.xssem.at[s, i],
            recv_sem=self.xrsem.at[s, i],
            device_id=self.sib,
            device_id_type=MESH,
        )

    def own(self, i):
        piece, ring, _, _, _ = self.streams[i]
        return self.ins[piece[0]].at[piece[1]], self.slot_of(ring, ring.me)

    def begin(self, group=None):
        wanted = [i for i, stream in enumerate(self.streams) if group in (None, stream[0][0])]
        for i in wanted:
            self.remote(i, 0, *self.own(i)).start()
        for i in wanted:
            stream = self.streams[i]
            if stream[2] == 0:
                src, slot = self.own(i)
                pltpu.make_async_copy(src, self.dst(stream[0], slot), self.lsem.at[stream[4]]).start()
                if not stream[1].over_dp:
                    self.across(i, 0, src, slot).start()

    def within(self, s, hops):
        return True if hops == self.longest else s <= hops

    def serve(self, unit):
        step = unit // self.groups + 1
        for i, stream in enumerate(self.streams):
            every = self.every[stream[0][3]]
            s = step // every

            def take(i=i, stream=stream, s=s):
                slot = self.origin(stream, s)
                block = self.dst(stream[0], slot)
                self.remote(i, s - 1, block, slot).wait_recv()
                pl.when(s < stream[3])(lambda: self.remote(i, s, block, slot).start())
                if not stream[1].over_dp:
                    self.across(i, s, block, slot).start()

            condition = self.within(s, stream[3])
            if every > 1:
                condition = (lax.rem(step, every) == 0) & (s <= stream[3])
            if self.groups > 1:
                turn = lax.rem(unit, self.groups) == stream[0][0]
                condition = turn if condition is True else turn & condition
            on_condition(condition, take)

    def serve_range(self, low, high):
        def body(s, carry):
            self.serve(s)
            return carry

        lax.fori_loop(low, high, body, 0)

    def finish(self):
        def last(s, carry):
            for i, stream in enumerate(self.streams):

                def end(i=i, stream=stream):
                    slot = self.origin(stream, s)
                    block = self.dst(stream[0], slot)
                    pl.when(s < stream[3])(lambda: self.remote(i, s, block, slot).wait_send())
                    if not stream[1].over_dp:

                        def crossed():
                            self.across(i, s, block, slot).wait_send()
                            theirs = slot + 1 - 2 * self.core
                            self.across(i, s, block, theirs).wait_recv()

                        on_condition(True if stream[2] == 0 else s > 0, crossed)

                on_condition(self.within(s, stream[3]), end)
            return carry

        lax.fori_loop(0, self.longest + 1, last, 0)
        for i, stream in enumerate(self.streams):
            if stream[2] == 0:
                src, slot = self.own(i)
                pltpu.make_async_copy(src, self.dst(stream[0], slot), self.lsem.at[stream[4]]).wait()


def gather_kernel(D, V, spec, count, *refs):
    gather = Gather(D, V, spec, refs[:count], refs[count : 2 * count], refs[2 * count :])
    greet(gather.neighbours)
    gather.begin()
    gather.serve_range(0, gather.units)
    gather.finish()


def gather_plan(D, V, arrays, spec):
    shapes = []
    for which, array in enumerate(arrays):
        piece = next(p for p in spec if p[0] == which)
        places = D if piece[3] == "dp" else D * V
        lead = array.shape[:1]
        shape = lead + (places,) if piece[2] else (places,) + lead
        shapes.append(jax.ShapeDtypeStruct(shape + array.shape[1:], array.dtype))
    longest = max((D if p[3] == "dp" else D * V // 2) // 2 for p in spec) + 1
    sems = pltpu.SemaphoreType.DMA((longest, 2 * len(spec)))
    return shapes, [sems] * 4 + [pltpu.SemaphoreType.DMA((len(spec),))]


def ring_gather(D, V, arrays, spec, ident):
    shapes, sems = gather_plan(D, V, arrays, spec)
    return pl.pallas_call(
        functools.partial(gather_kernel, D, V, spec, len(arrays)),
        out_shape=shapes,
        in_specs=[ANYWHERE] * len(arrays),
        out_specs=[ANYWHERE] * len(arrays),
        scratch_shapes=sems,
        compiler_params=pltpu.CompilerParams(collective_id=ident, has_side_effects=True),
    )(*arrays)


class Scatter:
    def __init__(self, pieces, sems):
        self.pieces = pieces
        self.ssem, self.rsem = sems
        self.streams = []
        for number, (ring, parity, _, _) in enumerate(pieces):
            for turn, hops in zip((0, 1), ring.hops(parity)):
                if hops:
                    self.streams.append((number, ring, turn, hops))
        self.longest = max(s[3] for s in self.streams)

    def place(self, stream, ahead):
        return stream[1].at(ahead) if stream[2] == 0 else stream[1].at(-ahead)

    def slots(self, stream):
        return self.pieces[stream[0]][3][stream[2]]

    def remote(self, i, s, src):
        stream = self.streams[i]
        return pltpu.make_async_remote_copy(
            src_ref=src,
            dst_ref=self.slots(stream).at[s],
            send_sem=self.ssem.at[s, i],
            recv_sem=self.rsem.at[s, i],
            device_id=stream[1].device(self.place(stream, 1)),
            device_id_type=MESH,
        )

    def first(self, i):
        stream = self.streams[i]
        return self.remote(i, 0, self.pieces[stream[0]][2].at[self.place(stream, stream[3])])

    def begin(self, number):
        for i, stream in enumerate(self.streams):
            if stream[0] == number:
                self.first(i).start()

    def take(self, i, s):
        stream = self.streams[i]
        block = self.slots(stream).at[s - 1]
        self.remote(i, s - 1, block).wait_recv()

        def onward():
            mine = self.pieces[stream[0]][2].at[self.place(stream, stream[3] - s)]
            block[...] = (block[...].astype(F32) + mine[...].astype(F32)).astype(B16)
            self.remote(i, s, block).start()

        on_condition(s < stream[3], onward)

    def serve(self, s):
        for i, stream in enumerate(self.streams):
            whole = stream[3] == self.longest
            on_condition(True if whole else s <= stream[3], functools.partial(self.take, i, s))

    def serve_piece(self, number, s):
        for i, stream in enumerate(self.streams):
            if stream[0] == number and s <= stream[3]:
                self.take(i, s)

    def serve_range(self, low, high):
        def body(s, carry):
            self.serve(s)
            return carry

        lax.fori_loop(low, high, body, 0)

    def total(self, number):
        ring, parity, terms, slots = self.pieces[number]
        total = terms[ring.me].astype(F32)
        for turn, hops in zip((0, 1), ring.hops(parity)):
            if hops:
                total = total + slots[turn][hops - 1].astype(F32)
        return total

    def finish(self):
        for i, stream in enumerate(self.streams):
            self.first(i).wait_send()

            def sent(s, carry, i=i, stream=stream):
                self.remote(i, s, self.slots(stream).at[s - 1]).wait_send()
                return carry

            lax.fori_loop(1, stream[3], sent, 0)


def settle_kernel(D, V, rings, *refs):
    count = len(rings)
    dl_in, turned_ref, dx_ref, ids_ref, gains_ref = refs[:5]
    dense_in, refs = refs[5 : 5 + count], refs[5 + count :]
    table_out, totals_out = refs[:2]
    dense_out, refs = refs[2 : 2 + count], refs[2 + count :]
    dl_ref, dl_sem, dx_all, table_sums, table_slots, first, second = refs[:7]
    dense_sums, refs = refs[7 : 7 + count], refs[7 + count :]
    dense_slots, refs = refs[: 2 * count], refs[2 * count :]
    ts, tr, ds, dr, cs, cr, hs, hr, xs, xr, ns, nr = refs
    d, v = lax.axis_index("dp"), lax.axis_index("vocab")
    half = V // 2
    core, chip = lax.rem(v, 2), v // 2
    sib = sibling()
    width, length = dx_ref.shape
    chunks, _, columns, tile = table_sums.shape
    over_dp = Ring(D, V, "dp")
    chips = {w: Ring(D, V, w) for w in dict.fromkeys(rings)}
    more, less = over_dp.hops(0)
    table = Scatter(
        [
            (over_dp, c % 2, table_sums.at[c], (table_slots.at[c], table_slots.at[c, pl.ds(over_dp.hops(c % 2)[0], over_dp.hops(c % 2)[1])]))
            for c in range(chunks)
        ],
        (ts, tr),
    )
    dense = Scatter(
        [
            (chips[w], k % 2, dense_sums[k], (dense_slots[2 * k], dense_slots[2 * k + 1]))
            for k, w in enumerate(rings)
        ],
        (ds, dr),
    )
    peers = [(d, lax.rem(v + k, V)) for k in range(1, V)]
    peers += [(lax.rem(d + k, D), v) for k in range(1, D)]
    near = [r.device(r.at(k)) for r in (over_dp, *chips.values()) for k in (1, -1)]

    def load(c):
        return pltpu.make_async_copy(dl_in.at[c], dl_ref.at[c % 2], dl_sem.at[c])

    load(0).start()
    greet(near + peers)

    def other(k):
        return lax.rem(chip + k + half, half) * 2 + core

    def send(k):
        return pltpu.make_async_remote_copy(
            src_ref=dx_ref, dst_ref=dx_all.at[v], send_sem=hs.at[k], recv_sem=hr.at[k],
            device_id=(d, other(k)), device_id_type=MESH,
        )

    def across(k, src, slot):
        return pltpu.make_async_remote_copy(
            src_ref=src, dst_ref=dx_all.at[slot], send_sem=xs.at[k], recv_sem=xr.at[k],
            device_id=sib, device_id_type=MESH,
        )

    def crossing(k):
        return pltpu.make_async_remote_copy(
            src_ref=dense_in[k].at[:, 1 - core], dst_ref=dense_sums[k], send_sem=cs.at[k], recv_sem=cr.at[k],
            device_id=sib, device_id_type=MESH,
        )

    for k in range(1, half):
        send(k).start()
    for k in range(count):
        crossing(k).start()
    across(0, dx_ref, v).start()
    dx_all[v] = dx_ref[...]
    for k in range(count):
        crossing(k).wait_recv()

        def add(place, carry, k=k):
            total = dense_sums[k][place].astype(F32) + dense_in[k][place, core].astype(F32)
            dense_sums[k][place] = total.astype(B16)
            return carry

        lax.fori_loop(0, D * half, add, 0)
        dense.begin(k)
    across(0, dx_ref, v + 1 - 2 * core).wait_recv()

    def head(c):
        if c + 1 < chunks:
            load(c + 1).start()
        load(c).wait()
        return mm(turned_ref[...], dl_ref[c % 2])

    def spread(grad, c, parts):
        lane = lax.broadcasted_iota(jnp.int32, (length, tile), 1) + c * tile
        for part in parts:
            for slot in (lax.rem(chip + part, half) * 2, lax.rem(chip + part, half) * 2 + 1):
                ids = ids_ref[pl.ds(pl.multiple_of(slot * length, length), length), :]
                grad = grad + mm(dx_all[slot], jnp.where(lane == ids, 1.0, 0.0).astype(B16))
        return grad

    def store(c, grad):
        table_sums[c] = grad.astype(B16).reshape(D, columns, tile)

    early = min(2, chunks)
    for c in range(early):
        store(c, spread(head(c), c, [0]))
    for k in range(1, half):
        slot = other(-k)
        send(k).wait_recv()
        across(k, dx_all.at[slot], slot).start()
    for k in range(1, half):
        across(k, dx_ref, other(-k) + 1 - 2 * core).wait_recv()
    waves = chunks + table.longest
    for w in range(waves):
        if w < early:
            store(w, spread(table_sums[w].reshape(width, tile).astype(F32), w, range(1, half)))
        elif w < chunks:
            store(w, spread(head(w), w, range(half)))
        if w < chunks:
            table.begin(w)
        for c in range(max(0, w - table.longest), min(w, chunks)):
            table.serve_piece(c, w - c)
        dense.serve_range(1 + w * dense.longest // waves, 1 + (w + 1) * dense.longest // waves)
    squares = jnp.zeros((1, 1), F32)
    for k in range(count):
        total = dense.total(k)
        dense_out[k][...] = total
        squares += jnp.sum(jnp.sum(total * total, 1, keepdims=True), 0, keepdims=True)
    for c in range(chunks):
        total = table.total(c)
        table_out[:, c * tile : (c + 1) * tile] = total
        squares += jnp.sum(jnp.sum(total * total, 1, keepdims=True), 0, keepdims=True)
    row = lax.broadcasted_iota(jnp.int32, gains_ref.shape, 0)
    lane = lax.broadcasted_iota(jnp.int32, gains_ref.shape, 1)
    local = jnp.where((row == gains_ref.shape[0] - 1) & (lane == 0), squares, gains_ref[...])

    def tell(k):
        over, mine = (first, v) if k < V - 1 else (second, d)
        return pltpu.make_async_remote_copy(
            src_ref=over.at[mine], dst_ref=over.at[mine], send_sem=ns.at[k], recv_sem=nr.at[k],
            device_id=peers[k], device_id_type=MESH,
        )

    def stage(slots, mine, value, low, high):
        slots[mine] = value
        for k in range(low, high):
            tell(k).start()
        for k in range(low, high):
            tell(k).wait_recv()
        total = slots[0]
        for k in range(1, slots.shape[0]):
            total = total + slots[k]
        return total

    local = stage(first, v, local, 0, V - 1)
    totals_out[...] = stage(second, d, local, V - 1, V + D - 2)
    for k in range(V + D - 2):
        tell(k).wait_send()
    for k in range(1, half):
        send(k).wait_send()
    for k in range(half):
        across(k, dx_ref, v).wait_send()
    for k in range(count):
        crossing(k).wait_send()
    dense.finish()
    table.finish()


def settle(D, V, dl, turned, dx, ids, gains, dense, rings, ident):
    width, length = dx.shape
    chunks, tokens, tile = dl.shape
    size, columns = chunks * tile, width // D
    n = D * V // 2
    count = len(dense)
    blocks = [a.shape[-2:] for a in dense]
    more, less = n // 2, n - 1 - n // 2
    slots = []
    for k, block in enumerate(blocks):
        slots += [pltpu.VMEM((h,) + block, B16) for h in ((more, less), (less, more))[k % 2]]
    sems = lambda *shape: pltpu.SemaphoreType.DMA(shape)
    return pl.pallas_call(
        functools.partial(settle_kernel, D, V, rings),
        out_shape=[jax.ShapeDtypeStruct((columns, size), F32), jax.ShapeDtypeStruct(gains.shape, F32)]
        + [jax.ShapeDtypeStruct(block, F32) for block in blocks],
        in_specs=[ANYWHERE] + [IN_VMEM] * (4 + count),
        out_specs=[IN_VMEM] * (2 + count),
        scratch_shapes=[
            pltpu.VMEM((2, tokens, tile), B16),
            sems(chunks),
            pltpu.VMEM((V, width, length), B16),
            pltpu.VMEM((chunks, D, columns, tile), B16),
            pltpu.VMEM((chunks, D - 1, columns, tile), B16),
            pltpu.VMEM((V,) + gains.shape, F32),
            pltpu.VMEM((D,) + gains.shape, F32),
        ]
        + [pltpu.VMEM((n,) + block, B16) for block in blocks]
        + slots
        + [sems(D // 2, 2 * chunks)] * 2
        + [sems(n // 2, 2 * count)] * 2
        + [sems(count)] * 2
        + [sems(V // 2)] * 4
        + [sems(V + D - 2)] * 2,
        compiler_params=pltpu.CompilerParams(
            collective_id=ident, has_side_effects=True, vmem_limit_bytes=62 * MIB
        ),
    )(dl, turned, dx, ids, gains, *dense)


def tile_of(size, tokens=1):
    return next(t for t in (1280, 768, 640, 512, 256, 128) if size % t == 0 and (t * tokens <= 1280 * 2048 or t == 128))


def lane_fold(values, combine):
    out = values[:, :128]
    for k in range(1, values.shape[1] // 128):
        out = combine(out, values[:, k * 128 : (k + 1) * 128])
    return out


def running(values, top_ref, sum_ref, rows):
    old = top_ref[rows, :]
    top = jnp.maximum(old, lane_fold(values, jnp.maximum))
    fade = jnp.exp(old - top)
    expd = jnp.concatenate(
        [jnp.exp(values[:, k * 128 : (k + 1) * 128] - top) for k in range(values.shape[1] // 128)], 1
    )
    top_ref[rows, :] = top
    sum_ref[rows, :] = sum_ref[rows, :] * fade + lane_fold(expd, jnp.add)
    return expd, fade


def pack_rows(columns):
    lane = lax.broadcasted_iota(jnp.int32, (columns[0].shape[0], 128), 1)
    packed = jnp.zeros(lane.shape, F32)
    for k, column in enumerate(columns):
        packed = jnp.where(lane == k, column, packed)
    return packed.T[:8]


def study_kernel(D, V, spec, *refs):
    first_ref, mid_ref, second_ref, table_ref, given_ref, segment_ref, pos_ref, attention_ref, up_ref, down_ref, gains_ref = refs[:11]
    first_out, mid_out, second_out, hidden_ref, turned_out, rows_out = refs[11:17]
    kept, refs = refs[17:23], refs[23:]
    top_ref, sum_ref, pick_ref, dh_ref, dl_ref, slots, own_ref, bias_ref, sums, taken = refs[:10]
    hs, hr, xs, xr, es, er, fs, fr, ps, pr = refs[10:20]
    gather = Gather(D, V, spec, (first_ref, mid_ref, second_ref), (first_out, mid_out, second_out), refs[20:])
    d, v = lax.axis_index("dp"), lax.axis_index("vocab")
    half = V // 2
    core, chip = lax.rem(v, 2), v // 2
    length, width = own_ref.shape
    tokens, size = V * length, table_ref.shape[1]
    tile, block = tile_of(size, tokens), min(256, length)
    tiles, blocks = size // tile, tokens // block
    peers = [(d, lax.rem(v + k, V)) for k in range(1, V)]
    greet(gather.neighbours + peers)
    marks = [k * gather.units // 24 for k in range(25)]
    gather.begin()

    def other(k):
        return lax.rem(chip + k + half, half) * 2 + core

    def columns(t):
        return pl.ds(pl.multiple_of(t * tile, tile), tile)

    def rows_of(slot, part=0, size=length):
        return pl.ds(pl.multiple_of(slot * length + part * size, size), size)

    dh_ref[...] = jnp.zeros(dh_ref.shape, F32)

    def pick_for(k, low, high):
        slots_of = [other(k) - core + c for c in range(2)]

        def pick(t, carry):
            for slot in slots_of:
                lane = lax.broadcasted_iota(jnp.int32, (length, tile), 1)
                hit = lane == given_ref[rows_of(slot), 2:3].astype(jnp.int32) - t * tile
                hit = jnp.where(hit, 1.0, 0.0).astype(B16)
                dh_ref[rows_of(slot), :] += mm(hit, table_ref[:, columns(t)], (1, 1))
            return carry

        lax.fori_loop(low, high, pick, 0)
        if high == tiles:
            for slot in slots_of:
                dl_ref[rows_of(slot), :] = dh_ref[rows_of(slot), :].astype(B16)

    def slab(slot):
        return dl_ref.at[rows_of(slot)]

    def swap(k):
        to = other(k)
        return pltpu.make_async_remote_copy(
            src_ref=slab(to + 1 - 2 * core), dst_ref=sums.at[to // 2], send_sem=es.at[k], recv_sem=er.at[k],
            device_id=sibling(), device_id_type=MESH,
        )

    def pass_on(k):
        return pltpu.make_async_remote_copy(
            src_ref=sums.at[other(k) // 2], dst_ref=taken.at[k - 1], send_sem=fs.at[k], recv_sem=fr.at[k],
            device_id=(d, other(k)), device_id_type=MESH,
        )

    def join(k):
        swap(k).wait()
        to = other(k)
        sums[to // 2] = (sums[to // 2].astype(F32) + slab(to)[...].astype(F32)).astype(B16)

    for k in range(1, half):
        pick_for(k, 0, tiles)
        swap(k).start()
    gather.serve_range(marks[0], marks[1])
    for k in range(1, half):
        join(k)
        pass_on(k).start()
    pick_for(0, 0, tiles // 2)
    gather.serve_range(marks[1], marks[2])
    pick_for(0, tiles // 2, tiles)
    swap(0).start()
    gather.serve_range(marks[2], marks[4])
    join(0)
    x = sums[chip].astype(F32)
    for k in range(1, half):
        pass_on(k).wait_recv()
        x = x + taken[k - 1].astype(F32)
    place_of = bias_of(segment_ref, bias_ref)
    lane = lax.broadcasted_iota(jnp.int32, (length, pos_ref.shape[0]), 1)
    x = x + mm(jnp.where(lane == place_of, 1.0, 0.0).astype(B16), pos_ref[...])
    gather.serve_range(marks[4], marks[5])
    between = lambda: gather.serve_range(marks[5], marks[7])
    learn(x, attention_ref, up_ref, down_ref, gains_ref, bias_ref, own_ref, kept, between)
    gather.serve_range(marks[7], marks[8])

    def place(slot):
        return hidden_ref.at[pl.ds(pl.multiple_of(slot * length, length), length)]

    def send(k):
        return pltpu.make_async_remote_copy(
            src_ref=own_ref, dst_ref=place(v), send_sem=hs.at[k], recv_sem=hr.at[k],
            device_id=(d, other(k)), device_id_type=MESH,
        )

    def across(k, src, slot):
        return pltpu.make_async_remote_copy(
            src_ref=src, dst_ref=place(slot), send_sem=xs.at[k], recv_sem=xr.at[k],
            device_id=sibling(), device_id_type=MESH,
        )

    for k in range(1, half):
        send(k).start()
    across(0, own_ref, v).start()
    place(v)[...] = own_ref[...]
    top_ref[...] = jnp.full(top_ref.shape, -jnp.inf, F32)
    sum_ref[...] = jnp.zeros(sum_ref.shape, F32)
    pick_ref[...] = jnp.zeros(pick_ref.shape, F32)
    across(0, own_ref, v + 1 - 2 * core).wait_recv()

    def due(t, parts, low, high):
        return low + t * (high - low) // parts

    def pass_one(u, carry):
        near = lax.rem(chip + u // tiles, half) * 2
        t = lax.rem(u, tiles)
        for slot in (near, near + 1):
            for k in range(length // block):
                rows = rows_of(slot, k, block)
                logits = mm(hidden_ref[rows, :], table_ref[:, columns(t)])
                running(logits, top_ref, sum_ref, rows)
                lane = lax.broadcasted_iota(jnp.int32, logits.shape, 1)
                hit = lane == given_ref[rows, 1:2].astype(jnp.int32) - t * tile
                pick_ref[rows, :] += lane_fold(jnp.where(hit, logits, 0.0), jnp.add)
        parts = half * tiles
        gather.serve_range(due(u, parts, marks[8], marks[23]), due(u + 1, parts, marks[8], marks[23]))
        return carry

    lax.fori_loop(0, tiles, pass_one, 0)
    for k in range(1, half):
        slot = other(-k)
        send(k).wait_recv()
        across(k, place(slot), slot).start()
    for k in range(1, half):
        across(k, place(other(-k)), other(-k) + 1 - 2 * core).wait_recv()
    lax.fori_loop(tiles, half * tiles, pass_one, 0)
    top = jnp.max(top_ref[...], 1, keepdims=True)
    total = jnp.sum(sum_ref[...] * jnp.exp(top_ref[...] - top), 1, keepdims=True)
    picked = jnp.sum(pick_ref[...], 1, keepdims=True)
    slots[v] = pack_rows([top, total, picked])

    def tell(k):
        return pltpu.make_async_remote_copy(
            src_ref=slots.at[v], dst_ref=slots.at[v], send_sem=ps.at[k], recv_sem=pr.at[k],
            device_id=peers[k], device_id_type=MESH,
        )

    for k in range(V - 1):
        tell(k).start()
    for q in range(tokens // length):
        rows = slice(q * length, (q + 1) * length)
        turned_out[:, rows] = hidden_ref[rows, :].T
    for k in range(V - 1):
        tell(k).wait_recv()
    top = slots[0, 0:1, :]
    for k in range(1, V):
        top = jnp.maximum(top, slots[k, 0:1, :])
    total, picked = jnp.zeros(top.shape, F32), jnp.zeros(top.shape, F32)
    for k in range(V):
        total = total + slots[k, 1:2, :] * jnp.exp(slots[k, 0:1, :] - top)
        picked = picked + slots[k, 2:3, :]
    rows_out[...] = jnp.broadcast_to(top + jnp.log(total), rows_out.shape)
    rows_out[1:2, :] = picked
    gather.serve_range(marks[23], marks[24])
    for k in range(1, half):
        pass_on(k).wait_send()
        send(k).wait_send()
    for k in range(half):
        across(k, place(other(-k)), other(-k)).wait_send()
    for k in range(V - 1):
        tell(k).wait_send()
    gather.finish()


def study(D, V, layers, table, given, segment, pos, attention, up, down, gains, ident):
    spec = tuple((q, r, True, r, (q + r) % 2) for r in range(3) for q in range(3))
    shapes, sems = gather_plan(D, V, layers, spec)
    length, width = segment.shape[1], gains.shape[1]
    tokens, size = V * length, table.shape[1]
    tile = tile_of(size, tokens)
    halves, singles = pltpu.SemaphoreType.DMA((V // 2,)), pltpu.SemaphoreType.DMA((V,))
    column = pltpu.VMEM((tokens, 128), F32)
    square, half = jax.ShapeDtypeStruct((length, width), F32), jax.ShapeDtypeStruct((length, width), B16)
    return pl.pallas_call(
        functools.partial(study_kernel, D, V, spec),
        out_shape=shapes
        + [
            jax.ShapeDtypeStruct((tokens, width), B16),
            jax.ShapeDtypeStruct((width, tokens), B16),
            jax.ShapeDtypeStruct((8, tokens), F32),
            square, square, square,
            jax.ShapeDtypeStruct((length, 128), F32),
            jax.ShapeDtypeStruct((length, 3 * width), B16),
            half,
        ],
        in_specs=[ANYWHERE] * 3 + [IN_VMEM] * 8,
        out_specs=[ANYWHERE] * 3 + [IN_VMEM] * 9,
        scratch_shapes=[column] * 3
        + [
            pltpu.VMEM((tokens, width), F32),
            pltpu.VMEM((tokens, width), B16),
            pltpu.VMEM((V, 8, tokens), F32),
            pltpu.VMEM((length, width), B16),
            pltpu.VMEM((length, length), F32),
            pltpu.VMEM((V // 2, length, width), B16),
            pltpu.VMEM((max(V // 2 - 1, 1), length, width), B16),
        ]
        + [halves] * 8
        + [singles] * 2
        + sems,
        compiler_params=pltpu.CompilerParams(
            collective_id=ident, has_side_effects=True, vmem_limit_bytes=63 * MIB
        ),
    )(*layers, table, given, segment, pos, attention, up, down, gains)


def share_rows(V, slots, values, send, recv):
    d, v = lax.axis_index("dp"), lax.axis_index("vocab")

    def tell(k):
        return pltpu.make_async_remote_copy(
            src_ref=slots.at[v], dst_ref=slots.at[v], send_sem=send.at[k], recv_sem=recv.at[k],
            device_id=(d, lax.rem(v + k + 1, V)), device_id_type=MESH,
        )

    slots[v] = values
    for k in range(V - 1):
        tell(k).start()
    for k in range(V - 1):
        tell(k).wait()


def teacher_stats_kernel(
    V, group_ref, own_ref, table_ref, out_ref, rows_ref,
    hidden_ref, top_ref, sum_ref, cross_ref, slots, hs, hr, xs, xr, ps, pr,
):
    step = pl.program_id(0)
    half = V // 2
    tiles = pl.num_programs(0) // half
    d, v = lax.axis_index("dp"), lax.axis_index("vocab")
    core, chip = lax.rem(v, 2), v // 2
    length = own_ref.shape[0]
    block = min(256, length)

    def other(k):
        return lax.rem(chip + k + half, half) * 2 + core

    def send(k):
        return pltpu.make_async_remote_copy(
            src_ref=own_ref, dst_ref=hidden_ref.at[v], send_sem=hs.at[k], recv_sem=hr.at[k],
            device_id=(d, other(k)), device_id_type=MESH,
        )

    def across(k, src, slot):
        return pltpu.make_async_remote_copy(
            src_ref=src, dst_ref=hidden_ref.at[slot], send_sem=xs.at[k], recv_sem=xr.at[k],
            device_id=sibling(), device_id_type=MESH,
        )

    @pl.when(step == 0)
    def _():
        greet([(d, lax.rem(v + k, V)) for k in range(1, V)])
        for k in range(1, half):
            send(k).start()
        across(0, own_ref, v).start()
        hidden_ref[v] = own_ref[...]
        top_ref[...] = jnp.full(top_ref.shape, -jnp.inf, F32)
        sum_ref[...] = jnp.zeros(sum_ref.shape, F32)
        cross_ref[...] = jnp.zeros(cross_ref.shape, F32)
        across(0, own_ref, v + 1 - 2 * core).wait_recv()

    for part in range(1, half):
        k = half - part

        @pl.when(step == part * tiles)
        def _(k=k):
            slot = other(-k)
            send(k).wait_recv()
            across(k, hidden_ref.at[slot], slot).start()
            across(k, hidden_ref.at[slot], slot + 1 - 2 * core).wait_recv()

    for c in range(2):
        slot = lax.rem(chip + step // tiles, half) * 2 + c
        table = table_ref[group_ref[slot]]
        for k in range(length // block):
            inside = slice(k * block, (k + 1) * block)
            rows = pl.ds(pl.multiple_of(slot * length + k * block, block), block)
            rounded = mm(hidden_ref[slot, inside, :], table).astype(B16)
            out_ref[c, inside, :] = rounded
            values = rounded.astype(F32)
            expd, fade = running(values, top_ref, sum_ref, rows)
            cross_ref[rows, :] = cross_ref[rows, :] * fade + lane_fold(expd * values, jnp.add)

    @pl.when(step == pl.num_programs(0) - 1)
    def _():
        top = jnp.max(top_ref[...], 1, keepdims=True)
        scale = jnp.exp(top_ref[...] - top)
        total = jnp.sum(sum_ref[...] * scale, 1, keepdims=True)
        cross = jnp.sum(cross_ref[...] * scale, 1, keepdims=True)
        share_rows(V, slots, pack_rows([top, total, cross]), ps, pr)
        top = slots[0, 0:1, :]
        for k in range(1, V):
            top = jnp.maximum(top, slots[k, 0:1, :])
        total, cross = jnp.zeros(top.shape, F32), jnp.zeros(top.shape, F32)
        for k in range(V):
            scale = jnp.exp(slots[k, 0:1, :] - top)
            total = total + slots[k, 1:2, :] * scale
            cross = cross + slots[k, 2:3, :] * scale
        rows_ref[...] = jnp.broadcast_to(top + jnp.log(total), rows_ref.shape)
        rows_ref[1:2, :] = cross / total
        for k in range(1, half):
            send(k).wait_send()
        for k in range(half):
            across(k, own_ref, v).wait_send()


def teacher_stats(V, groups, own, tables, ident):
    length, width = own.shape
    kinds, _, size = tables.shape
    tokens = V * length
    tile = tile_of(size, tokens)
    tiles = size // tile
    halves = pltpu.SemaphoreType.DMA((V // 2,))
    singles = pltpu.SemaphoreType.DMA((V,))
    return pl.pallas_call(
        functools.partial(teacher_stats_kernel, V),
        grid=(V // 2 * tiles,),
        in_specs=[
            pl.BlockSpec(memory_space=pltpu.SMEM),
            pl.BlockSpec((length, width), lambda i: (0, 0)),
            pl.BlockSpec((kinds, width, tile), lambda i: (0, 0, i % tiles)),
        ],
        out_specs=[
            pl.BlockSpec((2, length, tile), lambda i: (i // tiles, 0, i % tiles)),
            pl.BlockSpec((8, tokens), lambda i: (0, 0)),
        ],
        out_shape=[
            jax.ShapeDtypeStruct((V, length, size), B16),
            jax.ShapeDtypeStruct((8, tokens), F32),
        ],
        scratch_shapes=[pltpu.VMEM((V, length, width), B16)]
        + [pltpu.VMEM((tokens, 128), F32)] * 3
        + [pltpu.VMEM((V, 8, tokens), F32)]
        + [halves] * 4
        + [singles] * 2,
        compiler_params=pltpu.CompilerParams(
            collective_id=ident, has_side_effects=True, vmem_limit_bytes=60 * MIB
        ),
    )(groups, own, tables)


def head_grad_kernel(
    V, teacher_ref, hidden_ref, table_ref, given_ref, dtwo_ref, dl_ref, rows_ref,
    sum_ref, cross_ref, dh_ref, sums, taken, es, er, fs, fr,
):
    step = pl.program_id(0)
    tile = table_ref.shape[1]
    half = V // 2
    d, v = lax.axis_index("dp"), lax.axis_index("vocab")
    core, chip = lax.rem(v, 2), v // 2

    def other(k):
        return lax.rem(chip + k + half, half) * 2 + core
    count, length = teacher_ref.shape[:2]
    block = min(256, length)

    @pl.when(step == 0)
    def _():
        greet([(d, other(k)) for k in range(1, half)] + [sibling()])
        sum_ref[...] = jnp.zeros(sum_ref.shape, F32)
        cross_ref[...] = jnp.zeros(cross_ref.shape, F32)

    for row in range(count):
        near = lax.rem(row // 2 - chip + half, half) * 2 + row % 2
        for k in range(length // block):
            inside = slice(k * block, (k + 1) * block)
            rows = slice(row * length + k * block, row * length + (k + 1) * block)
            logits = mm(hidden_ref[rows, :], table_ref[...])
            weight = given_ref[rows, 0:1]
            target = jnp.exp(teacher_ref[near, inside, :].astype(F32) - given_ref[rows, 3:4])
            soft = jnp.exp(logits - given_ref[rows, 2:3])
            cross_ref[rows, :] += lane_fold(target * logits, jnp.add)
            lane = lax.broadcasted_iota(jnp.int32, logits.shape, 1)
            hit = lane == given_ref[rows, 1:2].astype(jnp.int32) - step * tile
            both = soft * ((1.0 + MIX_ALPHA) * weight) - target * (MIX_ALPHA * weight)
            dl_ref[0, rows, :] = jnp.where(hit, both - weight, both).astype(B16)
        rows = slice(row * length, (row + 1) * length)
        sum_ref[rows, :] += mm(dl_ref[0, rows, :], table_ref[...], (1, 1))

    @pl.when(step == pl.num_programs(0) - 1)
    def _():
        dh_ref[...] = sum_ref[...].astype(B16)

        def slab(slot):
            return dh_ref.at[pl.ds(pl.multiple_of(slot * length, length), length)]

        def swap(k):
            to = other(k)
            return pltpu.make_async_remote_copy(
                src_ref=slab(to + 1 - 2 * core), dst_ref=sums.at[to // 2], send_sem=es.at[k], recv_sem=er.at[k],
                device_id=sibling(), device_id_type=MESH,
            )

        def pass_on(k):
            return pltpu.make_async_remote_copy(
                src_ref=sums.at[other(k) // 2], dst_ref=taken.at[k - 1], send_sem=fs.at[k], recv_sem=fr.at[k],
                device_id=(d, other(k)), device_id_type=MESH,
            )

        order = [*range(1, half), 0]
        for k in order:
            swap(k).start()
        for k in order:
            swap(k).wait()
            to = other(k)
            sums[to // 2] = (sums[to // 2].astype(F32) + slab(to)[...].astype(F32)).astype(B16)
            if k:
                pass_on(k).start()
        rows_ref[...] = pack_rows([jnp.sum(cross_ref[...], 1, keepdims=True)])
        total = sums[chip].astype(F32)
        for k in range(1, half):
            pass_on(k).wait_recv()
            total = total + taken[k - 1].astype(F32)
        dtwo_ref[...] = total
        for k in range(1, half):
            pass_on(k).wait_send()


def head_grad(V, teacher, hidden, table, given, ident):
    count, length, size = teacher.shape
    tokens, width = hidden.shape
    tile = tile_of(size, tokens)
    whole = lambda *shape: pl.BlockSpec(shape, lambda j: (0, 0))
    striped = pl.BlockSpec((width, tile), lambda j: (0, j))
    return pl.pallas_call(
        functools.partial(head_grad_kernel, V),
        grid=(size // tile,),
        out_shape=[
            jax.ShapeDtypeStruct((length, width), F32),
            jax.ShapeDtypeStruct((size // tile, tokens, tile), B16),
            jax.ShapeDtypeStruct((8, tokens), F32),
        ],
        in_specs=[
            pl.BlockSpec((count, length, tile), lambda j: (0, 0, j)),
            whole(tokens, width), striped, whole(tokens, 4),
        ],
        out_specs=[whole(length, width), pl.BlockSpec((1, tokens, tile), lambda j: (j, 0, 0)), whole(8, tokens)],
        scratch_shapes=[
            pltpu.VMEM((tokens, width), F32),
            pltpu.VMEM((tokens, 128), F32),
            pltpu.VMEM((tokens, width), B16),
            pltpu.VMEM((V // 2, length, width), B16),
            pltpu.VMEM((max(V // 2 - 1, 1), length, width), B16),
        ]
        + [pltpu.SemaphoreType.DMA((V // 2,))] * 4,
        compiler_params=pltpu.CompilerParams(
            collective_id=ident, has_side_effects=True, vmem_limit_bytes=62 * MIB
        ),
    )(teacher, hidden, table, given)


def mm(a, b, over=(1, 0)):
    return lax.dot_general(a, b, (((over[0],), (over[1],)), ((), ())), preferred_element_type=F32)


def norm_rows(values, gain, shift):
    center = values - jnp.mean(values, -1, keepdims=True)
    scaler = lax.rsqrt(jnp.mean(center * center, -1, keepdims=True) + NORM_EPS)
    normed = center * scaler
    return (normed * gain + shift, normed, scaler)


def norm_back(grad, normed, scaler, gain):
    scaled = grad * gain
    inward = scaler * (
        scaled
        - jnp.mean(scaled, -1, keepdims=True)
        - normed * jnp.mean(scaled * normed, -1, keepdims=True)
    )
    return (inward, jnp.sum(grad * normed, 0, keepdims=True), jnp.sum(grad, 0, keepdims=True))


def gelu_both(values):
    square = values * values
    tangent = jnp.tanh(GELU_C * values * (1.0 + 0.044715 * square))
    half = 0.5 * (1.0 + tangent)
    slope = half + 0.5 * values * (1.0 - tangent * tangent) * (GELU_C * (1.0 + 3.0 * 0.044715 * square))
    return values * half, slope


def bias_of(segment_ref, bias_ref):
    length = segment_ref.shape[1]
    row = segment_ref[...]
    column = jnp.broadcast_to(row, (128, length)).T[:, :1]
    bias_ref[...] = jnp.where(column == row, 0.0, -1e30)
    place = lax.broadcasted_iota(jnp.int32, (length, 1), 0)
    for code in range(SEGS):
        start = jnp.sum((row < code).astype(jnp.int32), 1, keepdims=True)
        place = place - jnp.where(column == code, start, 0)
    return place


def softmax(queries, keys, bias):
    scores = mm(queries, keys, (1, 1)) * 0.125 + bias
    expd = jnp.exp(scores - jnp.max(scores, -1, keepdims=True))
    return expd / jnp.sum(expd, -1, keepdims=True)


def pair_of(ref, part, pair, width):
    return ref[:, pl.ds(pl.multiple_of(part * width + pair * 128, 128), 128)]


def layer_forward(x, weights, gains_ref, bias_ref, packed_ref, context_ref, between=lambda: None):
    qkv_ref, out_ref, up_ref, down_ref = weights
    length, width = x.shape
    gain = lambda k: gains_ref[k : k + 1, :]
    h_zero, normed_a, scaler_a = norm_rows(x, gain(0), gain(1))
    packed_ref[...] = mm(h_zero.astype(B16), qkv_ref[...]).astype(B16)
    low = lax.broadcasted_iota(jnp.int32, (length, 128), 1) < 64

    def heads(pair, carry):
        queries, keys, values = (pair_of(packed_ref, part, pair, width) for part in range(3))
        none = jnp.zeros_like(queries)
        parts = []
        for picked in (jnp.where(low, queries, none), jnp.where(low, none, queries)):
            parts.append(mm(softmax(picked, keys, bias_ref[...]).astype(B16), values))
        context_ref[:, pl.ds(pl.multiple_of(pair * 128, 128), 128)] = jnp.where(low, *parts).astype(B16)
        return carry

    lax.fori_loop(0, width // 128, heads, 0)
    between()
    h_one, normed_b, scaler_b = norm_rows(h_zero + mm(context_ref[...], out_ref[...]), gain(2), gain(3))
    one_b = h_one.astype(B16)
    total = h_one
    chunk = 512
    for c in range(up_ref.shape[1] // chunk):
        part = slice(c * chunk, (c + 1) * chunk)
        active = gelu_both(mm(one_b, up_ref[:, part]))[0].astype(B16)
        total = total + mm(active, down_ref[part, :])
    h_two, normed_c, scaler_c = norm_rows(total, gain(4), gain(5))
    return h_two, (normed_a, normed_b, normed_c), (scaler_a, scaler_b, scaler_c)


def teach_kernel(group_ref, x_ref, segment_ref, first_ref, mid_ref, second_ref, gains_ref, top_ref, bias_ref, packed_ref, context_ref):
    width = x_ref.shape[2]
    bias_of(segment_ref, bias_ref)
    first, second = first_ref.at[0], second_ref.at[0]
    weights = (first.at[:, : 3 * width], first.at[:, 3 * width :], mid_ref.at[0], second)
    h_two, _, _ = layer_forward(
        x_ref[0].astype(F32), weights, gains_ref.at[0], bias_ref, packed_ref, context_ref
    )
    top_ref[...] = h_two.astype(B16)


def teach(group, x, segment, first, mid, second, gains):
    _, length, width = x.shape
    chosen = lambda shape: pl.BlockSpec((1,) + shape[1:], lambda i, g: (g[0], 0, 0))
    return pl.pallas_call(
        teach_kernel,
        grid_spec=pltpu.PrefetchScalarGridSpec(
            num_scalar_prefetch=1,
            grid=(1,),
            in_specs=[
                pl.BlockSpec((1, length, width), lambda i, g: (0, 0, 0)),
                pl.BlockSpec((1, length), lambda i, g: (0, 0)),
                chosen(first.shape),
                chosen(mid.shape),
                chosen(second.shape),
                chosen(gains.shape),
            ],
            out_specs=pl.BlockSpec((length, width), lambda i, g: (0, 0)),
            scratch_shapes=[
                pltpu.VMEM((length, length), F32),
                pltpu.VMEM((length, 3 * width), B16),
                pltpu.VMEM((length, width), B16),
            ],
        ),
        out_shape=jax.ShapeDtypeStruct((length, width), B16),
        compiler_params=pltpu.CompilerParams(vmem_limit_bytes=60 * MIB),
    )(group, x, segment, first, mid, second, gains)


def learn(x, attention_ref, up_ref, down_ref, gains_ref, bias_ref, own_ref, kept, between):
    length, width = x.shape
    weights = (attention_ref.at[:, : 3 * width], attention_ref.at[:, 3 * width :], up_ref, down_ref)
    h_two, normed, scalers = layer_forward(x, weights, gains_ref, bias_ref, kept[4], kept[5], between)
    own_ref[...] = h_two.astype(B16)
    for ref, value in zip(kept, normed):
        ref[...] = value
    lane = lax.broadcasted_iota(jnp.int32, (length, 128), 1)
    kept[3][...] = jnp.where(lane == 0, scalers[0], jnp.where(lane == 1, scalers[1], scalers[2]))


def back_kernel(
    dtwo_ref, segment_ref, attention_ref, up_ref, down_ref, gains_ref,
    na_ref, nb_ref, nc_ref, scalers_ref, packed_ref, context_ref,
    dx_ref, dattention_ref, dup_ref, ddown_ref, dpos_ref, dgains_ref, bias_ref, dpacked_ref, dcontext_ref,
):
    length, width = dtwo_ref.shape
    gain = lambda k: gains_ref[k : k + 1, :]
    place = bias_of(segment_ref, bias_ref)
    dz_two, gain_c, shift_c = norm_back(dtwo_ref[...], nc_ref[...], scalers_ref[:, 2:3], gain(4))
    dbranch = dz_two.astype(B16)
    one_b = (nb_ref[...] * gain(2) + gain(3)).astype(B16)
    dh_one = dz_two
    chunk = 512
    for c in range(up_ref.shape[1] // chunk):
        part = slice(c * chunk, (c + 1) * chunk)
        active, slope = gelu_both(mm(one_b, up_ref[:, part]))
        ddown_ref[part, :] = mm(active.astype(B16), dbranch, (0, 0)).astype(B16)
        dinner = (mm(dbranch, down_ref[part, :], (1, 1)) * slope).astype(B16)
        dup_ref[:, part] = mm(one_b, dinner, (0, 0)).astype(B16)
        dh_one = dh_one + mm(dinner, up_ref[:, part], (1, 1))
    dz_one, gain_b, shift_b = norm_back(dh_one, nb_ref[...], scalers_ref[:, 1:2], gain(2))
    dproj = dz_one.astype(B16)
    dattention_ref[:, 3 * width :] = mm(context_ref[...], dproj, (0, 0)).astype(B16)
    dcontext_ref[...] = mm(dproj, attention_ref[:, 3 * width :], (1, 1)).astype(B16)
    low = lax.broadcasted_iota(jnp.int32, (length, 128), 1) < 64

    def heads(pair, carry):
        queries, keys, values = (pair_of(packed_ref, part, pair, width) for part in range(3))
        grads = pair_of(dcontext_ref, 0, pair, width)
        none = jnp.zeros_like(queries)
        parts = []
        for first in (True, False):
            pick = lambda a: jnp.where(low, a, none) if first else jnp.where(low, none, a)
            probs = softmax(pick(queries), keys, bias_ref[...])
            dprobs = mm(pick(grads), values, (1, 1))
            inner = jnp.sum(probs * dprobs, -1, keepdims=True)
            dscore = (probs * (dprobs - inner) * 0.125).astype(B16)
            parts.append(
                (mm(dscore, keys), mm(dscore, queries, (0, 0)), mm(probs.astype(B16), grads, (0, 0)))
            )
        for part in range(3):
            columns = pl.ds(pl.multiple_of(part * width + pair * 128, 128), 128)
            dpacked_ref[:, columns] = jnp.where(low, parts[0][part], parts[1][part]).astype(B16)
        return carry

    lax.fori_loop(0, width // 128, heads, 0)
    zero_b = (na_ref[...] * gain(0) + gain(1)).astype(B16)
    dattention_ref[:, : 3 * width] = mm(zero_b, dpacked_ref[...], (0, 0)).astype(B16)
    dh_zero = dz_one + mm(dpacked_ref[...], attention_ref[:, : 3 * width], (1, 1))
    dx, gain_a, shift_a = norm_back(dh_zero, na_ref[...], scalers_ref[:, 0:1], gain(0))
    dx_b = dx.astype(B16)
    lane = lax.broadcasted_iota(jnp.int32, (length, dpos_ref.shape[0]), 1)
    onehot = jnp.where(lane == place, 1.0, 0.0).astype(B16)
    dpos_ref[...] = mm(onehot, dx_b, (0, 0)).astype(B16)
    dx_ref[...] = dx_b.T
    for k, row in enumerate((gain_a, shift_a, gain_b, shift_b, gain_c, shift_c)):
        dgains_ref[k : k + 1, :] = row


def back(dtwo, segment, pos_count, attention, up, down, gains, kept):
    length, width = dtwo.shape
    inputs = (dtwo, segment, attention, up, down, gains) + tuple(kept)
    half = lambda *shape: jax.ShapeDtypeStruct(shape, B16)
    return pl.pallas_call(
        back_kernel,
        in_specs=[IN_VMEM] * len(inputs),
        out_specs=[IN_VMEM] * 6,
        out_shape=[
            half(width, length), half(*attention.shape), half(*up.shape), half(*down.shape),
            half(pos_count, width), jax.ShapeDtypeStruct(gains.shape, F32),
        ],
        scratch_shapes=[
            pltpu.VMEM((length, length), F32),
            pltpu.VMEM((length, 3 * width), B16),
            pltpu.VMEM((length, width), B16),
        ],
        compiler_params=pltpu.CompilerParams(vmem_limit_bytes=60 * MIB),
    )(*inputs)


def adam(weight, first, second, grad, fix_one, fix_two, rate):
    first = BETA_ONE * first + (1.0 - BETA_ONE) * grad
    second = BETA_TWO * second + (1.0 - BETA_TWO) * grad * grad
    update = first / fix_one / (jnp.sqrt(second / fix_two) + ADAM_EPS)
    return (first, second, weight - rate * (update + WEIGHT_DECAY * weight))


def on_device(
    D, V,
    token_ids, segment_ids, labels, loss_mask, teacher_group, teacher_inputs, teacher_table,
    teacher_qkv, teacher_out, teacher_up, teacher_down, teacher_gains, step_count,
    embed_w, embed_m, embed_v, pos_w, pos_m, pos_v, qkv_w, qkv_m, qkv_v,
    out_w, out_m, out_v, up_w, up_m, up_v, down_w, down_m, down_v, gains_w, gains_m, gains_v,
):
    length = token_ids.shape[1]
    slice_len, columns = embed_w.shape
    width = gains_w.shape[1]
    d, v = lax.axis_index("dp"), lax.axis_index("vocab")

    turned_table = embed_w.astype(B16).T.reshape(2, columns // 2, slice_len)
    attention = jnp.concatenate([qkv_w, out_w], 1).astype(B16)[None]
    integers = jnp.concatenate(
        [token_ids, labels, loss_mask, jnp.broadcast_to(teacher_group[:, None], (1, length)),
         jnp.zeros((4, length), jnp.int32)], 0
    )[None]
    table, attention, up_t, down_t, pos_t, integers = ring_gather(
        D, V,
        [turned_table, attention, up_w.astype(B16)[None], down_w.astype(B16)[None], pos_w.astype(B16)[None], integers],
        ((0, 0, False, "dp", 0), (0, 1, False, "dp", 1), (5, 0, True, 2, 1), (1, 0, True, 0, 0), (2, 0, True, 1, 1),
         (3, 0, True, 2, 0), (4, 0, True, 1, 0)),
        1,
    )
    table = table.reshape(width, slice_len)
    attention = attention.reshape(width, -1)
    up_t, down_t, pos_t = up_t.reshape(width, -1), down_t.reshape(-1, width), pos_t.reshape(-1, width)
    integers = integers.reshape(D, V, 8, length)
    counted = jnp.maximum(jnp.sum(integers[:, :, 2].astype(F32)), 1.0)
    group_ints = lax.dynamic_index_in_dim(integers, d, 0, False)
    offset = v * slice_len
    ids_here = (group_ints[:, 0].reshape(-1, 1) - offset)
    labels_here = (group_ints[:, 1].reshape(-1, 1) - offset)
    counts = group_ints[:, 2].reshape(-1).astype(F32)
    groups = group_ints[:, 3, 0]

    weight = counts / counted
    given = jnp.concatenate([weight[:, None], labels_here.astype(F32), ids_here.astype(F32)], 1)
    layers = [jnp.concatenate([teacher_qkv, teacher_out], 2), teacher_up, teacher_down]
    first, mid, second, hidden_all, turned, told, *kept = study(
        D, V, layers, table, given, segment_ids, pos_t, attention, up_t, down_t, gains_w, 4
    )
    student_lse, picked = told[0], told[1]
    tw = teacher_gains.shape[2]
    top = teach(
        teacher_group, teacher_inputs, segment_ids, first.reshape(3, tw, -1), mid.reshape(3, tw, -1),
        second.reshape(3, -1, tw), teacher_gains,
    )

    teacher, told = teacher_stats(V, groups, top, teacher_table, 5)
    teacher_lse, tcross = told[0], told[1]
    given = jnp.stack([weight, labels_here[:, 0].astype(F32), student_lse, teacher_lse], 1)
    dtwo, dlogits, cross = head_grad(V, teacher, hidden_all, table, given, 6)
    once = jnp.sum(weight * (MIX_ALPHA * (tcross - teacher_lse + student_lse) + student_lse - picked))
    loss_part = jnp.where(v == 0, once, 0.0) - MIX_ALPHA * jnp.sum(weight * cross[0])

    turned_dx, grad_attention, grad_up, grad_down, grad_pos, grad_gains = back(
        dtwo, segment_ids, pos_t.shape[0], attention, up_t, down_t, gains_w, kept
    )

    lane = lax.broadcasted_iota(jnp.int32, (2, width), 1)
    scalars = jnp.where(lane == 1, loss_part, 0.0)
    owners = lambda g: g.reshape(D * V // 2, 2, -1, g.shape[1])
    grad_embed, totals, owned_attention, owned_up, owned_down, owned_pos = settle(
        D, V, dlogits, turned, turned_dx, ids_here, jnp.concatenate([grad_gains, scalars], 0),
        [owners(grad_attention), owners(grad_up), owners(grad_down), owners(grad_pos)], (0, 1, 2, 1), 7,
    )
    owned = (owned_pos, owned_attention[:, : 3 * width], owned_attention[:, 3 * width :], owned_up, owned_down)
    gains_grad, squares, loss = totals[:6], totals[7, 0], totals[7, 1]

    grad_norm = jnp.sqrt(squares + jnp.sum(gains_grad * gains_grad))
    factor = CLIP_NORM / jnp.maximum(grad_norm, CLIP_NORM)
    count_f = step_count.astype(F32)
    fix_one = 1.0 - jnp.power(BETA_ONE, count_f)
    fix_two = 1.0 - jnp.power(BETA_TWO, count_f)

    def update(weight, first, second, grad, rate):
        return adam(weight, first, second, grad * factor, fix_one, fix_two, rate)

    out = [loss, grad_norm]
    out += update(embed_w, embed_m, embed_v, grad_embed.T, LEARN_RATE)
    out += update(pos_w, pos_m, pos_v, owned[0], LEARN_RATE)
    out += update(qkv_w, qkv_m, qkv_v, owned[1], LEARN_RATE)
    out += update(out_w, out_m, out_v, owned[2], LEARN_RATE)
    out += update(up_w, up_m, up_v, owned[3], LEARN_RATE)
    out += update(down_w, down_m, down_v, owned[4], LEARN_RATE)
    out += update(gains_w, gains_m, gains_v, gains_grad, GAIN_RATE)
    return tuple(out)


def solution(mesh):
    rows, whole = P(("dp", "vocab"), None), P()
    split = P(None, ("dp", "vocab"), None)
    embed = P("vocab", "dp")
    return jax.shard_map(
        functools.partial(on_device, mesh.shape["dp"], mesh.shape["vocab"]),
        mesh=mesh,
        in_specs=(rows, rows, rows, rows, P(("dp", "vocab")), P(("dp", "vocab"), None, None), P(None, None, "vocab"),
                  split, split, split, split, whole, whole)
        + (embed,) * 3 + (rows,) * 15 + (whole,) * 3,
        out_specs=(whole, whole) + (embed,) * 3 + (rows,) * 15 + (whole,) * 3,
        check_vma=False,
    )
```
